256 devices in a mesh: group: 16 (over z, core), tp: 16 (over y, x).
Axes of the slice: x: 4, y: 4, z: 8, core: 2. Of those that a mesh axis runs over, the one named last changes fastest.
Arguments:
- hidden: bfloat16 [2, 2048, 8192], P(None, 'group'), may hold values from -6 to 6
- w_query: bfloat16 [8192, 4096], P(None, 'tp'), may hold values from -0.0625 to 0.0625
- w_key: bfloat16 [8192, 512], P(None, 'tp'), may hold values from -0.0625 to 0.0625
- w_value: bfloat16 [8192, 512], P(None, 'tp'), may hold values from -0.0625 to 0.0625
- w_out: bfloat16 [4096, 8192], P('tp'), may hold values from -0.09375 to 0.09375
- key_cache: bfloat16 [2048, 512, 512], P(('group', 'tp')), may hold values from -80 to 80
- value_cache: bfloat16 [2048, 512, 512], P(('group', 'tp')), may hold values from -6 to 6
- lengths: int32 [2048], P(('group', 'tp')), may hold values from 1 to 510, as said below
- row_slot: int32 [2, 2048], P(None, 'group'), may hold values from 0 to 12, as said below
- evict_slot: int32 [2, 192], replicated, may hold values from 0 to 12, as said below
- evict_adapter: int32 [2, 192], replicated, may hold values from 0 to 191, as said below
- owner: int32 [192], replicated, may hold values from 0 to 191, as said below
- pool_a_in: bfloat16 [192, 48, 8192], P('group', None, 'tp'), may hold values from -0.0625 to 0.0625
- pool_b_q: bfloat16 [192, 16, 4096], P('group', None, 'tp'), may hold values from -1.5 to 1.5
- pool_b_k: bfloat16 [192, 16, 512], P('group', None, 'tp'), may hold values from -1.5 to 1.5
- pool_b_v: bfloat16 [192, 16, 512], P('group', None, 'tp'), may hold values from -1.5 to 1.5
- pool_a_o: bfloat16 [192, 16, 4096], P('group', None, 'tp'), may hold values from -0.09375 to 0.09375
- pool_b_o: bfloat16 [192, 16, 8192], P('group', None, 'tp'), may hold values from -1.5 to 1.5
- slot_a_in: bfloat16 [208, 48, 8192], P('group', None, 'tp'), may hold values from -0.0625 to 0.0625
- slot_b_q: bfloat16 [208, 16, 4096], P('group', None, 'tp'), may hold values from -1.5 to 1.5
- slot_b_k: bfloat16 [208, 16, 512], P('group', None, 'tp'), may hold values from -1.5 to 1.5
- slot_b_v: bfloat16 [208, 16, 512], P('group', None, 'tp'), may hold values from -1.5 to 1.5
- slot_a_o: bfloat16 [208, 16, 4096], P('group', None, 'tp'), may hold values from -0.09375 to 0.09375
- slot_b_o: bfloat16 [208, 16, 8192], P('group', None, 'tp'), may hold values from -1.5 to 1.5
Outputs:
- attn_out: bfloat16 [2, 2048, 8192], P(None, 'group', 'tp')
The draws below stay inside these ranges and needn't reach their ends.
Inputs may be any that keep to these rules, and one draw needn't show every extreme that they name: `lengths`: one row of each replica has exactly 510. `row_slot`: at each step every one of a replica's 13 slots is used by some row of that replica. `evict_slot`: the 12 slots one replica refills in a step are distinct. `evict_adapter`: the adapters one replica loads in a step are distinct; at most 2 of them have pool positions held by any one replica (position p is held by replica p // 12), and exactly 2 for some replica, at every replica and step. `owner`: A permutation.
All inputs are finite; a program needn't handle non-finite values.
Results may differ from the reference program's by a relative error of at most 0.013.
Values may be sent and summed in bfloat16 or wider, within the bound.
No kernel may reach another device: no remote copies, remote signals or barrier semaphores. Data moves between devices by JAX's collectives and lax.ppermute only.
A program may use at most 128 MiB of HBM per device.

```python
import math
import jax
import jax.numpy as jnp
from jax import lax

D = 8192
QH = 32
KH = 4
HD = 128
RANK = 16
STEPS = 2
ROWS_G = 128
LEN = 512
ADP_GROUP = 12
SLOTS = 13
LOADS = 12
CAP = 2
QW = 4096
KW = 512
TOKENS = 2048
ADAPTERS = 192
N_GROUP = 16


def adapter_table(key):
    return jax.random.permutation(jax.random.fold_in(key, 101), ADAPTERS).astype(jnp.int32)


def draw_owner(key, part):
    return adapter_table(key)


def draw_evict_adapter(key, part):
    table = adapter_table(key)
    key = jax.random.fold_in(key, 7)
    first, second, third = jax.random.split(key, 3)
    count = STEPS * N_GROUP
    inverse = jnp.argsort(table).astype(jnp.int32)
    orders = jax.vmap(lambda sub: jax.random.permutation(sub, N_GROUP))(jax.random.split(first, count))
    load_index = jnp.arange(LOADS)
    column = jnp.where(load_index < CAP, 0, 1 + (load_index - CAP) % (N_GROUP - 1))
    sources = orders[:, column]
    offset = jax.random.randint(second, (count, 1), 0, ADP_GROUP)
    local_index = (offset + load_index[None, :]) % ADP_GROUP
    chosen = inverse[sources * ADP_GROUP + local_index]
    shuffle = jax.vmap(lambda sub: jax.random.permutation(sub, LOADS))(jax.random.split(third, count))
    chosen = jnp.take_along_axis(chosen, shuffle, axis=1)
    return chosen.reshape(STEPS, N_GROUP * LOADS).astype(jnp.int32)


def draw_evict_slot(key, part):
    key = jax.random.fold_in(key, 11)
    count = STEPS * N_GROUP
    orders = jax.vmap(lambda sub: jax.random.permutation(sub, SLOTS))(jax.random.split(key, count))
    return orders[:, :LOADS].reshape(STEPS, N_GROUP * LOADS).astype(jnp.int32)


def draw_row_slot(key, part):
    key = jax.random.fold_in(key, 13)
    first, second, third = jax.random.split(key, 3)
    count = STEPS * N_GROUP
    covered = jax.vmap(lambda sub: jax.random.permutation(sub, SLOTS))(jax.random.split(first, count))
    others = jax.random.randint(second, (count, ROWS_G - SLOTS), 0, SLOTS)
    chosen = jnp.concatenate([covered, others], axis=1)
    shuffle = jax.vmap(lambda sub: jax.random.permutation(sub, ROWS_G))(jax.random.split(third, count))
    chosen = jnp.take_along_axis(chosen, shuffle, axis=1)
    return chosen.reshape(STEPS, N_GROUP * ROWS_G).astype(jnp.int32)


def draw_lengths(key, part):
    key = jax.random.fold_in(key, 17)
    first, second = jax.random.split(key)
    drawn = jax.random.randint(first, (N_GROUP, ROWS_G), 1, LEN - STEPS + 1)
    longest = jax.random.randint(second, (N_GROUP, 1), 0, ROWS_G)
    drawn = jnp.where(jnp.arange(ROWS_G)[None, :] == longest, LEN - STEPS, drawn)
    return drawn.reshape(TOKENS).astype(jnp.int32)


def draw_key_cache(key, part):
    key = jax.random.fold_in(key, 19)
    first = jax.random.fold_in(key, 0)
    shape = (TOKENS, LEN, KW)
    drawn = jnp.clip(jax.random.normal(first, shape, jnp.float32), -6.0, 6.0)
    return drawn.astype(jnp.bfloat16)


def levels(own_key, shape, cuts, smallest, largest):
    loudness = 1.0
    for position, blocks in cuts:
        steps = jax.random.uniform(jax.random.fold_in(jax.random.fold_in(own_key, 6), position), (blocks,), jnp.float32, smallest / len(cuts), largest / len(cuts))
        loudness = loudness * jnp.repeat(jnp.exp(steps), shape[position] // blocks).reshape((-1,) + (1,) * (len(shape) - 1 - position))
    return loudness


def normal_values(rng, dims, deviation, reach, cuts=(), kind=jnp.bfloat16):
    entries = jax.random.normal(rng, dims, jnp.float32) * deviation
    if len(cuts) > 0:
        entries = levels(rng, dims, cuts, -0.22, 0.18) * entries
    return jnp.clip(entries, min=-reach, max=reach).astype(kind)


def setup_inputs(seed: int = 0) -> dict:
    streams_of = jax.random.split(jax.random.key(seed), 25)
    hidden = normal_values(streams_of[0], (STEPS, TOKENS, D), 1.0, 6.0, ((1, 16),))
    w_query = normal_values(streams_of[1], (D, QW), D ** -0.5, 0.0625, ((1, 16),))
    w_key = normal_values(streams_of[2], (D, KW), D ** -0.5, 0.0625, ((1, 16),))
    w_value = normal_values(streams_of[3], (D, KW), D ** -0.5, 0.0625, ((1, 16),))
    w_out = normal_values(streams_of[4], (QW, D), QW ** -0.5, 0.09375, ((0, 16),))
    key_cache = draw_key_cache(jax.random.fold_in(streams_of[24], 71), 0)
    value_cache = normal_values(streams_of[6], (TOKENS, LEN, KW), 1.0, 6.0, ((0, 256),))
    lengths = draw_lengths(jax.random.fold_in(streams_of[24], 71), 0)
    row_slot = draw_row_slot(jax.random.fold_in(streams_of[24], 71), 0)
    evict_slot = draw_evict_slot(jax.random.fold_in(streams_of[24], 71), 0)
    evict_adapter = draw_evict_adapter(jax.random.fold_in(streams_of[24], 71), 0)
    owner = draw_owner(jax.random.fold_in(streams_of[24], 71), 0)
    pool_a_in = normal_values(streams_of[12], (ADAPTERS, 3 * RANK, D), D ** -0.5, 0.0625, ((0, 16), (2, 16)))
    pool_b_q = normal_values(streams_of[13], (ADAPTERS, RANK, QW), RANK ** -0.5, 1.5, ((0, 16), (2, 16)))
    pool_b_k = normal_values(streams_of[14], (ADAPTERS, RANK, KW), RANK ** -0.5, 1.5, ((0, 16), (2, 16)))
    pool_b_v = normal_values(streams_of[15], (ADAPTERS, RANK, KW), RANK ** -0.5, 1.5, ((0, 16), (2, 16)))
    pool_a_o = normal_values(streams_of[16], (ADAPTERS, RANK, QW), QW ** -0.5, 0.09375, ((0, 16), (2, 16)))
    pool_b_o = normal_values(streams_of[17], (ADAPTERS, RANK, D), RANK ** -0.5, 1.5, ((0, 16), (2, 16)))
    slot_a_in = normal_values(streams_of[18], (N_GROUP * SLOTS, 3 * RANK, D), D ** -0.5, 0.0625, ((0, 16), (2, 16)))
    slot_b_q = normal_values(streams_of[19], (N_GROUP * SLOTS, RANK, QW), RANK ** -0.5, 1.5, ((0, 16), (2, 16)))
    slot_b_k = normal_values(streams_of[20], (N_GROUP * SLOTS, RANK, KW), RANK ** -0.5, 1.5, ((0, 16), (2, 16)))
    slot_b_v = normal_values(streams_of[21], (N_GROUP * SLOTS, RANK, KW), RANK ** -0.5, 1.5, ((0, 16), (2, 16)))
    slot_a_o = normal_values(streams_of[22], (N_GROUP * SLOTS, RANK, QW), QW ** -0.5, 0.09375, ((0, 16), (2, 16)))
    slot_b_o = normal_values(streams_of[23], (N_GROUP * SLOTS, RANK, D), RANK ** -0.5, 1.5, ((0, 16), (2, 16)))
    return {"hidden": hidden, "w_query": w_query, "w_key": w_key, "w_value": w_value, "w_out": w_out, "key_cache": key_cache, "value_cache": value_cache, "lengths": lengths, "row_slot": row_slot, "evict_slot": evict_slot, "evict_adapter": evict_adapter, "owner": owner, "pool_a_in": pool_a_in, "pool_b_q": pool_b_q, "pool_b_k": pool_b_k, "pool_b_v": pool_b_v, "pool_a_o": pool_a_o, "pool_b_o": pool_b_o, "slot_a_in": slot_a_in, "slot_b_q": slot_b_q, "slot_b_k": slot_b_k, "slot_b_v": slot_b_v, "slot_a_o": slot_a_o, "slot_b_o": slot_b_o}


low_rank_scale = 0.5

def reference(hidden, w_query, w_key, w_value, w_out, key_cache, value_cache, lengths, row_slot, evict_slot, evict_adapter, owner, pool_a_in, pool_b_q, pool_b_k, pool_b_v, pool_a_o, pool_b_o, slot_a_in, slot_b_q, slot_b_k, slot_b_v, slot_a_o, slot_b_o):
    score_scale = 1.0 / math.sqrt(HD)
    pool_arrays = (pool_a_in, pool_b_q, pool_b_k, pool_b_v, pool_a_o, pool_b_o)
    slot_arrays = (slot_a_in, slot_b_q, slot_b_k, slot_b_v, slot_a_o, slot_b_o)

    def project(tokens, weight, shrunk, adapter_output):
        base_contribution = jnp.dot(tokens, weight, preferred_element_type=jnp.float32)
        adapter_delta = jnp.einsum('rk,rkc->rc', shrunk.astype(jnp.float32), adapter_output.astype(jnp.float32))
        return (base_contribution + low_rank_scale * adapter_delta).astype(jnp.bfloat16)

    def one_group(group_id):
        group_id = group_id.astype(jnp.int32)
        first_row = group_id * ROWS_G
        first_slot = group_id * SLOTS
        first_load = group_id * LOADS
        stored = tuple((lax.dynamic_slice_in_dim(piece, first_slot, SLOTS, 0) for piece in slot_arrays))
        cached_keys = lax.dynamic_slice_in_dim(key_cache, first_row, ROWS_G, 0)
        cached_values = lax.dynamic_slice_in_dim(value_cache, first_row, ROWS_G, 0)
        row_lengths = lax.dynamic_slice_in_dim(lengths, first_row, ROWS_G, 0)
        row_index = jnp.arange(ROWS_G, dtype=jnp.int32)
        positions = jnp.arange(LEN, dtype=jnp.int32)
        step_outputs = []
        for step in range(STEPS):
            wanted = lax.dynamic_slice_in_dim(evict_adapter[step], first_load, LOADS, 0)
            targets = lax.dynamic_slice_in_dim(evict_slot[step], first_load, LOADS, 0)
            sources = owner[wanted]
            stored = tuple((piece.at[targets].set(whole[sources]) for piece, whole in zip(stored, pool_arrays)))
            users = lax.dynamic_slice_in_dim(row_slot[step], first_row, ROWS_G, 0)
            a_in, b_q, b_k, b_v, a_o, b_o = tuple((piece[users] for piece in stored))
            tokens = lax.dynamic_slice_in_dim(hidden[step], first_row, ROWS_G, 0)
            shrunk = jnp.einsum('rd,rkd->rk', tokens.astype(jnp.float32), a_in.astype(jnp.float32)).astype(jnp.bfloat16)
            query = project(tokens, w_query, shrunk[:, :RANK], b_q)
            key_new = project(tokens, w_key, shrunk[:, RANK:2 * RANK], b_k)
            value_new = project(tokens, w_value, shrunk[:, 2 * RANK:], b_v)
            spot = row_lengths + step
            cached_keys = cached_keys.at[row_index, spot].set(key_new)
            cached_values = cached_values.at[row_index, spot].set(value_new)
            query_heads = query.reshape(ROWS_G, KH, QH // KH, HD).astype(jnp.float32)
            key_heads = cached_keys.reshape(ROWS_G, LEN, KH, HD).astype(jnp.float32)
            value_heads = cached_values.reshape(ROWS_G, LEN, KH, HD).astype(jnp.float32)
            scores = jnp.einsum('rkgc,rlkc->rkgl', query_heads, key_heads) * score_scale
            visible = (positions[None, :] <= spot[:, None])[:, None, None, :]
            scores = jnp.where(visible, scores, -jnp.inf)
            highest = lax.optimization_barrier(jnp.max(scores, axis=-1, keepdims=True))
            weights = jnp.exp(scores - highest)
            totals = lax.optimization_barrier(jnp.sum(weights, axis=-1, keepdims=True))
            mixed = jnp.einsum('rkgl,rlkc->rkgc', weights, value_heads)
            attended = (mixed / totals).reshape(ROWS_G, QW).astype(jnp.bfloat16)
            shrunk_out = jnp.einsum('rc,rkc->rk', attended.astype(jnp.float32), a_o.astype(jnp.float32)).astype(jnp.bfloat16)
            base_output = jnp.dot(attended, w_out, preferred_element_type=jnp.float32)
            adapter_output = jnp.einsum('rk,rkc->rc', shrunk_out.astype(jnp.float32), b_o.astype(jnp.float32))
            step_outputs.append((base_output + low_rank_scale * adapter_output).astype(jnp.bfloat16))
        return jnp.stack(step_outputs)
    per_group = lax.map(one_group, jnp.arange(N_GROUP, dtype=jnp.int32))
    return jnp.transpose(per_group, (1, 0, 2, 3)).reshape(STEPS, TOKENS, D)
```

```python
import math

import jax
import jax.numpy as jnp
from jax import lax
from jax.experimental import pallas as pl
from jax.experimental.pallas import tpu as pltpu
from jax.sharding import PartitionSpec as P

QH = 32
KH = 4
HD = 128
STEPS = 2
ROWS = 128
RANK = 16
LOADS = 12
SLOTS = 13
HELD = 12
N = 16
ALL_ROWS = STEPS * ROWS
LOCAL = ROWS // N
MINE = STEPS * LOCAL
ENTRIES = 1 + STEPS * LOADS
IN_RANK = 3 * RANK
PER_DOT = 5
QF = 256
KF = 32
IN_PART = 512
OUT_PART = 512
FEATURES = QH * HD
LENGTH = 512
KW = KH * HD
BF16 = jnp.bfloat16
F32 = jnp.float32
low_rank_scale = 0.5


def vmem():
    return pl.BlockSpec(memory_space=pltpu.VMEM)


def hbm():
    return pl.BlockSpec(memory_space=pl.ANY)


def smem():
    return pl.BlockSpec(memory_space=pltpu.SMEM)


def params():
    return pltpu.CompilerParams(vmem_limit_bytes=40 * 1024 * 1024)


def cost(flops, nbytes):
    return pl.CostEstimate(flops=flops, bytes_accessed=nbytes, transcendentals=0)


def shrink_kernel(index, pool, slot, tokens, entry, out, maps, arrived):
    copies = []
    for i in range(ENTRIES):
        origin = slot.at[index[0]] if i == 0 else pool.at[index[i]]
        copy = pltpu.make_async_copy(origin, maps.at[pl.ds(i * IN_RANK, IN_RANK)], arrived.at[i])
        copy.start()
        copies.append(copy)
    used = entry[...]
    total = jnp.zeros((IN_RANK, ALL_ROWS), F32)
    for first in range(0, ENTRIES, PER_DOT):
        for i in range(first, first + PER_DOT):
            copies[i].wait()
        block = maps[pl.ds(first * IN_RANK, PER_DOT * IN_RANK), :]
        product = lax.dot_general(
            block, tokens[...], (((1,), (1,)), ((), ())), preferred_element_type=F32
        )
        for k in range(PER_DOT):
            piece = product[k * IN_RANK : (k + 1) * IN_RANK]
            total = total + jnp.where(used == first + k, piece, 0.0)
    out[...] = total.astype(BF16)


def expand(shrunk, entry):
    loads = STEPS * LOADS
    load = lax.broadcasted_iota(jnp.int32, (loads, ALL_ROWS), 0) + 1
    chosen = load == entry
    blocks = [jnp.where(chosen, shrunk[r : r + 1, :], 0.0) for r in range(RANK)]
    kept = jnp.where(entry == 0, shrunk, 0.0)
    return jnp.concatenate(blocks + [kept], axis=0).astype(BF16)


def contract(left, right):
    return lax.dot_general(left, right, (((0,), (0,)), ((), ())), preferred_element_type=F32)


def project_kernel(parts, entry, base_q, base_kv, up_q, up_kv, out):
    shrunk = jnp.sum(parts[...].astype(F32), axis=0).astype(BF16).astype(F32)
    used = entry[...]
    wide_q = expand(shrunk[:RANK], used)
    wide_k = expand(shrunk[RANK : 2 * RANK], used)
    wide_v = expand(shrunk[2 * RANK :], used)
    query = base_q[...] + low_rank_scale * contract(wide_q, up_q[...])
    delta_k = contract(wide_k, up_kv[...])
    delta_v = contract(wide_v, up_kv[...])
    column = lax.broadcasted_iota(jnp.int32, delta_k.shape, 1)
    delta = jnp.where(column < KF, delta_k, delta_v)
    fresh = base_kv[...] + low_rank_scale * delta
    for t in range(N):
        for s in range(STEPS):
            low = s * ROWS + t * LOCAL
            out[t, s * LOCAL : (s + 1) * LOCAL, :QF] = query[low : low + LOCAL]
            out[t, s * LOCAL : (s + 1) * LOCAL, QF:] = fresh[low : low + LOCAL]


def attend_kernel(lengths, queries, keys_new, values_new, keys, values, out):
    row = pl.program_id(0)
    length = lengths[row]
    position = lax.broadcasted_iota(jnp.int32, (LENGTH, 1), 0)
    first, second = position == length, position == length + 1
    key_rows = keys[0]
    value_rows = values[0]
    key_rows = jnp.where(first, keys_new[0, 0:1], jnp.where(second, keys_new[0, 1:2], key_rows))
    value_rows = jnp.where(
        first, values_new[0, 0:1], jnp.where(second, values_new[0, 1:2], value_rows)
    )
    head_rows = STEPS * QH
    group = lax.broadcasted_iota(jnp.int32, (head_rows, KW), 0) % N // (N // KH)
    own = group == lax.broadcasted_iota(jnp.int32, (head_rows, KW), 1) // HD
    asked = queries[0]
    spread = jnp.where(own, jnp.concatenate([asked] * KH, axis=1), jnp.zeros((), BF16))
    scores = lax.dot_general(
        spread, key_rows, (((1,), (1,)), ((), ())), preferred_element_type=F32
    ) * (1.0 / math.sqrt(HD))
    step = lax.broadcasted_iota(jnp.int32, (head_rows, LENGTH), 0) // QH
    seen = lax.broadcasted_iota(jnp.int32, (head_rows, LENGTH), 1) <= length + step
    scores = jnp.where(seen, scores, -jnp.inf)
    weights = jnp.exp(scores - jnp.max(scores, axis=1, keepdims=True))
    totals = jnp.sum(weights, axis=1, keepdims=True)
    mixed = jnp.dot(weights.astype(BF16), value_rows, preferred_element_type=F32)
    mixed = jnp.where(own, mixed, 0.0)
    attended = mixed[:, :HD]
    for k in range(1, KH):
        attended = attended + mixed[:, k * HD : (k + 1) * HD]
    out[0] = (attended / totals).astype(BF16)


def shrink_out_kernel(attended, entry, maps, kept, out):
    part = attended[...].reshape(ALL_ROWS, QF)
    used = entry[...]
    dims = (((1,), (1,)), ((), ()))
    loaded = lax.dot_general(maps[...], part, dims, preferred_element_type=F32)
    first = lax.dot_general(kept[...], part, dims, preferred_element_type=F32)
    loads = STEPS * LOADS
    chosen = lax.broadcasted_iota(jnp.int32, (loads, ALL_ROWS), 0) + 1 == used
    rows = [
        jnp.sum(jnp.where(chosen, loaded[r * loads : (r + 1) * loads], 0.0), axis=0, keepdims=True)
        for r in range(RANK)
    ]
    out[...] = (jnp.concatenate(rows, axis=0) + jnp.where(used == 0, first, 0.0)).astype(BF16)


def base_out_kernel(attended, weight, out, total):
    total[...] = jnp.zeros_like(total)

    @pl.loop(0, N)
    def _(t):
        part = attended[:, t].reshape(ALL_ROWS, QF)
        total[...] += jnp.dot(part, weight[t], preferred_element_type=F32)

    out[...] = total[...]


def final_kernel(parts, entry, base, up, out):
    shrunk = jnp.sum(parts[...].astype(F32), axis=0).astype(BF16).astype(F32)
    wide = expand(shrunk, entry[...])
    total = base[...] + low_rank_scale * contract(wide, up[...])
    for t in range(N):
        for s in range(STEPS):
            low = t * MINE + s * LOCAL
            out[s, t * LOCAL : (t + 1) * LOCAL, :] = total[low : low + LOCAL]


def shard(
    hidden, w_query, w_key, w_value, w_out, key_cache, value_cache, lengths, row_slot, evict_slot,
    evict_adapter, owner, pool_a_in, pool_b_q, pool_b_k, pool_b_v, pool_a_o, pool_b_o,
    slot_a_in, slot_b_q, slot_b_k, slot_b_v, slot_a_o, slot_b_o,
):
    me = lax.axis_index("group")
    part = lax.axis_index("tp")

    with jax.named_scope("gather_in_maps"):
        whole_in = lax.all_gather(pool_a_in, "group").reshape(N * HELD, IN_RANK, IN_PART)

    with jax.named_scope("positions"):
        position = jnp.sum(
            jnp.where(evict_adapter[..., None] == jnp.arange(N * HELD), owner, 0), axis=-1
        )
        wanted = position.reshape(STEPS, N, LOADS).transpose(1, 0, 2).reshape(N, STEPS * LOADS)
        targets = lax.dynamic_slice_in_dim(evict_slot, me * LOADS, LOADS, 1)
        survivor = SLOTS * (SLOTS - 1) // 2 - jnp.sum(targets[0])
        placed = targets[:, :, None] == jnp.arange(SLOTS)
        order = 1 + jnp.arange(STEPS * LOADS).reshape(STEPS, LOADS, 1)
        slot_entry = jnp.sum(jnp.where(placed, order, 0), axis=1)
        second = jnp.where(slot_entry[1] > 0, slot_entry[1], slot_entry[0])
        slot_entry = jnp.stack([slot_entry[0], second])
        entry = jnp.sum(
            jnp.where(
                row_slot[:, :, None] == jnp.arange(SLOTS), slot_entry[:, None, :], 0
            ),
            axis=-1,
        )
        by_step = entry.reshape(1, ALL_ROWS)
        by_owner = entry.reshape(STEPS, N, LOCAL).transpose(1, 0, 2).reshape(1, ALL_ROWS)
        my_wanted = lax.dynamic_index_in_dim(wanted, me, 0, keepdims=False)
        index = jnp.concatenate([survivor[None], my_wanted]).astype(jnp.int32)

    with jax.named_scope("exchange_rest"):
        rest = jnp.concatenate([pool_b_q, pool_b_k, pool_b_v, pool_a_o, pool_b_o], axis=2)
        width = rest.shape[2]
        by_rank = lax.all_to_all(
            rest.transpose(1, 0, 2), "group", split_axis=0, concat_axis=0, tiled=True
        ).reshape(N * HELD, width)
        pick = (wanted.reshape(-1, 1) == jnp.arange(N * HELD)).astype(BF16)
        sent = jnp.dot(pick, by_rank, preferred_element_type=F32).astype(BF16)
        loaded = lax.all_to_all(
            sent.reshape(N, STEPS * LOADS, width), "group", split_axis=0, concat_axis=0, tiled=True
        ).reshape(RANK * STEPS * LOADS, width)
        kept = jnp.concatenate(
            [
                lax.dynamic_index_in_dim(piece, survivor, 0, keepdims=False)
                for piece in (slot_b_q, slot_b_k, slot_b_v, slot_a_o, slot_b_o)
            ],
            axis=1,
        )
        ends = (QF, QF + 2 * KF, 2 * QF + 2 * KF)
        up = jnp.concatenate([loaded, kept], axis=0)
        up_q, up_kv, up_o = up[:, : ends[0]], up[:, ends[0] : ends[1]], up[:, ends[2] :]
        out_maps, out_kept = loaded[:, ends[1] : ends[2]], kept[:, ends[1] : ends[2]]

    with jax.named_scope("columns_of_w_out"):
        columns = lax.all_to_all(
            w_out.reshape(QF, N, OUT_PART).transpose(1, 0, 2),
            "tp", split_axis=0, concat_axis=0, tiled=True,
        )

    with jax.named_scope("base_projections"):
        tokens = hidden.reshape(ALL_ROWS, -1)
        base_q = jnp.dot(tokens, w_query, preferred_element_type=F32)
        base_kv = jnp.concatenate(
            [
                jnp.dot(tokens, w_key, preferred_element_type=F32),
                jnp.dot(tokens, w_value, preferred_element_type=F32),
            ],
            axis=1,
        )
        tokens_part = lax.dynamic_slice_in_dim(tokens, part * IN_PART, IN_PART, 1)

    with jax.named_scope("shrink"):
        partial_in = pl.pallas_call(
            shrink_kernel,
            out_shape=jax.ShapeDtypeStruct((IN_RANK, ALL_ROWS), BF16),
            in_specs=[smem(), hbm(), hbm(), vmem(), vmem()],
            out_specs=vmem(),
            scratch_shapes=[
                pltpu.VMEM((ENTRIES * IN_RANK, IN_PART), BF16),
                pltpu.SemaphoreType.DMA((ENTRIES,)),
            ],
            compiler_params=params(),
            cost_estimate=cost(2 * ENTRIES * IN_RANK * IN_PART * ALL_ROWS, 2 << 20),
            name="shrink",
        )(index, whole_in, slot_a_in, tokens_part, by_step)
        copies = jnp.broadcast_to(partial_in, (N, IN_RANK, ALL_ROWS))
        partials = lax.all_to_all(copies, "tp", split_axis=0, concat_axis=0, tiled=True)

    with jax.named_scope("project"):
        projected = pl.pallas_call(
            project_kernel,
            out_shape=jax.ShapeDtypeStruct((N, MINE, QF + 2 * KF), F32),
            in_specs=[vmem()] * 6,
            out_specs=vmem(),
            compiler_params=params(),
            cost_estimate=cost(2 * 400 * 512 * ALL_ROWS, 1 << 20),
            name="project",
        )(partials, by_step, base_q, base_kv, up_q, up_kv)
        received = lax.all_to_all(
            projected.astype(BF16), "tp", split_axis=0, concat_axis=0, tiled=True
        )

    with jax.named_scope("attend"):
        received = received.reshape(N, STEPS, LOCAL, QF + 2 * KF)
        queries = received[..., :QF].reshape(N, STEPS, LOCAL, 2, HD)
        queries = queries.transpose(2, 1, 3, 0, 4).reshape(LOCAL, STEPS * QH, HD)
        fresh = received[..., QF:].reshape(N, STEPS, LOCAL, 2, KF)
        fresh = fresh.transpose(3, 2, 1, 0, 4).reshape(2, LOCAL, STEPS, KW)
        attended = pl.pallas_call(
            attend_kernel,
            out_shape=jax.ShapeDtypeStruct((LOCAL, STEPS * QH, HD), BF16),
            grid_spec=pltpu.PrefetchScalarGridSpec(
                num_scalar_prefetch=1,
                grid=(LOCAL,),
                in_specs=[
                    pl.BlockSpec((1, STEPS * QH, HD), lambda i, _: (i, 0, 0)),
                    pl.BlockSpec((1, STEPS, KW), lambda i, _: (i, 0, 0)),
                    pl.BlockSpec((1, STEPS, KW), lambda i, _: (i, 0, 0)),
                    pl.BlockSpec((1, LENGTH, KW), lambda i, _: (i, 0, 0)),
                    pl.BlockSpec((1, LENGTH, KW), lambda i, _: (i, 0, 0)),
                ],
                out_specs=pl.BlockSpec((1, STEPS * QH, HD), lambda i, _: (i, 0, 0)),
            ),
            compiler_params=params(),
            cost_estimate=cost(4 * LOCAL * 64 * KW * LENGTH, 8 << 20),
            name="attend",
        )(lengths, queries, fresh[0], fresh[1], key_cache, value_cache)
        attended = attended.reshape(LOCAL, STEPS, 2, N, HD).transpose(3, 1, 0, 2, 4)
        attended = attended.reshape(N, MINE, QF)
        gathered = lax.all_to_all(
            jnp.broadcast_to(attended, (N, N, MINE, QF)),
            "tp", split_axis=0, concat_axis=0, tiled=True,
        )

    with jax.named_scope("output"):
        own_heads = lax.dynamic_index_in_dim(gathered, part, 1, keepdims=False)
        partial_out = pl.pallas_call(
            shrink_out_kernel,
            out_shape=jax.ShapeDtypeStruct((RANK, ALL_ROWS), BF16),
            in_specs=[vmem()] * 4,
            out_specs=vmem(),
            compiler_params=params(),
            cost_estimate=cost(2 * 400 * QF * ALL_ROWS, 1 << 20),
            name="shrink_out",
        )(own_heads, by_owner, out_maps, out_kept)
        partials_out = lax.all_to_all(
            jnp.broadcast_to(partial_out, (N, RANK, ALL_ROWS)),
            "tp", split_axis=0, concat_axis=0, tiled=True,
        )
        base_out = pl.pallas_call(
            base_out_kernel,
            out_shape=jax.ShapeDtypeStruct((ALL_ROWS, OUT_PART), F32),
            in_specs=[vmem()] * 2,
            out_specs=vmem(),
            scratch_shapes=[pltpu.VMEM((ALL_ROWS, OUT_PART), F32)],
            compiler_params=params(),
            cost_estimate=cost(2 * ALL_ROWS * FEATURES * OUT_PART, 6 << 20),
            name="base_out",
        )(gathered, columns)
        return pl.pallas_call(
            final_kernel,
            out_shape=jax.ShapeDtypeStruct((STEPS, ROWS, OUT_PART), F32),
            in_specs=[vmem()] * 4,
            out_specs=vmem(),
            compiler_params=params(),
            cost_estimate=cost(2 * 400 * OUT_PART * ALL_ROWS, 1 << 20),
            name="final",
        )(partials_out, by_owner, base_out, up_o).astype(BF16)


def solution(mesh):
    pooled = P("group", None, "tp")
    cached = P(("group", "tp"), None, None)
    placed = (
        P(None, "group", None), P(None, "tp"), P(None, "tp"), P(None, "tp"), P("tp", None),
        cached, cached, P(("group", "tp")), P(None, "group"), P(), P(), P(),
    ) + (pooled,) * 12
    return jax.shard_map(
        shard, mesh=mesh, in_specs=placed, out_specs=P(None, "group", "tp"), check_vma=False
    )
```

```python
import math

import jax
import jax.numpy as jnp
from jax import lax
from jax.experimental import pallas as pl
from jax.experimental.pallas import tpu as pltpu
from jax.sharding import PartitionSpec as P

QH = 32
KH = 4
HD = 128
STEPS = 2
ROWS = 128
RANK = 16
LOADS = 12
SLOTS = 13
HELD = 12
N = 16
ALL_ROWS = STEPS * ROWS
LOCAL = ROWS // N
MINE = STEPS * LOCAL
ENTRIES = 1 + STEPS * LOADS
IN_RANK = 3 * RANK
PER_DOT = 5
QF = 256
KF = 32
IN_PART = 512
OUT_PART = 512
FEATURES = QH * HD
LENGTH = 512
KW = KH * HD
BF16 = jnp.bfloat16
F32 = jnp.float32
low_rank_scale = 0.5


def vmem():
    return pl.BlockSpec(memory_space=pltpu.VMEM)


def hbm():
    return pl.BlockSpec(memory_space=pl.ANY)


def smem():
    return pl.BlockSpec(memory_space=pltpu.SMEM)


def params(mib=40):
    return pltpu.CompilerParams(vmem_limit_bytes=mib * 1024 * 1024)


def cost(flops, nbytes):
    return pl.CostEstimate(flops=flops, bytes_accessed=nbytes, transcendentals=0)


def shrink_kernel(index, pool, slot, tokens, entry, out, maps, arrived):
    copies = []
    for i in range(ENTRIES):
        origin = slot.at[index[0]] if i == 0 else pool.at[index[i]]
        copy = pltpu.make_async_copy(origin, maps.at[pl.ds(i * IN_RANK, IN_RANK)], arrived.at[i])
        copy.start()
        copies.append(copy)
    used = entry[...]
    total = jnp.zeros((IN_RANK, ALL_ROWS), F32)
    for first in range(0, ENTRIES, PER_DOT):
        for i in range(first, first + PER_DOT):
            copies[i].wait()
        block = maps[pl.ds(first * IN_RANK, PER_DOT * IN_RANK), :]
        product = lax.dot_general(
            block, tokens[...], (((1,), (1,)), ((), ())), preferred_element_type=F32
        )
        for k in range(PER_DOT):
            piece = product[k * IN_RANK : (k + 1) * IN_RANK]
            total = total + jnp.where(used == first + k, piece, 0.0)
    out[...] = total.astype(BF16)


def expand(shrunk, entry):
    loads = STEPS * LOADS
    load = lax.broadcasted_iota(jnp.int32, (loads, ALL_ROWS), 0) + 1
    chosen = load == entry
    blocks = [jnp.where(chosen, shrunk[r : r + 1, :], 0.0) for r in range(RANK)]
    kept = jnp.where(entry == 0, shrunk, 0.0)
    return jnp.concatenate(blocks + [kept], axis=0).astype(BF16)


def contract(left, right):
    return lax.dot_general(left, right, (((0,), (0,)), ((), ())), preferred_element_type=F32)


def project_kernel(parts, entry, base_q, base_kv, up_q, up_kv, out):
    shrunk = jnp.sum(parts[...].astype(F32), axis=0).astype(BF16).astype(F32)
    used = entry[...]
    wide_q = expand(shrunk[:RANK], used)
    wide_k = expand(shrunk[RANK : 2 * RANK], used)
    wide_v = expand(shrunk[2 * RANK :], used)
    query = base_q[...] + low_rank_scale * contract(wide_q, up_q[...])
    delta_k = contract(wide_k, up_kv[...])
    delta_v = contract(wide_v, up_kv[...])
    column = lax.broadcasted_iota(jnp.int32, delta_k.shape, 1)
    delta = jnp.where(column < KF, delta_k, delta_v)
    fresh = base_kv[...] + low_rank_scale * delta
    for t in range(N):
        for s in range(STEPS):
            low = s * ROWS + t * LOCAL
            out[t, s * LOCAL : (s + 1) * LOCAL, :QF] = query[low : low + LOCAL]
            out[t, s * LOCAL : (s + 1) * LOCAL, QF:] = fresh[low : low + LOCAL]


def attend_kernel(lengths, queries, keys_new, values_new, keys, values, out):
    row = pl.program_id(0)
    length = lengths[row]
    position = lax.broadcasted_iota(jnp.int32, (LENGTH, 1), 0)
    first, second = position == length, position == length + 1
    key_rows = keys[0]
    value_rows = values[0]
    key_rows = jnp.where(first, keys_new[0, 0:1], jnp.where(second, keys_new[0, 1:2], key_rows))
    value_rows = jnp.where(
        first, values_new[0, 0:1], jnp.where(second, values_new[0, 1:2], value_rows)
    )
    head_rows = STEPS * QH
    group = lax.broadcasted_iota(jnp.int32, (head_rows, KW), 0) % N // (N // KH)
    own = group == lax.broadcasted_iota(jnp.int32, (head_rows, KW), 1) // HD
    asked = queries[0]
    spread = jnp.where(own, jnp.concatenate([asked] * KH, axis=1), jnp.zeros((), BF16))
    scores = lax.dot_general(
        spread, key_rows, (((1,), (1,)), ((), ())), preferred_element_type=F32
    ) * (1.0 / math.sqrt(HD))
    step = lax.broadcasted_iota(jnp.int32, (head_rows, LENGTH), 0) // QH
    seen = lax.broadcasted_iota(jnp.int32, (head_rows, LENGTH), 1) <= length + step
    scores = jnp.where(seen, scores, -jnp.inf)
    weights = jnp.exp(scores - jnp.max(scores, axis=1, keepdims=True))
    totals = jnp.sum(weights, axis=1, keepdims=True)
    mixed = jnp.dot(weights.astype(BF16), value_rows, preferred_element_type=F32)
    mixed = jnp.where(own, mixed, 0.0)
    attended = mixed[:, :HD]
    for k in range(1, KH):
        attended = attended + mixed[:, k * HD : (k + 1) * HD]
    out[0] = (attended / totals).astype(BF16)


def shrink_out_kernel(attended, entry, maps, out):
    total = jnp.zeros((MINE, ENTRIES * RANK), F32)
    for t in range(N):
        total = total + lax.dot_general(
            attended[t], maps[t], (((1,), (1,)), ((), ())), preferred_element_type=F32
        )
    column = lax.broadcasted_iota(jnp.int32, total.shape, 1)
    placed = jnp.where(order_of(column) == entry[...], total, 0.0).astype(BF16)
    shape = (ENTRIES * RANK, QF)
    fold = rank_of(lax.broadcasted_iota(jnp.int32, shape, 0)) == lax.broadcasted_iota(
        jnp.int32, shape, 1
    )
    shrunk = jnp.dot(placed, fold.astype(BF16), preferred_element_type=F32)
    out[...] = shrunk.astype(BF16)


def order_of(column):
    loads = STEPS * LOADS
    return jnp.where(column < RANK * loads, column % loads + 1, 0)


def rank_of(column):
    loads = STEPS * LOADS
    return jnp.where(column < RANK * loads, column // loads, column - RANK * loads)


def output_kernel(index, side, attended, entry, mine, others, pool, slot, out, up, arrived):
    copies = []
    for i in range(ENTRIES):
        origin = slot.at[index[0]] if i == 0 else pool.at[index[i]]
        copy = pltpu.make_async_copy(origin, up.at[pl.ds(i * RANK, RANK)], arrived.at[i])
        copy.start()
        copies.append(copy)
    total = jnp.zeros((ALL_ROWS, OUT_PART), F32)
    for t in range(N):
        low = attended[:, t, :, : QF // 2].reshape(ALL_ROWS, QF // 2)
        high = attended[:, t, :, QF // 2 :].reshape(ALL_ROWS, QF // 2)
        near = jnp.where(side[0] == 0, low, high)
        far = jnp.where(side[0] == 0, high, low)
        left = jnp.concatenate([near, far], axis=1)
        right = jnp.concatenate([mine[t], others[t]], axis=0)
        total = total + jnp.dot(left, right, preferred_element_type=F32)
    shrunk = attended[:, N].reshape(ALL_ROWS, QF)
    shape = (QF, ENTRIES * RANK)
    repeat = lax.broadcasted_iota(jnp.int32, shape, 1) % RANK == lax.broadcasted_iota(
        jnp.int32, shape, 0
    )
    wide = jnp.dot(shrunk, repeat.astype(BF16), preferred_element_type=F32)
    column = lax.broadcasted_iota(jnp.int32, wide.shape, 1)
    wide = jnp.where(column // RANK == entry[...], wide, 0.0).astype(BF16)
    for copy in copies:
        copy.wait()
    total = total + low_rank_scale * jnp.dot(wide, up[...], preferred_element_type=F32)
    total = total.astype(BF16).astype(F32)
    for t in range(N):
        for s in range(STEPS):
            low = t * MINE + s * LOCAL
            out[s, t * LOCAL : (t + 1) * LOCAL, :] = total[low : low + LOCAL]


def shard(
    hidden, w_query, w_key, w_value, w_out, key_cache, value_cache, lengths, row_slot, evict_slot,
    evict_adapter, owner, pool_a_in, pool_b_q, pool_b_k, pool_b_v, pool_a_o, pool_b_o,
    slot_a_in, slot_b_q, slot_b_k, slot_b_v, slot_a_o, slot_b_o,
):
    me = lax.axis_index("group")
    part = lax.axis_index("tp")

    with jax.named_scope("gather_in_maps"):
        whole_in = lax.all_gather(pool_a_in, "group").reshape(N * HELD, IN_RANK, IN_PART)

    with jax.named_scope("positions"):
        position = jnp.sum(
            jnp.where(evict_adapter[..., None] == jnp.arange(N * HELD), owner, 0), axis=-1
        )
        wanted = position.reshape(STEPS, N, LOADS).transpose(1, 0, 2).reshape(N, STEPS * LOADS)
        targets = lax.dynamic_slice_in_dim(evict_slot, me * LOADS, LOADS, 1)
        survivor = SLOTS * (SLOTS - 1) // 2 - jnp.sum(targets[0])
        placed = targets[:, :, None] == jnp.arange(SLOTS)
        order = 1 + jnp.arange(STEPS * LOADS).reshape(STEPS, LOADS, 1)
        slot_entry = jnp.sum(jnp.where(placed, order, 0), axis=1)
        second = jnp.where(slot_entry[1] > 0, slot_entry[1], slot_entry[0])
        slot_entry = jnp.stack([slot_entry[0], second])
        entry = jnp.sum(
            jnp.where(
                row_slot[:, :, None] == jnp.arange(SLOTS), slot_entry[:, None, :], 0
            ),
            axis=-1,
        )
        by_step = entry.reshape(1, ALL_ROWS)
        by_owner = entry.reshape(STEPS, N, LOCAL).transpose(1, 0, 2)
        of_mine = lax.dynamic_index_in_dim(by_owner, part, 0, keepdims=False).reshape(MINE, 1)
        by_owner = by_owner.reshape(ALL_ROWS, 1)
        my_wanted = lax.dynamic_index_in_dim(wanted, me, 0, keepdims=False)
        index = jnp.concatenate([survivor[None], my_wanted]).astype(jnp.int32)

    with jax.named_scope("exchange_rest"):
        rest = jnp.concatenate([pool_b_q, pool_b_k, pool_b_v, pool_a_o], axis=2)
        width = rest.shape[2]
        by_rank = lax.all_to_all(
            rest.transpose(1, 0, 2), "group", split_axis=0, concat_axis=0, tiled=True
        ).reshape(N * HELD, width)
        pick = (wanted.reshape(-1, 1) == jnp.arange(N * HELD)).astype(BF16)
        sent = jnp.dot(pick, by_rank, preferred_element_type=F32).astype(BF16)
        loaded = lax.all_to_all(
            sent.reshape(N, STEPS * LOADS, width), "group", split_axis=0, concat_axis=0, tiled=True
        ).reshape(RANK * STEPS * LOADS, width)
        kept = jnp.concatenate(
            [
                lax.dynamic_index_in_dim(piece, survivor, 0, keepdims=False)
                for piece in (slot_b_q, slot_b_k, slot_b_v, slot_a_o)
            ],
            axis=1,
        )
        up = jnp.concatenate([loaded, kept], axis=0)
        up_q, up_kv, out_maps = up[:, :QF], up[:, QF : QF + 2 * KF], up[:, QF + 2 * KF :]
        whole_out_maps = lax.all_gather(out_maps, "tp")

    with jax.named_scope("columns_of_w_out"):
        side = me % 2
        half = lax.dynamic_slice_in_dim(w_out, side * (QF // 2), QF // 2, 0)
        half = jnp.stack([half[:, t * OUT_PART : (t + 1) * OUT_PART] for t in range(N)])
        mine = lax.all_to_all(half, "tp", split_axis=0, concat_axis=0, tiled=True)
        others = lax.ppermute(mine, "group", [(i, i ^ 1) for i in range(N)])

    with jax.named_scope("base_projections"):
        tokens = hidden.reshape(ALL_ROWS, -1)
        base_q = jnp.dot(tokens, w_query, preferred_element_type=F32)
        base_kv = jnp.concatenate(
            [
                jnp.dot(tokens, w_key, preferred_element_type=F32),
                jnp.dot(tokens, w_value, preferred_element_type=F32),
            ],
            axis=1,
        )
        tokens_part = lax.dynamic_slice_in_dim(tokens, part * IN_PART, IN_PART, 1)

    with jax.named_scope("shrink"):
        partial_in = pl.pallas_call(
            shrink_kernel,
            out_shape=jax.ShapeDtypeStruct((IN_RANK, ALL_ROWS), BF16),
            in_specs=[smem(), hbm(), hbm(), vmem(), vmem()],
            out_specs=vmem(),
            scratch_shapes=[
                pltpu.VMEM((ENTRIES * IN_RANK, IN_PART), BF16),
                pltpu.SemaphoreType.DMA((ENTRIES,)),
            ],
            compiler_params=params(56),
            cost_estimate=cost(2 * ENTRIES * IN_RANK * IN_PART * ALL_ROWS, 2 << 20),
            name="shrink",
        )(index, whole_in, slot_a_in, tokens_part, by_step)
        partial_in, mine = lax.optimization_barrier((partial_in, mine))
        partial_in, pool_b_o = lax.optimization_barrier((partial_in, pool_b_o))
        whole_b_o = lax.all_gather(pool_b_o, "group").reshape(N * HELD, RANK, OUT_PART)
        copies = jnp.broadcast_to(partial_in, (N, IN_RANK, ALL_ROWS))
        partials = lax.all_to_all(copies, "tp", split_axis=0, concat_axis=0, tiled=True)

    with jax.named_scope("project"):
        projected = pl.pallas_call(
            project_kernel,
            out_shape=jax.ShapeDtypeStruct((N, MINE, QF + 2 * KF), F32),
            in_specs=[vmem()] * 6,
            out_specs=vmem(),
            compiler_params=params(),
            cost_estimate=cost(2 * 400 * 512 * ALL_ROWS, 1 << 20),
            name="project",
        )(partials, by_step, base_q, base_kv, up_q, up_kv)
        received = lax.all_to_all(
            projected.astype(BF16), "tp", split_axis=0, concat_axis=0, tiled=True
        )

    with jax.named_scope("attend"):
        received = received.reshape(N, STEPS, LOCAL, QF + 2 * KF)
        queries = received[..., :QF].reshape(N, STEPS, LOCAL, 2, HD)
        queries = queries.transpose(2, 1, 3, 0, 4).reshape(LOCAL, STEPS * QH, HD)
        fresh = received[..., QF:].reshape(N, STEPS, LOCAL, 2, KF)
        fresh = fresh.transpose(3, 2, 1, 0, 4).reshape(2, LOCAL, STEPS, KW)
        attended = pl.pallas_call(
            attend_kernel,
            out_shape=jax.ShapeDtypeStruct((LOCAL, STEPS * QH, HD), BF16),
            grid_spec=pltpu.PrefetchScalarGridSpec(
                num_scalar_prefetch=1,
                grid=(LOCAL,),
                in_specs=[
                    pl.BlockSpec((1, STEPS * QH, HD), lambda i, _: (i, 0, 0)),
                    pl.BlockSpec((1, STEPS, KW), lambda i, _: (i, 0, 0)),
                    pl.BlockSpec((1, STEPS, KW), lambda i, _: (i, 0, 0)),
                    pl.BlockSpec((1, LENGTH, KW), lambda i, _: (i, 0, 0)),
                    pl.BlockSpec((1, LENGTH, KW), lambda i, _: (i, 0, 0)),
                ],
                out_specs=pl.BlockSpec((1, STEPS * QH, HD), lambda i, _: (i, 0, 0)),
            ),
            compiler_params=params(56),
            cost_estimate=cost(4 * LOCAL * 64 * KW * LENGTH, 8 << 20),
            name="attend",
        )(lengths, queries, fresh[0], fresh[1], key_cache, value_cache)
        attended = attended.reshape(LOCAL, STEPS, 2, N, HD).transpose(3, 1, 0, 2, 4)
        attended = attended.reshape(N, MINE, QF)
        shrunk_out = pl.pallas_call(
            shrink_out_kernel,
            out_shape=jax.ShapeDtypeStruct((MINE, QF), BF16),
            in_specs=[vmem()] * 3,
            out_specs=vmem(),
            compiler_params=params(),
            cost_estimate=cost(2 * 400 * FEATURES * MINE, 4 << 20),
            name="shrink_out",
        )(attended, of_mine, whole_out_maps)
        payload = jnp.concatenate([attended, shrunk_out[None]], axis=0)
        gathered = lax.all_to_all(
            jnp.broadcast_to(payload, (N, N + 1, MINE, QF)),
            "tp", split_axis=0, concat_axis=0, tiled=True,
        )

    with jax.named_scope("output"):
        return pl.pallas_call(
            output_kernel,
            out_shape=jax.ShapeDtypeStruct((STEPS, ROWS, OUT_PART), F32),
            in_specs=[smem(), smem(), vmem(), vmem(), vmem(), vmem(), hbm(), hbm()],
            out_specs=vmem(),
            scratch_shapes=[
                pltpu.VMEM((ENTRIES * RANK, OUT_PART), BF16),
                pltpu.SemaphoreType.DMA((ENTRIES,)),
            ],
            compiler_params=params(),
            cost_estimate=cost(2 * ALL_ROWS * (FEATURES + 400) * OUT_PART, 7 << 20),
            name="output",
        )(
            index, side[None], gathered, by_owner, mine, others, whole_b_o, slot_b_o
        ).astype(BF16)


def solution(mesh):
    pooled = P("group", None, "tp")
    cached = P(("group", "tp"), None, None)
    placed = (
        P(None, "group", None), P(None, "tp"), P(None, "tp"), P(None, "tp"), P("tp", None),
        cached, cached, P(("group", "tp")), P(None, "group"), P(), P(), P(),
    ) + (pooled,) * 12
    return jax.shard_map(
        shard, mesh=mesh, in_specs=placed, out_specs=P(None, "group", "tp"), check_vma=False
    )
```

```python
import math

import jax
import jax.numpy as jnp
from jax import lax
from jax.experimental import pallas as pl
from jax.experimental.pallas import tpu as pltpu
from jax.sharding import PartitionSpec as P

QH = 32
KH = 4
HD = 128
STEPS = 2
ROWS = 128
RANK = 16
LOADS = 12
SLOTS = 13
HELD = 12
N = 16
ALL_ROWS = STEPS * ROWS
LOCAL = ROWS // N
MINE = STEPS * LOCAL
ENTRIES = 1 + STEPS * LOADS
IN_RANK = 3 * RANK
PER_DOT = 5
QF = 256
KF = 32
IN_PART = 512
OUT_PART = 512
FEATURES = QH * HD
LENGTH = 512
KW = KH * HD
BF16 = jnp.bfloat16
F32 = jnp.float32
low_rank_scale = 0.5


def vmem():
    return pl.BlockSpec(memory_space=pltpu.VMEM)


def hbm():
    return pl.BlockSpec(memory_space=pl.ANY)


def smem():
    return pl.BlockSpec(memory_space=pltpu.SMEM)


def params(mib=40):
    return pltpu.CompilerParams(vmem_limit_bytes=mib * 1024 * 1024)


def cost(flops, nbytes):
    return pl.CostEstimate(flops=flops, bytes_accessed=nbytes, transcendentals=0)


def iota(shape, axis):
    return lax.broadcasted_iota(jnp.int32, shape, axis)


def shrink_kernel(index, pool, slot, tokens, entry, out, maps, arrived):
    copies = []
    for i in range(ENTRIES):
        origin = slot.at[index[0]] if i == 0 else pool.at[index[i]]
        copy = pltpu.make_async_copy(origin, maps.at[pl.ds(i * IN_RANK, IN_RANK)], arrived.at[i])
        copy.start()
        copies.append(copy)
    used = entry[...]
    total = jnp.zeros((IN_RANK, ALL_ROWS), F32)
    for first in range(0, ENTRIES, PER_DOT):
        for i in range(first, first + PER_DOT):
            copies[i].wait()
        block = maps[pl.ds(first * IN_RANK, PER_DOT * IN_RANK), :]
        product = lax.dot_general(
            block, tokens[...], (((1,), (1,)), ((), ())), preferred_element_type=F32
        )
        for k in range(PER_DOT):
            piece = product[k * IN_RANK : (k + 1) * IN_RANK]
            total = total + jnp.where(used == first + k, piece, 0.0)
    out[...] = total.astype(BF16)


def expand(shrunk, entry):
    loads = STEPS * LOADS
    load = iota((loads, ALL_ROWS), 0) + 1
    chosen = load == entry
    blocks = [jnp.where(chosen, shrunk[r : r + 1, :], 0.0) for r in range(RANK)]
    kept = jnp.where(entry == 0, shrunk, 0.0)
    return jnp.concatenate(blocks + [kept], axis=0).astype(BF16)


def contract(left, right):
    return lax.dot_general(left, right, (((0,), (0,)), ((), ())), preferred_element_type=F32)


def project_kernel(parts, entry, base_q, base_kv, up_q, up_kv, out):
    shrunk = jnp.sum(parts[...].astype(F32), axis=0).astype(BF16).astype(F32)
    used = entry[...]
    wide_q = expand(shrunk[:RANK], used)
    wide_k = expand(shrunk[RANK : 2 * RANK], used)
    wide_v = expand(shrunk[2 * RANK :], used)
    query = base_q[...] + low_rank_scale * contract(wide_q, up_q[...])
    delta_k = contract(wide_k, up_kv[...])
    delta_v = contract(wide_v, up_kv[...])
    column = iota(delta_k.shape, 1)
    delta = jnp.where(column < KF, delta_k, delta_v)
    fresh = base_kv[...] + low_rank_scale * delta
    for t in range(N):
        lows = [s * ROWS + t * LOCAL for s in range(STEPS)]
        out[t, :, :QF] = jnp.concatenate([query[n : n + LOCAL] for n in lows], 0).astype(BF16)
        out[t, :, QF:] = jnp.concatenate([fresh[n : n + LOCAL] for n in lows], 0).astype(BF16)


def split_kernel(side, weight, out, arrived):
    rows = pl.ds(pl.multiple_of(side[0] * (QF // 2), QF // 2), QF // 2)
    copies = [
        pltpu.make_async_copy(
            weight.at[rows, pl.ds(t * OUT_PART, OUT_PART)], out.at[t], arrived.at[t]
        )
        for t in range(N)
    ]
    for copy in copies:
        copy.start()
    for copy in copies:
        copy.wait()


def transposing():
    shape = (N * MINE, N * MINE)
    row, column = iota(shape, 0), iota(shape, 1)
    return ((row // N == column % N) & (row % N == column // N)).astype(BF16)


def attend_kernel(
    lengths, received, entry, keys, values, maps, out, key_rows, value_rows, map_rows, by_row,
    key_sem, value_sem, map_sem,
):
    loads = []
    for i in range(LOCAL):
        pair = (
            pltpu.make_async_copy(keys.at[i], key_rows.at[i], key_sem.at[i]),
            pltpu.make_async_copy(values.at[i], value_rows.at[i], value_sem.at[i]),
        )
        for copy in pair:
            copy.start()
        loads.append(pair)
    maps_load = pltpu.make_async_copy(maps, map_rows, map_sem)
    maps_load.start()

    swap = transposing()
    mine = jnp.dot(swap, received[...].reshape(N * MINE, -1), preferred_element_type=F32)
    mine = mine.astype(BF16)
    shape = (2 * KF, KW)
    feature, column = iota(shape, 0), iota(shape, 1) % KF
    block = iota((N * MINE, KW), 1) // KF == iota((N * MINE, KW), 0) % N
    fold = (iota((MINE, N * MINE), 1) // N == iota((MINE, N * MINE), 0)).astype(BF16)

    def fresh(first):
        repeat = (feature - first == column).astype(BF16)
        wide = jnp.dot(mine[:, QF:], repeat, preferred_element_type=F32)
        wide = jnp.where(block, wide, 0.0).astype(BF16)
        return jnp.dot(fold, wide, preferred_element_type=F32).astype(BF16)

    keys_new, values_new = fresh(0), fresh(KF)

    head_rows = STEPS * QH
    own = iota((head_rows, KW), 0) % N // (N // KH) == iota((head_rows, KW), 1) // HD
    place = iota((head_rows, LENGTH), 1)
    shape = (head_rows, MINE)
    new_step, new_row = iota(shape, 1) // LOCAL, iota(shape, 1) % LOCAL
    in_time = new_step <= iota(shape, 0) // QH
    scale = 1.0 / math.sqrt(HD)
    dims = (((1,), (1,)), ((), ()))
    for i in range(LOCAL):
        asked = []
        for s in range(STEPS):
            low = (s * LOCAL + i) * N
            asked += [mine[low : low + N, :HD], mine[low : low + N, HD:QF]]
        asked = jnp.concatenate(asked, axis=0)
        spread = jnp.where(own, jnp.concatenate([asked] * KH, axis=1), jnp.zeros((), BF16))
        new = lax.dot_general(spread, keys_new, dims, preferred_element_type=F32) * scale
        new = jnp.where(in_time & (new_row == i), new, -jnp.inf)
        loads[i][0].wait()
        old = lax.dot_general(spread, key_rows[i], dims, preferred_element_type=F32) * scale
        old = jnp.where(place < lengths[i], old, -jnp.inf)
        highest = jnp.maximum(
            jnp.max(old, axis=1, keepdims=True), jnp.max(new, axis=1, keepdims=True)
        )
        old, new = jnp.exp(old - highest), jnp.exp(new - highest)
        totals = jnp.sum(old, axis=1, keepdims=True) + jnp.sum(new, axis=1, keepdims=True)
        loads[i][1].wait()
        mixed = jnp.dot(old.astype(BF16), value_rows[i], preferred_element_type=F32)
        mixed = mixed + jnp.dot(new.astype(BF16), values_new, preferred_element_type=F32)
        mixed = jnp.where(own, mixed, 0.0)
        attended = mixed[:, :HD]
        for k in range(1, KH):
            attended = attended + mixed[:, k * HD : (k + 1) * HD]
        attended = (attended / totals).astype(BF16)
        for s in range(STEPS):
            low = (s * LOCAL + i) * N
            for half in range(2):
                piece = attended[(2 * s + half) * N : (2 * s + half + 1) * N]
                by_row[low : low + N, half * HD : (half + 1) * HD] = piece

    attended = jnp.dot(swap, by_row[...], preferred_element_type=F32).astype(BF16)
    maps_load.wait()
    total = jnp.zeros((MINE, ENTRIES * RANK), F32)
    for t in range(N):
        total = total + lax.dot_general(
            attended[t * MINE : (t + 1) * MINE], map_rows[t], dims, preferred_element_type=F32
        )
    column = iota(total.shape, 1)
    placed = jnp.where(order_of(column) == entry[...], total, 0.0).astype(BF16)
    shape = (ENTRIES * RANK, QF)
    gather = (rank_of(iota(shape, 0)) == iota(shape, 1)).astype(BF16)
    shrunk = jnp.dot(placed, gather, preferred_element_type=F32).astype(BF16)
    for n in range(N):
        for t in range(N):
            out[n, t] = attended[t * MINE : (t + 1) * MINE]
        out[n, N] = shrunk


def order_of(column):
    loads = STEPS * LOADS
    return jnp.where(column < RANK * loads, column % loads + 1, 0)


def rank_of(column):
    loads = STEPS * LOADS
    return jnp.where(column < RANK * loads, column // loads, column - RANK * loads)


def output_kernel(index, side, attended, entry, mine, others, pool, slot, out, up, arrived):
    copies = []
    for i in range(ENTRIES):
        origin = slot.at[index[0]] if i == 0 else pool.at[index[i]]
        copy = pltpu.make_async_copy(origin, up.at[pl.ds(i * RANK, RANK)], arrived.at[i])
        copy.start()
        copies.append(copy)
    total = jnp.zeros((ALL_ROWS, OUT_PART), F32)
    for t in range(N):
        low = attended[:, t, :, : QF // 2].reshape(ALL_ROWS, QF // 2)
        high = attended[:, t, :, QF // 2 :].reshape(ALL_ROWS, QF // 2)
        near = jnp.where(side[0] == 0, low, high)
        far = jnp.where(side[0] == 0, high, low)
        left = jnp.concatenate([near, far], axis=1)
        right = jnp.concatenate([mine[t], others[t]], axis=0)
        total = total + jnp.dot(left, right, preferred_element_type=F32)
    shrunk = attended[:, N].reshape(ALL_ROWS, QF)
    shape = (QF, ENTRIES * RANK)
    repeat = iota(shape, 1) % RANK == lax.broadcasted_iota(
        jnp.int32, shape, 0
    )
    wide = jnp.dot(shrunk, repeat.astype(BF16), preferred_element_type=F32)
    column = iota(wide.shape, 1)
    wide = jnp.where(column // RANK == entry[...], wide, 0.0).astype(BF16)
    for copy in copies:
        copy.wait()
    total = total + low_rank_scale * jnp.dot(wide, up[...], preferred_element_type=F32)
    for s in range(STEPS):
        lows = [t * MINE + s * LOCAL for t in range(N)]
        out[s] = jnp.concatenate([total[n : n + LOCAL] for n in lows], axis=0).astype(BF16)


def shard(
    hidden, w_query, w_key, w_value, w_out, key_cache, value_cache, lengths, row_slot, evict_slot,
    evict_adapter, owner, pool_a_in, pool_b_q, pool_b_k, pool_b_v, pool_a_o, pool_b_o,
    slot_a_in, slot_b_q, slot_b_k, slot_b_v, slot_a_o, slot_b_o,
):
    me = lax.axis_index("group")
    part = lax.axis_index("tp")

    with jax.named_scope("gather_in_maps"):
        whole_in = lax.all_gather(pool_a_in, "group").reshape(N * HELD, IN_RANK, IN_PART)

    with jax.named_scope("positions"):
        position = jnp.sum(
            jnp.where(evict_adapter[..., None] == jnp.arange(N * HELD), owner, 0), axis=-1
        )
        wanted = position.reshape(STEPS, N, LOADS).transpose(1, 0, 2).reshape(N, STEPS * LOADS)
        targets = lax.dynamic_slice_in_dim(evict_slot, me * LOADS, LOADS, 1)
        survivor = SLOTS * (SLOTS - 1) // 2 - jnp.sum(targets[0])
        placed = targets[:, :, None] == jnp.arange(SLOTS)
        order = 1 + jnp.arange(STEPS * LOADS).reshape(STEPS, LOADS, 1)
        slot_entry = jnp.sum(jnp.where(placed, order, 0), axis=1)
        second = jnp.where(slot_entry[1] > 0, slot_entry[1], slot_entry[0])
        slot_entry = jnp.stack([slot_entry[0], second])
        entry = jnp.sum(
            jnp.where(
                row_slot[:, :, None] == jnp.arange(SLOTS), slot_entry[:, None, :], 0
            ),
            axis=-1,
        )
        by_step = entry.reshape(1, ALL_ROWS)
        by_owner = entry.reshape(STEPS, N, LOCAL).transpose(1, 0, 2)
        of_mine = lax.dynamic_index_in_dim(by_owner, part, 0, keepdims=False).reshape(MINE, 1)
        by_owner = by_owner.reshape(ALL_ROWS, 1)
        my_wanted = lax.dynamic_index_in_dim(wanted, me, 0, keepdims=False)
        index = jnp.concatenate([survivor[None], my_wanted]).astype(jnp.int32)

    with jax.named_scope("columns_of_w_out"):
        side = (me % 2)[None]
        half = pl.pallas_call(
            split_kernel,
            out_shape=jax.ShapeDtypeStruct((N, QF // 2, OUT_PART), BF16),
            in_specs=[smem(), hbm()],
            out_specs=vmem(),
            scratch_shapes=[pltpu.SemaphoreType.DMA((N,))],
            compiler_params=params(56),
            cost_estimate=cost(0, 4 << 20),
            name="split",
        )(side, w_out)
        mine = lax.all_to_all(half, "tp", split_axis=0, concat_axis=0, tiled=True)
        others = lax.ppermute(mine, "group", [(i, i ^ 1) for i in range(N)])

    with jax.named_scope("base_projections"):
        tokens = hidden.reshape(ALL_ROWS, -1)
        base_q = jnp.dot(tokens, w_query, preferred_element_type=F32)
        base_kv = jnp.concatenate(
            [
                jnp.dot(tokens, w_key, preferred_element_type=F32),
                jnp.dot(tokens, w_value, preferred_element_type=F32),
            ],
            axis=1,
        )
        tokens_part = lax.dynamic_slice_in_dim(tokens, part * IN_PART, IN_PART, 1)

    with jax.named_scope("exchange_rest"):
        rest = jnp.concatenate([pool_b_q, pool_b_k, pool_b_v, pool_a_o], axis=2)
        width = rest.shape[2]
        rest, mine, base_q, base_kv, tokens_part = lax.optimization_barrier(
            (rest, mine, base_q, base_kv, tokens_part)
        )
        by_rank = lax.all_to_all(
            rest.transpose(1, 0, 2), "group", split_axis=0, concat_axis=0, tiled=True
        ).reshape(N * HELD, width)
        pick = (wanted.reshape(-1, 1) == jnp.arange(N * HELD)).astype(BF16)
        sent = jnp.dot(pick, by_rank, preferred_element_type=F32).astype(BF16)
        loaded = lax.all_to_all(
            sent.reshape(N, STEPS * LOADS, width), "group", split_axis=0, concat_axis=0, tiled=True
        ).reshape(RANK * STEPS * LOADS, width)
        kept = jnp.concatenate(
            [
                lax.dynamic_index_in_dim(piece, survivor, 0, keepdims=False)
                for piece in (slot_b_q, slot_b_k, slot_b_v, slot_a_o)
            ],
            axis=1,
        )
        up = jnp.concatenate([loaded, kept], axis=0)
        up_q, up_kv, out_maps = up[:, :QF], up[:, QF : QF + 2 * KF], up[:, QF + 2 * KF :]
        whole_out_maps = lax.all_gather(out_maps, "tp")

    with jax.named_scope("shrink"):
        partial_in = pl.pallas_call(
            shrink_kernel,
            out_shape=jax.ShapeDtypeStruct((IN_RANK, ALL_ROWS), BF16),
            in_specs=[smem(), hbm(), hbm(), vmem(), vmem()],
            out_specs=vmem(),
            scratch_shapes=[
                pltpu.VMEM((ENTRIES * IN_RANK, IN_PART), BF16),
                pltpu.SemaphoreType.DMA((ENTRIES,)),
            ],
            compiler_params=params(56),
            cost_estimate=cost(2 * ENTRIES * IN_RANK * IN_PART * ALL_ROWS, 2 << 20),
            name="shrink",
        )(index, whole_in, slot_a_in, tokens_part, by_step)
        partial_in, pool_b_o = lax.optimization_barrier((partial_in, pool_b_o))
        whole_b_o = lax.all_gather(pool_b_o, "group").reshape(N * HELD, RANK, OUT_PART)
        copies = jnp.broadcast_to(partial_in, (N, IN_RANK, ALL_ROWS))
        partials = lax.all_to_all(copies, "tp", split_axis=0, concat_axis=0, tiled=True)

    with jax.named_scope("project"):
        projected = pl.pallas_call(
            project_kernel,
            out_shape=jax.ShapeDtypeStruct((N, MINE, QF + 2 * KF), BF16),
            in_specs=[vmem()] * 6,
            out_specs=vmem(),
            compiler_params=params(),
            cost_estimate=cost(2 * 400 * 512 * ALL_ROWS, 1 << 20),
            name="project",
        )(partials, by_step, base_q, base_kv, up_q, up_kv)
        received = lax.all_to_all(projected, "tp", split_axis=0, concat_axis=0, tiled=True)

    with jax.named_scope("attend"):
        payload = pl.pallas_call(
            attend_kernel,
            out_shape=jax.ShapeDtypeStruct((N, N + 1, MINE, QF), BF16),
            in_specs=[smem(), vmem(), vmem(), hbm(), hbm(), hbm()],
            out_specs=vmem(),
            scratch_shapes=[
                pltpu.VMEM((LOCAL, LENGTH, KW), BF16),
                pltpu.VMEM((LOCAL, LENGTH, KW), BF16),
                pltpu.VMEM((N, ENTRIES * RANK, QF), BF16),
                pltpu.VMEM((N * MINE, QF), BF16),
                pltpu.SemaphoreType.DMA((LOCAL,)),
                pltpu.SemaphoreType.DMA((LOCAL,)),
                pltpu.SemaphoreType.DMA,
            ],
            compiler_params=params(56),
            cost_estimate=cost(4 * LOCAL * 64 * KW * LENGTH, 12 << 20),
            name="attend",
        )(lengths, received, of_mine, key_cache, value_cache, whole_out_maps)
        gathered = lax.all_to_all(payload, "tp", split_axis=0, concat_axis=0, tiled=True)

    with jax.named_scope("output"):
        return pl.pallas_call(
            output_kernel,
            out_shape=jax.ShapeDtypeStruct((STEPS, ROWS, OUT_PART), BF16),
            in_specs=[smem(), smem(), vmem(), vmem(), vmem(), vmem(), hbm(), hbm()],
            out_specs=vmem(),
            scratch_shapes=[
                pltpu.VMEM((ENTRIES * RANK, OUT_PART), BF16),
                pltpu.SemaphoreType.DMA((ENTRIES,)),
            ],
            compiler_params=params(56),
            cost_estimate=cost(2 * ALL_ROWS * (FEATURES + 400) * OUT_PART, 7 << 20),
            name="output",
        )(index, side, gathered, by_owner, mine, others, whole_b_o, slot_b_o)


def solution(mesh):
    pooled = P("group", None, "tp")
    cached = P(("group", "tp"), None, None)
    placed = (
        P(None, "group", None), P(None, "tp"), P(None, "tp"), P(None, "tp"), P("tp", None),
        cached, cached, P(("group", "tp")), P(None, "group"), P(), P(), P(),
    ) + (pooled,) * 12
    return jax.shard_map(
        shard, mesh=mesh, in_specs=placed, out_specs=P(None, "group", "tp"), check_vma=False
    )
```

```python
import math

import jax
import jax.numpy as jnp
from jax import lax
from jax.experimental import pallas as pl
from jax.experimental.pallas import tpu as pltpu
from jax.sharding import PartitionSpec as P

QH = 32
KH = 4
HD = 128
STEPS = 2
ROWS = 128
RANK = 16
LOADS = 12
SLOTS = 13
HELD = 12
N = 16
SIDE = 4
RING = 8
PAIR = 2
ALL_ROWS = STEPS * ROWS
LOCAL = ROWS // N
MINE = STEPS * LOCAL
ENTRIES = 1 + STEPS * LOADS
IN_RANK = 3 * RANK
PER_DOT = 5
QF = 256
KF = 32
IN_PART = 512
OUT_PART = 512
FEATURES = QH * HD
WIDE = RING * QF
QKV = QF + 2 * KF
TP = ("hi", "lo", "x")
AROUND = ("hi", "x")
LENGTH = 512
KW = KH * HD
BF16 = jnp.bfloat16
F32 = jnp.float32
low_rank_scale = 0.5


def vmem():
    return pl.BlockSpec(memory_space=pltpu.VMEM)


def hbm():
    return pl.BlockSpec(memory_space=pl.ANY)


def smem():
    return pl.BlockSpec(memory_space=pltpu.SMEM)


def params(mib=40):
    return pltpu.CompilerParams(vmem_limit_bytes=mib * 1024 * 1024)


def cost(flops, nbytes):
    return pl.CostEstimate(flops=flops, bytes_accessed=nbytes, transcendentals=0)


def iota(shape, axis):
    return lax.broadcasted_iota(jnp.int32, shape, axis)


def shrink_kernel(index, pool, slot, tokens, entry, out, maps, arrived):
    copies = []
    for i in range(ENTRIES):
        origin = slot.at[index[0]] if i == 0 else pool.at[index[i]]
        copy = pltpu.make_async_copy(origin, maps.at[pl.ds(i * IN_RANK, IN_RANK)], arrived.at[i])
        copy.start()
        copies.append(copy)
    used = entry[...]
    total = jnp.zeros((IN_RANK, ALL_ROWS), F32)
    for first in range(0, ENTRIES, PER_DOT):
        for i in range(first, first + PER_DOT):
            copies[i].wait()
        block = maps[pl.ds(first * IN_RANK, PER_DOT * IN_RANK), :]
        product = lax.dot_general(
            block, tokens[...], (((1,), (1,)), ((), ())), preferred_element_type=F32
        )
        for k in range(PER_DOT):
            piece = product[k * IN_RANK : (k + 1) * IN_RANK]
            total = total + jnp.where(used == first + k, piece, 0.0)
    total = total.astype(BF16)
    for n in range(N):
        out[n] = total


def expand(shrunk, entry):
    blocks = [jnp.where(entry == i, shrunk, 0.0) for i in range(ENTRIES)]
    return jnp.concatenate(blocks, axis=0).astype(BF16)


def expand_by_rank(shrunk, entry):
    loads = STEPS * LOADS
    chosen = iota((loads, ALL_ROWS), 0) + 1 == entry
    blocks = [jnp.where(chosen, shrunk[r : r + 1, :], 0.0) for r in range(RANK)]
    kept = jnp.where(entry == 0, shrunk, 0.0)
    return jnp.concatenate(blocks + [kept], axis=0).astype(BF16)


def contract(left, right):
    return lax.dot_general(left, right, (((0,), (0,)), ((), ())), preferred_element_type=F32)


def project_kernel(parts, entry, base_q, base_kv, up, out):
    shrunk = jnp.sum(parts[...].astype(F32), axis=0).astype(BF16).astype(F32)
    used = entry[...]
    up_q, up_kv = up[:, :QF], up[:, QF:]
    wide_q = expand_by_rank(shrunk[:RANK], used)
    wide_k = expand_by_rank(shrunk[RANK : 2 * RANK], used)
    wide_v = expand_by_rank(shrunk[2 * RANK :], used)
    query = base_q[...] + low_rank_scale * contract(wide_q, up_q)
    delta_k = contract(wide_k, up_kv)
    delta_v = contract(wide_v, up_kv)
    column = iota(delta_k.shape, 1)
    delta = jnp.where(column < KF, delta_k, delta_v)
    fresh = base_kv[...] + low_rank_scale * delta
    for t in range(N):
        lows = [s * ROWS + t * LOCAL for s in range(STEPS)]
        out[t, :, :QF] = jnp.concatenate([query[n : n + LOCAL] for n in lows], 0).astype(BF16)
        out[t, :, QF:] = jnp.concatenate([fresh[n : n + LOCAL] for n in lows], 0).astype(BF16)


def split_kernel(place, weight, *rest):
    outs, arrived = rest[:RING], rest[RING]
    copies = []
    for k in range(RING):
        other = lax.rem(place[0] + k, RING)
        for n in range(PAIR):
            block = (other // SIDE * PAIR + n) * SIDE + lax.rem(other, SIDE)
            column = pl.multiple_of(block * OUT_PART, OUT_PART)
            source = weight.at[:, pl.ds(column, OUT_PART)]
            copies.append(pltpu.make_async_copy(source, outs[k].at[n], arrived.at[k, n]))
    for copy in copies:
        copy.start()
    for copy in copies:
        copy.wait()


def transposing():
    shape = (N * MINE, N * MINE)
    row, column = iota(shape, 0), iota(shape, 1)
    return ((row // N == column % N) & (row % N == column // N)).astype(BF16)


def attend_kernel(
    lengths, received, keys, values, out, key_rows, value_rows, by_row, ready, key_sem, value_sem,
    sent,
):
    loads = []
    for i in range(LOCAL):
        pair = (
            pltpu.make_async_copy(keys.at[i], key_rows.at[i], key_sem.at[i]),
            pltpu.make_async_copy(values.at[i], value_rows.at[i], value_sem.at[i]),
        )
        for copy in pair:
            copy.start()
        loads.append(pair)
    swap = transposing()
    mine = jnp.dot(swap, received[...].reshape(N * MINE, -1), preferred_element_type=F32)
    mine = mine.astype(BF16)
    shape = (2 * KF, KW)
    feature, column = iota(shape, 0), iota(shape, 1) % KF
    block = iota((N * MINE, KW), 1) // KF == iota((N * MINE, KW), 0) % N
    fold = (iota((MINE, N * MINE), 1) // N == iota((MINE, N * MINE), 0)).astype(BF16)

    def fresh(first):
        repeat = (feature - first == column).astype(BF16)
        wide = jnp.dot(mine[:, QF:], repeat, preferred_element_type=F32)
        wide = jnp.where(block, wide, 0.0).astype(BF16)
        return jnp.dot(fold, wide, preferred_element_type=F32).astype(BF16)

    keys_new, values_new = fresh(0), fresh(KF)

    head_rows = STEPS * QH
    own = iota((head_rows, KW), 0) % N // (N // KH) == iota((head_rows, KW), 1) // HD
    place = iota((head_rows, LENGTH), 1)
    shape = (head_rows, MINE)
    new_step, new_row = iota(shape, 1) // LOCAL, iota(shape, 1) % LOCAL
    in_time = new_step <= iota(shape, 0) // QH
    scale = 1.0 / math.sqrt(HD)
    dims = (((1,), (1,)), ((), ()))
    for i in range(LOCAL):
        asked = []
        for s in range(STEPS):
            low = (s * LOCAL + i) * N
            asked += [mine[low : low + N, :HD], mine[low : low + N, HD:QF]]
        asked = jnp.concatenate(asked, axis=0)
        spread = jnp.where(own, jnp.concatenate([asked] * KH, axis=1), jnp.zeros((), BF16))
        new = lax.dot_general(spread, keys_new, dims, preferred_element_type=F32) * scale
        new = jnp.where(in_time & (new_row == i), new, -jnp.inf)
        loads[i][0].wait()
        old = lax.dot_general(spread, key_rows[i], dims, preferred_element_type=F32) * scale
        old = jnp.where(place < lengths[i], old, -jnp.inf)
        highest = jnp.maximum(
            jnp.max(old, axis=1, keepdims=True), jnp.max(new, axis=1, keepdims=True)
        )
        old, new = jnp.exp(old - highest), jnp.exp(new - highest)
        totals = jnp.sum(old, axis=1, keepdims=True) + jnp.sum(new, axis=1, keepdims=True)
        loads[i][1].wait()
        mixed = jnp.dot(old.astype(BF16), value_rows[i], preferred_element_type=F32)
        mixed = mixed + jnp.dot(new.astype(BF16), values_new, preferred_element_type=F32)
        mixed = jnp.where(own, mixed, 0.0)
        attended = mixed[:, :HD]
        for k in range(1, KH):
            attended = attended + mixed[:, k * HD : (k + 1) * HD]
        attended = (attended / totals).astype(BF16)
        for s in range(STEPS):
            low = (s * LOCAL + i) * N
            for half in range(2):
                piece = attended[(2 * s + half) * N : (2 * s + half + 1) * N]
                by_row[low : low + N, half * HD : (half + 1) * HD] = piece

    attended = jnp.dot(swap, by_row[...], preferred_element_type=F32).astype(BF16)
    for t in range(N):
        high, low, x = t // (PAIR * SIDE), t // SIDE % PAIR, t % SIDE
        ready[low, high * SIDE + x] = attended[t * MINE : (t + 1) * MINE]
    copies = [
        pltpu.make_async_copy(ready.at[n // SIDE % PAIR], out.at[n], sent.at[n]) for n in range(N)
    ]
    for copy in copies:
        copy.start()
    for copy in copies:
        copy.wait()


def pick_kernel(index, slot_in, slot_up, pool, maps, up, map_sem, up_sem):
    copies = []
    for i in range(ENTRIES):
        if i == 0:
            first, second = slot_in.at[index[0]], slot_up.at[index[0]]
        else:
            first = pool.at[index[i], :, pl.ds(0, QF)]
            second = pool.at[index[i], :, pl.ds(QF, OUT_PART)]
        rows = pl.ds(i * RANK, RANK)
        copies.append(pltpu.make_async_copy(first, maps.at[rows], map_sem.at[i]))
        copies.append(pltpu.make_async_copy(second, up.at[rows], up_sem.at[i]))
    for copy in copies:
        copy.start()
    for copy in copies:
        copy.wait()


def shrink_out_kernel(place, attended, entry, maps, out):
    heads = attended[:, pl.ds(place[0], 1)].reshape(ALL_ROWS, QF)
    product = lax.dot_general(
        maps[...], heads, (((1,), (1,)), ((), ())), preferred_element_type=F32
    )
    used = entry[...]
    shrunk = jnp.zeros((RANK, ALL_ROWS), F32)
    for i in range(ENTRIES):
        shrunk = shrunk + jnp.where(used == i, product[i * RANK : (i + 1) * RANK], 0.0)
    shrunk = shrunk.astype(BF16)
    for n in range(N):
        out[n] = shrunk


def base_out_kernel(place, member, attended, *rest):
    sources = rest[:RING]
    out, columns, column_sem = rest[RING:]
    copies = []
    for k in range(RING):
        copy = pltpu.make_async_copy(
            sources[k].at[member[0]], columns.at[pl.ds(k * QF, QF)], column_sem.at[k]
        )
        copy.start()
        copies.append(copy)
    heads = []
    for k in range(RING):
        block = lax.rem(place[0] + RING - k, RING)
        heads.append(attended[:, pl.ds(block, 1)].reshape(ALL_ROWS, QF))
    total = jnp.zeros((ALL_ROWS, OUT_PART), F32)
    for k in range(0, RING, PAIR):
        for copy in copies[k : k + PAIR]:
            copy.wait()
        part = jnp.concatenate(heads[k : k + PAIR], axis=1)
        rows = columns[k * QF : (k + PAIR) * QF]
        total = total + jnp.dot(part, rows, preferred_element_type=F32)
    out[...] = total.astype(out.dtype)


def final_kernel(parts, entry, kept, arrived, up, out):
    shrunk = jnp.sum(parts[...].astype(F32), axis=0).astype(BF16).astype(F32)
    wide = expand(shrunk, entry[...])
    total = kept[...] + arrived[...].astype(F32)
    total = total + low_rank_scale * contract(wide, up[...])
    for s in range(STEPS):
        lows = [t * MINE + s * LOCAL for t in range(N)]
        out[s] = jnp.concatenate([total[n : n + LOCAL] for n in lows], axis=0).astype(BF16)


def shard(
    hidden, w_query, w_key, w_value, w_out, key_cache, value_cache, lengths, row_slot, evict_slot,
    evict_adapter, owner, pool_a_in, pool_b_q, pool_b_k, pool_b_v, pool_a_o, pool_b_o,
    slot_a_in, slot_b_q, slot_b_k, slot_b_v, slot_a_o, slot_b_o,
):
    me = lax.axis_index("group")
    part = lax.axis_index(TP)
    place = lax.axis_index(AROUND)[None]
    member = lax.axis_index("lo")[None]

    with jax.named_scope("gather_in_maps"):
        whole_in = lax.all_gather(pool_a_in, "group").reshape(N * HELD, IN_RANK, IN_PART)

    with jax.named_scope("positions"):
        position = jnp.sum(
            jnp.where(evict_adapter[..., None] == jnp.arange(N * HELD), owner, 0), axis=-1
        )
        position = position.reshape(STEPS, N, LOADS)
        wanted = position.transpose(1, 0, 2).reshape(N, STEPS * LOADS)
        targets = lax.dynamic_slice_in_dim(evict_slot, me * LOADS, LOADS, 1)
        survivor = SLOTS * (SLOTS - 1) // 2 - jnp.sum(targets[0])
        placed = targets[:, :, None] == jnp.arange(SLOTS)
        order = 1 + jnp.arange(STEPS * LOADS).reshape(STEPS, LOADS, 1)
        slot_entry = jnp.sum(jnp.where(placed, order, 0), axis=1)
        second = jnp.where(slot_entry[1] > 0, slot_entry[1], slot_entry[0])
        slot_entry = jnp.stack([slot_entry[0], second])
        entry = jnp.sum(
            jnp.where(
                row_slot[:, :, None] == jnp.arange(SLOTS), slot_entry[:, None, :], 0
            ),
            axis=-1,
        )
        by_step = entry.reshape(1, ALL_ROWS)
        by_owner = entry.reshape(STEPS, N, LOCAL).transpose(1, 0, 2)
        by_owner = by_owner.reshape(1, ALL_ROWS)
        my_wanted = lax.dynamic_index_in_dim(position, me, 1, keepdims=False)
        my_wanted = my_wanted.reshape(STEPS * LOADS)
        index = jnp.concatenate([survivor[None], my_wanted]).astype(jnp.int32)

    turns = [[(i, (i + k) % RING) for i in range(RING)] for k in range(1, RING)]
    with jax.named_scope("columns_of_w_out"):
        block = jax.ShapeDtypeStruct((PAIR, QF, OUT_PART), BF16)
        columns = pl.pallas_call(
            split_kernel,
            out_shape=[block] * RING,
            in_specs=[smem(), hbm()],
            out_specs=[vmem()] * RING,
            scratch_shapes=[pltpu.SemaphoreType.DMA((RING, PAIR))],
            compiler_params=params(56),
            cost_estimate=cost(0, 8 << 20),
            name="split",
        )(place, w_out)

    with jax.named_scope("base_projections"):
        tokens = hidden.reshape(ALL_ROWS, -1)
        base_q = jnp.dot(tokens, w_query, preferred_element_type=F32)
        base_kv = jnp.concatenate(
            [
                jnp.dot(tokens, w_key, preferred_element_type=F32),
                jnp.dot(tokens, w_value, preferred_element_type=F32),
            ],
            axis=1,
        )
        tokens_part = lax.dynamic_slice_in_dim(tokens, part * IN_PART, IN_PART, 1)

    with jax.named_scope("exchange_up_maps"):
        rest = jnp.concatenate([pool_b_q, pool_b_k, pool_b_v], axis=2)
        rest, *columns = lax.optimization_barrier((rest, *columns))
        by_rank = lax.all_to_all(
            rest.transpose(1, 0, 2), "group", split_axis=0, concat_axis=0, tiled=True
        ).reshape(N * HELD, QKV)
        pick = (wanted.reshape(-1, 1) == jnp.arange(N * HELD)).astype(BF16)
        sent = jnp.dot(pick, by_rank, preferred_element_type=F32).astype(BF16)
        loaded = lax.all_to_all(
            sent.reshape(N, STEPS * LOADS, QKV), "group", split_axis=0, concat_axis=0, tiled=True
        ).reshape(RANK * STEPS * LOADS, QKV)
        columns = columns[:1] + [
            lax.ppermute(c, AROUND, turn) for c, turn in zip(columns[1:], turns)
        ]
        survived = lambda piece: lax.dynamic_index_in_dim(piece, survivor, 0, keepdims=False)
        kept = jnp.concatenate([survived(p) for p in (slot_b_q, slot_b_k, slot_b_v)], axis=1)
        up = jnp.concatenate([loaded, kept], axis=0)

    with jax.named_scope("gather_out_maps"):
        out_pool = jnp.concatenate([pool_a_o, pool_b_o], axis=2)
        out_pool, index, up, base_q, base_kv, tokens_part, *columns = lax.optimization_barrier(
            (out_pool, index, up, base_q, base_kv, tokens_part, *columns)
        )
        out_pool = lax.all_gather(out_pool, "group").reshape(N * HELD, RANK, QF + OUT_PART)

    with jax.named_scope("shrink"):
        partial_in = pl.pallas_call(
            shrink_kernel,
            out_shape=jax.ShapeDtypeStruct((N, IN_RANK, ALL_ROWS), BF16),
            in_specs=[smem(), hbm(), hbm(), vmem(), vmem()],
            out_specs=vmem(),
            scratch_shapes=[
                pltpu.VMEM((ENTRIES * IN_RANK, IN_PART), BF16),
                pltpu.SemaphoreType.DMA((ENTRIES,)),
            ],
            compiler_params=params(56),
            cost_estimate=cost(2 * ENTRIES * IN_RANK * IN_PART * ALL_ROWS, 2 << 20),
            name="shrink",
        )(index, whole_in, slot_a_in, tokens_part, by_step)
        partials = lax.all_to_all(partial_in, TP, split_axis=0, concat_axis=0, tiled=True)

    with jax.named_scope("project"):
        projected = pl.pallas_call(
            project_kernel,
            out_shape=jax.ShapeDtypeStruct((N, MINE, QF + 2 * KF), BF16),
            in_specs=[vmem()] * 5,
            out_specs=vmem(),
            compiler_params=params(16),
            cost_estimate=cost(2 * 400 * 512 * ALL_ROWS, 1 << 20),
            name="project",
        )(partials, by_step, base_q, base_kv, up)

    with jax.named_scope("attend"):
        received = lax.all_to_all(projected, TP, split_axis=0, concat_axis=0, tiled=True)
        payload = pl.pallas_call(
            attend_kernel,
            out_shape=jax.ShapeDtypeStruct((N, RING, MINE, QF), BF16),
            in_specs=[smem(), vmem(), hbm(), hbm()],
            out_specs=hbm(),
            scratch_shapes=[
                pltpu.VMEM((LOCAL, LENGTH, KW), BF16),
                pltpu.VMEM((LOCAL, LENGTH, KW), BF16),
                pltpu.VMEM((N * MINE, QF), BF16),
                pltpu.VMEM((PAIR, RING, MINE, QF), BF16),
                pltpu.SemaphoreType.DMA((LOCAL,)),
                pltpu.SemaphoreType.DMA((LOCAL,)),
                pltpu.SemaphoreType.DMA((N,)),
            ],
            compiler_params=params(56),
            cost_estimate=cost(4 * LOCAL * 64 * KW * LENGTH, 12 << 20),
            name="attend",
        )(lengths, received, key_cache, value_cache)
        gathered = lax.all_to_all(payload, TP, split_axis=0, concat_axis=0, tiled=True)

        payload, picks = lax.optimization_barrier((payload, index))
        maps, up_o = pl.pallas_call(
            pick_kernel,
            out_shape=[
                jax.ShapeDtypeStruct((ENTRIES * RANK, QF), BF16),
                jax.ShapeDtypeStruct((ENTRIES * RANK, OUT_PART), BF16),
            ],
            in_specs=[smem()] + [hbm()] * 3,
            out_specs=[vmem()] * 2,
            scratch_shapes=[pltpu.SemaphoreType.DMA((ENTRIES,))] * 2,
            compiler_params=params(56),
            cost_estimate=cost(0, 3 << 20),
            name="pick",
        )(picks, slot_a_o, slot_b_o, out_pool)

    with jax.named_scope("output"):
        partial_out = pl.pallas_call(
            shrink_out_kernel,
            out_shape=jax.ShapeDtypeStruct((N, RANK, ALL_ROWS), BF16),
            in_specs=[smem()] + [vmem()] * 3,
            out_specs=vmem(),
            compiler_params=params(16),
            cost_estimate=cost(2 * 400 * QF * ALL_ROWS, 1 << 20),
            name="shrink_out",
        )(place, gathered, by_owner, maps)
        partial_out, member = lax.optimization_barrier((partial_out, member))
        partials_out = lax.all_to_all(partial_out, TP, split_axis=0, concat_axis=0, tiled=True)

        def base_out(whose, dtype):
            return pl.pallas_call(
                base_out_kernel,
                out_shape=jax.ShapeDtypeStruct((ALL_ROWS, OUT_PART), dtype),
                in_specs=[smem()] * 2 + [vmem()] + [hbm()] * RING,
                out_specs=vmem(),
                scratch_shapes=[
                    pltpu.VMEM((RING * QF, OUT_PART), BF16),
                    pltpu.SemaphoreType.DMA((RING,)),
                ],
                compiler_params=params(56),
                cost_estimate=cost(2 * ALL_ROWS * WIDE * OUT_PART, 3 << 20),
                name="base_out",
            )(place, whose, gathered, *columns)

        passed = lax.ppermute(base_out(1 - member, BF16), "lo", [(0, 1), (1, 0)])
        kept_out = base_out(member, F32)
        return pl.pallas_call(
            final_kernel,
            out_shape=jax.ShapeDtypeStruct((STEPS, ROWS, OUT_PART), BF16),
            in_specs=[vmem()] * 5,
            out_specs=vmem(),
            compiler_params=params(16),
            cost_estimate=cost(2 * 400 * OUT_PART * ALL_ROWS, 1 << 20),
            name="final",
        )(partials_out, by_owner, kept_out, passed, up_o)


def solution(mesh):
    grid = jax.sharding.Mesh(mesh.devices.reshape(N, SIDE // PAIR, PAIR, SIDE), ("group",) + TP)
    pooled = P("group", None, TP)
    cached = P(("group",) + TP, None, None)
    placed = (
        P(None, "group", None), P(None, TP), P(None, TP), P(None, TP), P(TP, None),
        cached, cached, P(("group",) + TP), P(None, "group"), P(), P(), P(),
    ) + (pooled,) * 12
    return jax.shard_map(
        shard, mesh=grid, in_specs=placed, out_specs=P(None, "group", TP), check_vma=False
    )
```

```python
import math

import jax
import jax.numpy as jnp
from jax import lax
from jax.experimental import pallas as pl
from jax.experimental.pallas import tpu as pltpu
from jax.sharding import PartitionSpec as P

QH = 32
KH = 4
HD = 128
STEPS = 2
ROWS = 128
RANK = 16
LOADS = 12
SLOTS = 13
HELD = 12
N = 16
SIDE = 4
RING = 8
GROUPED = 2
PAIR = 2
ALL_ROWS = STEPS * ROWS
LOCAL = ROWS // N
MINE = STEPS * LOCAL
ENTRIES = 1 + STEPS * LOADS
SHARED = 8
Q_AT = HELD * 48
KV_AT = Q_AT + HELD // 2 * RANK
PACKED = KV_AT + 2 * RANK
IN_RANK = 3 * RANK
PER_DOT = 5
QF = 256
KF = 32
IN_PART = 512
OUT_PART = 512
FEATURES = QH * HD
WIDE = RING * QF
QKV = QF + 2 * KF
TP = ("hi", "lo", "x")
AROUND = ("hi", "x")
LENGTH = 512
KW = KH * HD
BF16 = jnp.bfloat16
F32 = jnp.float32
low_rank_scale = 0.5


def vmem():
    return pl.BlockSpec(memory_space=pltpu.VMEM)


def hbm():
    return pl.BlockSpec(memory_space=pl.ANY)


def smem():
    return pl.BlockSpec(memory_space=pltpu.SMEM)


def params(mib=40):
    return pltpu.CompilerParams(vmem_limit_bytes=mib * 1024 * 1024)


def cost(flops, nbytes):
    return pl.CostEstimate(flops=flops, bytes_accessed=nbytes, transcendentals=0)


def iota(shape, axis):
    return lax.broadcasted_iota(jnp.int32, shape, axis)


def pack_kernel(maps_in, maps_q, maps_k, maps_v, out, all_q, all_k, all_v, in_sem, sem):
    copies = [
        pltpu.make_async_copy(maps_q, all_q, sem.at[0]),
        pltpu.make_async_copy(maps_k, all_k, sem.at[1]),
        pltpu.make_async_copy(maps_v, all_v, sem.at[2]),
    ]
    for k in range(HELD):
        rows = pl.ds(k * IN_RANK, IN_RANK)
        copies.append(pltpu.make_async_copy(maps_in.at[k], out.at[rows], in_sem.at[k]))
    for copy in copies:
        copy.start()
    for copy in copies[:3]:
        copy.wait()
    for k in range(HELD):
        low, block = Q_AT + k // 2 * RANK, k % 2 * QF
        out[low : low + RANK, block : block + QF] = all_q[k]
    empty = jnp.zeros((RANK, 2 * KF), BF16)
    for first in range(0, 2 * SHARED, SHARED):
        pieces = []
        for k in range(first, first + SHARED):
            pieces += [all_k[k], all_v[k]] if k < HELD else [empty]
        low = KV_AT + first // SHARED * RANK
        out[low : low + RANK] = jnp.concatenate(pieces, axis=1)
    for copy in copies[3:]:
        copy.wait()


def aligned(value, unit):
    return pl.multiple_of(value * unit, unit)


def shrink_kernel(index, pool, slot, tokens, entry, out, maps, arrived):
    copies = []
    for i in range(ENTRIES):
        if i == 0:
            origin = slot.at[index[0]]
        else:
            rows = pl.ds(aligned(lax.rem(index[i], HELD), IN_RANK), IN_RANK)
            origin = pool.at[index[i] // HELD, rows]
        copy = pltpu.make_async_copy(origin, maps.at[pl.ds(i * IN_RANK, IN_RANK)], arrived.at[i])
        copy.start()
        copies.append(copy)
    used = entry[...]
    total = jnp.zeros((IN_RANK, ALL_ROWS), F32)
    for first in range(0, ENTRIES, PER_DOT):
        for i in range(first, first + PER_DOT):
            copies[i].wait()
        block = maps[pl.ds(first * IN_RANK, PER_DOT * IN_RANK), :]
        product = lax.dot_general(
            block, tokens[...], (((1,), (1,)), ((), ())), preferred_element_type=F32
        )
        for k in range(PER_DOT):
            piece = product[k * IN_RANK : (k + 1) * IN_RANK]
            total = total + jnp.where(used == first + k, piece, 0.0)
    total = total.astype(BF16)
    for n in range(N):
        out[n] = total


def expand(shrunk, entry):
    blocks = [jnp.where(entry == i, shrunk, 0.0) for i in range(ENTRIES)]
    return jnp.concatenate(blocks, axis=0).astype(BF16)


def contract(left, right):
    return lax.dot_general(left, right, (((0,), (0,)), ((), ())), preferred_element_type=F32)


def pick_up_kernel(index, pool, slot_q, slot_k, slot_v, up_q, up_kv, q_sem, kv_sem):
    copies = []
    for i in range(ENTRIES):
        rows = pl.ds(i * RANK, RANK)
        if i == 0:
            copies.append(pltpu.make_async_copy(slot_q.at[index[0]], up_q.at[rows], q_sem.at[0]))
            continue
        source, k = index[i] // HELD, lax.rem(index[i], HELD)
        of_q = pl.ds(Q_AT + aligned(k // 2, RANK), RANK)
        block = pl.ds(aligned(lax.rem(k, 2), QF), QF)
        of_kv = pl.ds(KV_AT + aligned(k // SHARED, RANK), RANK)
        copies.append(
            pltpu.make_async_copy(pool.at[source, of_q, block], up_q.at[rows], q_sem.at[i])
        )
        copies.append(pltpu.make_async_copy(pool.at[source, of_kv], up_kv.at[rows], kv_sem.at[i]))
    for copy in copies:
        copy.start()
    empty = jnp.zeros((RANK, IN_PART - 2 * KF), BF16)
    up_kv[:RANK] = jnp.concatenate([slot_k[index[0]], slot_v[index[0]], empty], axis=1)
    for copy in copies:
        copy.wait()


def project_kernel(parts, entry, block, base_q, base_kv, up_q, up_kv, out):
    shrunk = jnp.sum(parts[...].astype(F32), axis=0).astype(BF16).astype(F32)
    used = entry[...]
    wide_q = expand(shrunk[:RANK], used)
    wide_k = expand(shrunk[RANK : 2 * RANK], used)
    wide_v = expand(shrunk[2 * RANK :], used)
    query = base_q[...] + low_rank_scale * contract(wide_q, up_q[...])
    delta_k = contract(wide_k, up_kv[...])
    delta_v = contract(wide_v, up_kv[...])
    delta = jnp.where(iota(delta_k.shape, 1) % (2 * KF) < KF, delta_k, delta_v)
    delta = jnp.where(iota(delta.shape, 1) // (2 * KF) == block[...], delta, 0.0)
    folded = jnp.zeros((ALL_ROWS, 2 * KF), F32)
    for j in range(SHARED):
        folded = folded + delta[:, j * 2 * KF : (j + 1) * 2 * KF]
    fresh = base_kv[...] + low_rank_scale * folded
    for t in range(N):
        lows = [s * ROWS + t * LOCAL for s in range(STEPS)]
        out[t, :, :QF] = jnp.concatenate([query[n : n + LOCAL] for n in lows], 0).astype(BF16)
        out[t, :, QF:] = jnp.concatenate([fresh[n : n + LOCAL] for n in lows], 0).astype(BF16)


def split_kernel(side, weight, out, arrived):
    half = QF // 2
    rows = pl.ds(aligned(side[0], half), half)
    copies = []
    for t in range(N):
        high, low, x = t // (PAIR * SIDE), t // SIDE % PAIR, t % SIDE
        source = weight.at[rows, pl.ds(t * OUT_PART, OUT_PART)]
        copies.append(
            pltpu.make_async_copy(source, out.at[high * SIDE + x, low], arrived.at[t])
        )
    for copy in copies:
        copy.start()
    for copy in copies:
        copy.wait()


def transposing():
    shape = (N * MINE, N * MINE)
    row, column = iota(shape, 0), iota(shape, 1)
    return ((row // N == column % N) & (row % N == column // N)).astype(BF16)


def attend_kernel(
    lengths, received, keys, values, out, key_rows, value_rows, by_row, ready, key_sem, value_sem,
    sent,
):
    loads = []
    for i in range(LOCAL):
        pair = (
            pltpu.make_async_copy(keys.at[i], key_rows.at[i], key_sem.at[i]),
            pltpu.make_async_copy(values.at[i], value_rows.at[i], value_sem.at[i]),
        )
        for copy in pair:
            copy.start()
        loads.append(pair)
    swap = transposing()
    mine = jnp.dot(swap, received[...].reshape(N * MINE, -1), preferred_element_type=F32)
    mine = mine.astype(BF16)
    shape = (2 * KF, KW)
    feature, column = iota(shape, 0), iota(shape, 1) % KF
    block = iota((N * MINE, KW), 1) // KF == iota((N * MINE, KW), 0) % N
    fold = (iota((MINE, N * MINE), 1) // N == iota((MINE, N * MINE), 0)).astype(BF16)

    def fresh(first):
        repeat = (feature - first == column).astype(BF16)
        wide = jnp.dot(mine[:, QF:], repeat, preferred_element_type=F32)
        wide = jnp.where(block, wide, 0.0).astype(BF16)
        return jnp.dot(fold, wide, preferred_element_type=F32).astype(BF16)

    keys_new, values_new = fresh(0), fresh(KF)

    head_rows = STEPS * QH
    own = iota((head_rows, KW), 0) % N // (N // KH) == iota((head_rows, KW), 1) // HD
    place = iota((head_rows, LENGTH), 1)
    shape = (head_rows, MINE)
    new_step, new_row = iota(shape, 1) // LOCAL, iota(shape, 1) % LOCAL
    in_time = new_step <= iota(shape, 0) // QH
    scale = 1.0 / math.sqrt(HD)
    dims = (((1,), (1,)), ((), ()))
    for i in range(LOCAL):
        if i % GROUPED == 0:
            for pair in loads[i : i + GROUPED]:
                for copy in pair:
                    copy.wait()
        asked = []
        for s in range(STEPS):
            low = (s * LOCAL + i) * N
            asked += [mine[low : low + N, :HD], mine[low : low + N, HD:QF]]
        asked = jnp.concatenate(asked, axis=0)
        spread = jnp.where(own, jnp.concatenate([asked] * KH, axis=1), jnp.zeros((), BF16))
        new = lax.dot_general(spread, keys_new, dims, preferred_element_type=F32) * scale
        new = jnp.where(in_time & (new_row == i), new, -jnp.inf)
        old = lax.dot_general(spread, key_rows[i], dims, preferred_element_type=F32) * scale
        old = jnp.where(place < lengths[i], old, -jnp.inf)
        highest = jnp.maximum(
            jnp.max(old, axis=1, keepdims=True), jnp.max(new, axis=1, keepdims=True)
        )
        old, new = jnp.exp(old - highest), jnp.exp(new - highest)
        totals = jnp.sum(old, axis=1, keepdims=True) + jnp.sum(new, axis=1, keepdims=True)
        mixed = jnp.dot(old.astype(BF16), value_rows[i], preferred_element_type=F32)
        mixed = mixed + jnp.dot(new.astype(BF16), values_new, preferred_element_type=F32)
        mixed = jnp.where(own, mixed, 0.0)
        attended = mixed[:, :HD]
        for k in range(1, KH):
            attended = attended + mixed[:, k * HD : (k + 1) * HD]
        attended = (attended / totals).astype(BF16)
        for s in range(STEPS):
            low = (s * LOCAL + i) * N
            for half in range(2):
                piece = attended[(2 * s + half) * N : (2 * s + half + 1) * N]
                by_row[low : low + N, half * HD : (half + 1) * HD] = piece

    attended = jnp.dot(swap, by_row[...], preferred_element_type=F32).astype(BF16)
    for t in range(N):
        high, low, x = t // (PAIR * SIDE), t // SIDE % PAIR, t % SIDE
        ready[low, high * SIDE + x] = attended[t * MINE : (t + 1) * MINE]
    copies = [
        pltpu.make_async_copy(ready.at[n // SIDE % PAIR], out.at[n], sent.at[n]) for n in range(N)
    ]
    for copy in copies:
        copy.start()
    for copy in copies:
        copy.wait()


def pick_kernel(index, slot_in, slot_up, pool, maps, up, map_sem, up_sem):
    copies = []
    for i in range(ENTRIES):
        if i == 0:
            first, second = slot_in.at[index[0]], slot_up.at[index[0]]
        else:
            first = pool.at[index[i], :, pl.ds(0, QF)]
            second = pool.at[index[i], :, pl.ds(QF, OUT_PART)]
        rows = pl.ds(i * RANK, RANK)
        copies.append(pltpu.make_async_copy(first, maps.at[rows], map_sem.at[i]))
        copies.append(pltpu.make_async_copy(second, up.at[rows], up_sem.at[i]))
    for copy in copies:
        copy.start()
    for copy in copies:
        copy.wait()


def shrink_out_kernel(place, attended, entry, maps, out):
    heads = attended[:, pl.ds(place[0], 1)].reshape(ALL_ROWS, QF)
    product = lax.dot_general(
        maps[...], heads, (((1,), (1,)), ((), ())), preferred_element_type=F32
    )
    used = entry[...]
    shrunk = jnp.zeros((RANK, ALL_ROWS), F32)
    for i in range(ENTRIES):
        shrunk = shrunk + jnp.where(used == i, product[i * RANK : (i + 1) * RANK], 0.0)
    shrunk = shrunk.astype(BF16)
    for n in range(N):
        out[n] = shrunk


def base_out_kernel(side, member, attended, mine, others, passed, kept, columns, sems):
    half = QF // 2
    near = aligned(side[0], half)
    loads = []
    for which in range(PAIR):
        whose = (1 - member[0], member[0])[which]
        for j in range(RING):
            for n, (source, low) in enumerate(((mine, near), (others, half - near))):
                rows = pl.ds(pl.multiple_of(j * QF + low, half), half)
                copy = pltpu.make_async_copy(
                    source.at[j, whose], columns.at[which, rows], sems.at[which, j, n]
                )
                copy.start()
                loads.append(copy)
    for which, out in enumerate((passed, kept)):
        total = jnp.zeros((ALL_ROWS, OUT_PART), F32)
        for j in range(0, RING, PAIR):
            first = 2 * (which * RING + j)
            for copy in loads[first : first + 2 * PAIR]:
                copy.wait()
            heads = [attended[:, n].reshape(ALL_ROWS, QF) for n in range(j, j + PAIR)]
            part = jnp.concatenate(heads, axis=1)
            rows = columns[which, j * QF : (j + PAIR) * QF]
            total = total + jnp.dot(part, rows, preferred_element_type=F32)
        out[...] = total.astype(out.dtype)


def final_kernel(parts, entry, kept, arrived, up, out):
    shrunk = jnp.sum(parts[...].astype(F32), axis=0).astype(BF16).astype(F32)
    wide = expand(shrunk, entry[...])
    total = kept[...] + arrived[...].astype(F32)
    total = total + low_rank_scale * contract(wide, up[...])
    for s in range(STEPS):
        lows = [t * MINE + s * LOCAL for t in range(N)]
        out[s] = jnp.concatenate([total[n : n + LOCAL] for n in lows], axis=0).astype(BF16)


def shard(
    hidden, w_query, w_key, w_value, w_out, key_cache, value_cache, lengths, row_slot, evict_slot,
    evict_adapter, owner, pool_a_in, pool_b_q, pool_b_k, pool_b_v, pool_a_o, pool_b_o,
    slot_a_in, slot_b_q, slot_b_k, slot_b_v, slot_a_o, slot_b_o,
):
    me = lax.axis_index("group")
    part = lax.axis_index(TP)
    place = lax.axis_index(AROUND)[None]
    member = lax.axis_index("lo")[None]
    side = (me % 2)[None]

    with jax.named_scope("gather_in_maps"):
        packed = pl.pallas_call(
            pack_kernel,
            out_shape=jax.ShapeDtypeStruct((PACKED, IN_PART), BF16),
            in_specs=[hbm()] * 4,
            out_specs=vmem(),
            scratch_shapes=[
                pltpu.VMEM((HELD, RANK, QF), BF16),
                pltpu.VMEM((HELD, RANK, KF), BF16),
                pltpu.VMEM((HELD, RANK, KF), BF16),
                pltpu.SemaphoreType.DMA((HELD,)),
                pltpu.SemaphoreType.DMA((3,)),
            ],
            compiler_params=params(58),
            cost_estimate=cost(0, 2 << 20),
            name="pack",
        )(pool_a_in, pool_b_q, pool_b_k, pool_b_v)
        pool = lax.all_gather(packed, "group")

    with jax.named_scope("positions"):
        position = jnp.sum(
            jnp.where(evict_adapter[..., None] == jnp.arange(N * HELD), owner, 0), axis=-1
        )
        targets = lax.dynamic_slice_in_dim(evict_slot, me * LOADS, LOADS, 1)
        survivor = SLOTS * (SLOTS - 1) // 2 - jnp.sum(targets[0])
        placed = targets[:, :, None] == jnp.arange(SLOTS)
        order = 1 + jnp.arange(STEPS * LOADS).reshape(STEPS, LOADS, 1)
        slot_entry = jnp.sum(jnp.where(placed, order, 0), axis=1)
        second = jnp.where(slot_entry[1] > 0, slot_entry[1], slot_entry[0])
        slot_entry = jnp.stack([slot_entry[0], second])
        entry = jnp.sum(
            jnp.where(
                row_slot[:, :, None] == jnp.arange(SLOTS), slot_entry[:, None, :], 0
            ),
            axis=-1,
        )
        by_step = entry.reshape(1, ALL_ROWS)
        blocks = position % HELD % SHARED
        blocks = lax.dynamic_slice_in_dim(blocks, me * LOADS, LOADS, 1).reshape(1, 1, -1)
        load = jnp.arange(STEPS * LOADS) + 1
        blocks = jnp.sum(jnp.where(entry[:, :, None] == load, blocks, 0), axis=-1)
        blocks = blocks.reshape(ALL_ROWS, 1)
        by_owner = entry.reshape(STEPS, N, LOCAL).transpose(1, 0, 2)
        by_owner = by_owner.reshape(1, ALL_ROWS)
        my_wanted = lax.dynamic_slice_in_dim(position, me * LOADS, LOADS, 1)
        my_wanted = my_wanted.reshape(STEPS * LOADS)
        index = jnp.concatenate([survivor[None], my_wanted]).astype(jnp.int32)

    with jax.named_scope("columns_of_w_out"):
        w_out, packed = lax.optimization_barrier((w_out, packed))
        half = pl.pallas_call(
            split_kernel,
            out_shape=jax.ShapeDtypeStruct((RING, PAIR, QF // 2, OUT_PART), BF16),
            in_specs=[smem(), hbm()],
            out_specs=vmem(),
            scratch_shapes=[pltpu.SemaphoreType.DMA((N,))],
            compiler_params=params(56),
            cost_estimate=cost(0, 8 << 20),
            name="split",
        )(side, w_out)
        mine = lax.all_to_all(half, AROUND, split_axis=0, concat_axis=0, tiled=True)
        others = lax.ppermute(mine, "group", [(i, i ^ 1) for i in range(N)])

    with jax.named_scope("base_projections"):
        tokens = hidden.reshape(ALL_ROWS, -1)
        base_q = jnp.dot(tokens, w_query, preferred_element_type=F32)
        base_kv = jnp.concatenate(
            [
                jnp.dot(tokens, w_key, preferred_element_type=F32),
                jnp.dot(tokens, w_value, preferred_element_type=F32),
            ],
            axis=1,
        )
        tokens_part = lax.dynamic_slice_in_dim(tokens, part * IN_PART, IN_PART, 1)

    with jax.named_scope("gather_out_maps"):
        out_pool = jnp.concatenate([pool_a_o, pool_b_o], axis=2)
        out_pool, index, base_q, base_kv, tokens_part, mine = lax.optimization_barrier(
            (out_pool, index, base_q, base_kv, tokens_part, mine)
        )
        out_pool = lax.all_gather(out_pool, "group").reshape(N * HELD, RANK, QF + OUT_PART)

    with jax.named_scope("shrink"):
        partial_in = pl.pallas_call(
            shrink_kernel,
            out_shape=jax.ShapeDtypeStruct((N, IN_RANK, ALL_ROWS), BF16),
            in_specs=[smem(), hbm(), hbm(), vmem(), vmem()],
            out_specs=vmem(),
            scratch_shapes=[
                pltpu.VMEM((ENTRIES * IN_RANK, IN_PART), BF16),
                pltpu.SemaphoreType.DMA((ENTRIES,)),
            ],
            compiler_params=params(56),
            cost_estimate=cost(2 * ENTRIES * IN_RANK * IN_PART * ALL_ROWS, 2 << 20),
            name="shrink",
        )(index, pool, slot_a_in, tokens_part, by_step)

        partial_in, picks = lax.optimization_barrier((partial_in, index))
        partials = lax.all_to_all(partial_in, TP, split_axis=0, concat_axis=0, tiled=True)

    with jax.named_scope("project"):
        up_q, up_kv = pl.pallas_call(
            pick_up_kernel,
            out_shape=[
                jax.ShapeDtypeStruct((ENTRIES * RANK, QF), BF16),
                jax.ShapeDtypeStruct((ENTRIES * RANK, IN_PART), BF16),
            ],
            in_specs=[smem(), hbm(), hbm(), vmem(), vmem()],
            out_specs=[vmem()] * 2,
            scratch_shapes=[pltpu.SemaphoreType.DMA((ENTRIES,))] * 2,
            compiler_params=params(52),
            cost_estimate=cost(0, 2 << 20),
            name="pick_up",
        )(picks, pool, slot_b_q, slot_b_k, slot_b_v)
        projected = pl.pallas_call(
            project_kernel,
            out_shape=jax.ShapeDtypeStruct((N, MINE, QF + 2 * KF), BF16),
            in_specs=[vmem()] * 7,
            out_specs=vmem(),
            compiler_params=params(16),
            cost_estimate=cost(2 * 400 * 512 * ALL_ROWS, 1 << 20),
            name="project",
        )(partials, by_step, blocks, base_q, base_kv, up_q, up_kv)

    with jax.named_scope("attend"):
        received = lax.all_to_all(projected, TP, split_axis=0, concat_axis=0, tiled=True)
        payload = pl.pallas_call(
            attend_kernel,
            out_shape=jax.ShapeDtypeStruct((N, RING, MINE, QF), BF16),
            in_specs=[smem(), vmem(), hbm(), hbm()],
            out_specs=hbm(),
            scratch_shapes=[
                pltpu.VMEM((LOCAL, LENGTH, KW), BF16),
                pltpu.VMEM((LOCAL, LENGTH, KW), BF16),
                pltpu.VMEM((N * MINE, QF), BF16),
                pltpu.VMEM((PAIR, RING, MINE, QF), BF16),
                pltpu.SemaphoreType.DMA((LOCAL,)),
                pltpu.SemaphoreType.DMA((LOCAL,)),
                pltpu.SemaphoreType.DMA((N,)),
            ],
            compiler_params=params(56),
            cost_estimate=cost(4 * LOCAL * 64 * KW * LENGTH, 12 << 20),
            name="attend",
        )(lengths, received, key_cache, value_cache)
        gathered = lax.all_to_all(payload, TP, split_axis=0, concat_axis=0, tiled=True)

        payload, picks = lax.optimization_barrier((payload, index))
        maps, up_o = pl.pallas_call(
            pick_kernel,
            out_shape=[
                jax.ShapeDtypeStruct((ENTRIES * RANK, QF), BF16),
                jax.ShapeDtypeStruct((ENTRIES * RANK, OUT_PART), BF16),
            ],
            in_specs=[smem()] + [hbm()] * 3,
            out_specs=[vmem()] * 2,
            scratch_shapes=[pltpu.SemaphoreType.DMA((ENTRIES,))] * 2,
            compiler_params=params(24),
            cost_estimate=cost(0, 3 << 20),
            name="pick",
        )(picks, slot_a_o, slot_b_o, out_pool)

    with jax.named_scope("output"):
        partial_out = pl.pallas_call(
            shrink_out_kernel,
            out_shape=jax.ShapeDtypeStruct((N, RANK, ALL_ROWS), BF16),
            in_specs=[smem()] + [vmem()] * 3,
            out_specs=vmem(),
            compiler_params=params(16),
            cost_estimate=cost(2 * 400 * QF * ALL_ROWS, 1 << 20),
            name="shrink_out",
        )(place, gathered, by_owner, maps)
        partial_out, member = lax.optimization_barrier((partial_out, member))
        partials_out = lax.all_to_all(partial_out, TP, split_axis=0, concat_axis=0, tiled=True)

        passed, kept_out = pl.pallas_call(
            base_out_kernel,
            out_shape=[
                jax.ShapeDtypeStruct((ALL_ROWS, OUT_PART), BF16),
                jax.ShapeDtypeStruct((ALL_ROWS, OUT_PART), F32),
            ],
            in_specs=[smem()] * 2 + [vmem()] + [hbm()] * 2,
            out_specs=[vmem()] * 2,
            scratch_shapes=[
                pltpu.VMEM((PAIR, RING * QF, OUT_PART), BF16),
                pltpu.SemaphoreType.DMA((PAIR, RING, 2)),
            ],
            compiler_params=params(24),
            cost_estimate=cost(4 * ALL_ROWS * WIDE * OUT_PART, 5 << 20),
            name="base_out",
        )(side, member, gathered, mine, others)
        passed = lax.ppermute(passed, "lo", [(0, 1), (1, 0)])
        return pl.pallas_call(
            final_kernel,
            out_shape=jax.ShapeDtypeStruct((STEPS, ROWS, OUT_PART), BF16),
            in_specs=[vmem()] * 5,
            out_specs=vmem(),
            compiler_params=params(16),
            cost_estimate=cost(2 * 400 * OUT_PART * ALL_ROWS, 1 << 20),
            name="final",
        )(partials_out, by_owner, kept_out, passed, up_o)


def solution(mesh):
    grid = jax.sharding.Mesh(mesh.devices.reshape(N, SIDE // PAIR, PAIR, SIDE), ("group",) + TP)
    pooled = P("group", None, TP)
    cached = P(("group",) + TP, None, None)
    placed = (
        P(None, "group", None), P(None, TP), P(None, TP), P(None, TP), P(TP, None),
        cached, cached, P(("group",) + TP), P(None, "group"), P(), P(), P(),
    ) + (pooled,) * 12
    return jax.shard_map(
        shard, mesh=grid, in_specs=placed, out_specs=P(None, "group", TP), check_vma=False
    )
```

```python
import math

import jax
import jax.numpy as jnp
from jax import lax
from jax.experimental import pallas as pl
from jax.experimental.pallas import tpu as pltpu
from jax.sharding import PartitionSpec as P

QH = 32
KH = 4
HD = 128
STEPS = 2
ROWS = 128
RANK = 16
LOADS = 12
SLOTS = 13
HELD = 12
N = 16
SIDE = 4
GROUPED = 2
ALL_ROWS = STEPS * ROWS
LOCAL = ROWS // N
MINE = STEPS * LOCAL
ENTRIES = 1 + STEPS * LOADS
SHARED = 8
Q_AT = HELD * 48
KV_AT = Q_AT + HELD // 2 * RANK
PACKED = KV_AT + 2 * RANK
IN_RANK = 3 * RANK
QF = 256
KF = 32
IN_PART = 512
OUT_PART = 512
FEATURES = QH * HD
WIDE = SIDE * QF
QKV = QF + 2 * KF
TP = ("y", "x")
LENGTH = 512
KW = KH * HD
BF16 = jnp.bfloat16
F32 = jnp.float32
low_rank_scale = 0.5


def vmem():
    return pl.BlockSpec(memory_space=pltpu.VMEM)


def hbm():
    return pl.BlockSpec(memory_space=pl.ANY)


def smem():
    return pl.BlockSpec(memory_space=pltpu.SMEM)


def params(mib=40):
    return pltpu.CompilerParams(vmem_limit_bytes=mib * 1024 * 1024)


def cost(flops, nbytes):
    return pl.CostEstimate(flops=flops, bytes_accessed=nbytes, transcendentals=0)


def iota(shape, axis):
    return lax.broadcasted_iota(jnp.int32, shape, axis)


def pack_kernel(maps_in, maps_q, maps_k, maps_v, out, all_q, all_k, all_v, in_sem, sem):
    copies = [
        pltpu.make_async_copy(maps_q, all_q, sem.at[0]),
        pltpu.make_async_copy(maps_k, all_k, sem.at[1]),
        pltpu.make_async_copy(maps_v, all_v, sem.at[2]),
    ]
    for k in range(HELD):
        rows = pl.ds(k * IN_RANK, IN_RANK)
        copies.append(pltpu.make_async_copy(maps_in.at[k], out.at[rows], in_sem.at[k]))
    for copy in copies:
        copy.start()
    for copy in copies[:3]:
        copy.wait()
    for k in range(HELD):
        low, block = Q_AT + k // 2 * RANK, k % 2 * QF
        out[low : low + RANK, block : block + QF] = all_q[k]
    empty = jnp.zeros((RANK, 2 * KF), BF16)
    for first in range(0, 2 * SHARED, SHARED):
        pieces = []
        for k in range(first, first + SHARED):
            pieces += [all_k[k], all_v[k]] if k < HELD else [empty]
        low = KV_AT + first // SHARED * RANK
        out[low : low + RANK] = jnp.concatenate(pieces, axis=1)
    for copy in copies[3:]:
        copy.wait()


def aligned(value, unit):
    return pl.multiple_of(value * unit, unit)


def shrink_kernel(index, pool, slot, tokens, entry, out, maps, arrived):
    copies = []
    for i in range(ENTRIES):
        if i == 0:
            origin = slot.at[index[0]]
        else:
            rows = pl.ds(aligned(lax.rem(index[i], HELD), IN_RANK), IN_RANK)
            origin = pool.at[index[i] // HELD, rows]
        copy = pltpu.make_async_copy(origin, maps.at[pl.ds(i * IN_RANK, IN_RANK)], arrived.at[i])
        copy.start()
        copies.append(copy)
    for copy in copies:
        copy.wait()
    used = entry[...]
    product = jnp.dot(maps[...], tokens[...], preferred_element_type=F32)
    total = jnp.zeros((IN_RANK, ALL_ROWS), F32)
    for i in range(ENTRIES):
        total = total + jnp.where(used == i, product[i * IN_RANK : (i + 1) * IN_RANK], 0.0)
    total = total.astype(BF16)
    for n in range(N):
        out[n] = total


def expand(shrunk, entry):
    blocks = [jnp.where(entry == i, shrunk, 0.0) for i in range(ENTRIES)]
    return jnp.concatenate(blocks, axis=0).astype(BF16)


def contract(left, right):
    return lax.dot_general(left, right, (((0,), (0,)), ((), ())), preferred_element_type=F32)


def pick_up_kernel(index, pool, slot_q, slot_k, slot_v, up_q, up_kv, q_sem, kv_sem):
    copies = []
    for i in range(ENTRIES):
        rows = pl.ds(i * RANK, RANK)
        if i == 0:
            copies.append(pltpu.make_async_copy(slot_q.at[index[0]], up_q.at[rows], q_sem.at[0]))
            continue
        source, k = index[i] // HELD, lax.rem(index[i], HELD)
        of_q = pl.ds(Q_AT + aligned(k // 2, RANK), RANK)
        block = pl.ds(aligned(lax.rem(k, 2), QF), QF)
        of_kv = pl.ds(KV_AT + aligned(k // SHARED, RANK), RANK)
        copies.append(
            pltpu.make_async_copy(pool.at[source, of_q, block], up_q.at[rows], q_sem.at[i])
        )
        copies.append(pltpu.make_async_copy(pool.at[source, of_kv], up_kv.at[rows], kv_sem.at[i]))
    for copy in copies:
        copy.start()
    empty = jnp.zeros((RANK, IN_PART - 2 * KF), BF16)
    up_kv[:RANK] = jnp.concatenate([slot_k[index[0]], slot_v[index[0]], empty], axis=1)
    for copy in copies:
        copy.wait()


def project_kernel(parts, entry, block, base_q, base_kv, up_q, up_kv, out):
    shrunk = jnp.sum(parts[...].astype(F32), axis=0).astype(BF16).astype(F32)
    used = entry[...]
    wide_q = expand(shrunk[:RANK], used)
    wide_k = expand(shrunk[RANK : 2 * RANK], used)
    wide_v = expand(shrunk[2 * RANK :], used)
    query = base_q[...] + low_rank_scale * contract(wide_q, up_q[...])
    delta_k = contract(wide_k, up_kv[...])
    delta_v = contract(wide_v, up_kv[...])
    delta = jnp.where(iota(delta_k.shape, 1) % (2 * KF) < KF, delta_k, delta_v)
    delta = jnp.where(iota(delta.shape, 1) // (2 * KF) == block[...], delta, 0.0)
    folded = jnp.zeros((ALL_ROWS, 2 * KF), F32)
    for j in range(SHARED):
        folded = folded + delta[:, j * 2 * KF : (j + 1) * 2 * KF]
    fresh = base_kv[...] + low_rank_scale * folded
    for t in range(N):
        lows = [s * ROWS + t * LOCAL for s in range(STEPS)]
        out[t, :, :QF] = jnp.concatenate([query[n : n + LOCAL] for n in lows], 0).astype(BF16)
        out[t, :, QF:] = jnp.concatenate([fresh[n : n + LOCAL] for n in lows], 0).astype(BF16)


def split_kernel(weight, out, arrived):
    copies = []
    for t in range(N):
        source = weight.at[:, pl.ds(t * OUT_PART, OUT_PART)]
        copies.append(
            pltpu.make_async_copy(source, out.at[t % SIDE, t // SIDE], arrived.at[t])
        )
    for copy in copies:
        copy.start()
    for copy in copies:
        copy.wait()


def transposing():
    shape = (N * MINE, N * MINE)
    row, column = iota(shape, 0), iota(shape, 1)
    return ((row // N == column % N) & (row % N == column // N)).astype(BF16)


def attend_kernel(
    lengths, received, keys, values, out, key_rows, value_rows, by_row, ready, key_sem, value_sem,
    sent,
):
    loads = []
    for i in range(LOCAL):
        pair = (
            pltpu.make_async_copy(keys.at[i], key_rows.at[i], key_sem.at[i]),
            pltpu.make_async_copy(values.at[i], value_rows.at[i], value_sem.at[i]),
        )
        for copy in pair:
            copy.start()
        loads.append(pair)
    swap = transposing()
    mine = jnp.dot(swap, received[...].reshape(N * MINE, -1), preferred_element_type=F32)
    mine = mine.astype(BF16)
    shape = (2 * KF, KW)
    feature, column = iota(shape, 0), iota(shape, 1) % KF
    block = iota((N * MINE, KW), 1) // KF == iota((N * MINE, KW), 0) % N
    fold = (iota((MINE, N * MINE), 1) // N == iota((MINE, N * MINE), 0)).astype(BF16)

    def fresh(first):
        repeat = (feature - first == column).astype(BF16)
        wide = jnp.dot(mine[:, QF:], repeat, preferred_element_type=F32)
        wide = jnp.where(block, wide, 0.0).astype(BF16)
        return jnp.dot(fold, wide, preferred_element_type=F32).astype(BF16)

    keys_new, values_new = fresh(0), fresh(KF)

    head_rows = STEPS * QH
    own = iota((head_rows, KW), 0) % N // (N // KH) == iota((head_rows, KW), 1) // HD
    place = iota((head_rows, LENGTH), 1)
    shape = (head_rows, MINE)
    new_step, new_row = iota(shape, 1) // LOCAL, iota(shape, 1) % LOCAL
    in_time = new_step <= iota(shape, 0) // QH
    scale = 1.0 / math.sqrt(HD)
    dims = (((1,), (1,)), ((), ()))
    for i in range(LOCAL):
        if i % GROUPED == 0:
            for pair in loads[i : i + GROUPED]:
                for copy in pair:
                    copy.wait()
        asked = []
        for s in range(STEPS):
            low = (s * LOCAL + i) * N
            asked += [mine[low : low + N, :HD], mine[low : low + N, HD:QF]]
        asked = jnp.concatenate(asked, axis=0)
        spread = jnp.where(own, jnp.concatenate([asked] * KH, axis=1), jnp.zeros((), BF16))
        new = lax.dot_general(spread, keys_new, dims, preferred_element_type=F32) * scale
        new = jnp.where(in_time & (new_row == i), new, -jnp.inf)
        old = lax.dot_general(spread, key_rows[i], dims, preferred_element_type=F32) * scale
        old = jnp.where(place < lengths[i], old, -jnp.inf)
        highest = jnp.maximum(
            jnp.max(old, axis=1, keepdims=True), jnp.max(new, axis=1, keepdims=True)
        )
        old, new = jnp.exp(old - highest), jnp.exp(new - highest)
        totals = jnp.sum(old, axis=1, keepdims=True) + jnp.sum(new, axis=1, keepdims=True)
        mixed = jnp.dot(old.astype(BF16), value_rows[i], preferred_element_type=F32)
        mixed = mixed + jnp.dot(new.astype(BF16), values_new, preferred_element_type=F32)
        mixed = jnp.where(own, mixed, 0.0)
        attended = mixed[:, :HD]
        for k in range(1, KH):
            attended = attended + mixed[:, k * HD : (k + 1) * HD]
        attended = (attended / totals).astype(BF16)
        for s in range(STEPS):
            low = (s * LOCAL + i) * N
            for half in range(2):
                piece = attended[(2 * s + half) * N : (2 * s + half + 1) * N]
                by_row[low : low + N, half * HD : (half + 1) * HD] = piece

    attended = jnp.dot(swap, by_row[...], preferred_element_type=F32).astype(BF16)
    ready[...] = attended.reshape(SIDE, SIDE, MINE, QF)
    copies = [
        pltpu.make_async_copy(ready.at[n // SIDE], out.at[n], sent.at[n]) for n in range(N)
    ]
    for copy in copies:
        copy.start()
    for copy in copies:
        copy.wait()


def pick_kernel(index, slot_in, slot_up, pool, maps, up, map_sem, up_sem):
    copies = []
    for i in range(ENTRIES):
        if i == 0:
            first, second = slot_in.at[index[0]], slot_up.at[index[0]]
        else:
            first = pool.at[index[i], :, pl.ds(0, QF)]
            second = pool.at[index[i], :, pl.ds(QF, OUT_PART)]
        rows = pl.ds(i * RANK, RANK)
        copies.append(pltpu.make_async_copy(first, maps.at[rows], map_sem.at[i]))
        copies.append(pltpu.make_async_copy(second, up.at[rows], up_sem.at[i]))
    for copy in copies:
        copy.start()
    for copy in copies:
        copy.wait()


def base_out_kernel(
    place, member, attended, entry, maps, source, partial, first, second, third, kept, columns, sems
):
    loads = []
    for n, k in enumerate((1, 2, 3, 0)):
        whose = lax.rem(member[0] + k, SIDE)
        for j in range(SIDE):
            rows = pl.ds(j * QF, QF)
            copy = pltpu.make_async_copy(
                source.at[j, whose], columns.at[n, rows], sems.at[n, j]
            )
            copy.start()
            loads.append(copy)
    heads = attended[:, pl.ds(place[0], 1)].reshape(ALL_ROWS, QF)
    product = lax.dot_general(
        maps[...], heads, (((1,), (1,)), ((), ())), preferred_element_type=F32
    )
    used = entry[...]
    shrunk = jnp.zeros((RANK, ALL_ROWS), F32)
    for i in range(ENTRIES):
        shrunk = shrunk + jnp.where(used == i, product[i * RANK : (i + 1) * RANK], 0.0)
    shrunk = shrunk.astype(BF16)
    for n in range(N):
        partial[n] = shrunk
    for n, out in enumerate((first, second, third, kept)):
        total = jnp.zeros((ALL_ROWS, OUT_PART), F32)
        for j in range(0, SIDE, 2):
            for copy in loads[n * SIDE + j : n * SIDE + j + 2]:
                copy.wait()
            heads = [attended[:, t].reshape(ALL_ROWS, QF) for t in (j, j + 1)]
            rows = columns[n, j * QF : (j + 2) * QF]
            total = total + jnp.dot(
                jnp.concatenate(heads, axis=1), rows, preferred_element_type=F32
            )
        out[...] = total.astype(out.dtype)


def final_kernel(parts, entry, kept, first, second, third, up, out):
    shrunk = jnp.sum(parts[...].astype(F32), axis=0).astype(BF16).astype(F32)
    wide = expand(shrunk, entry[...])
    total = kept[...]
    for arrived in (first, second, third):
        total = total + arrived[...].astype(F32)
    total = total + low_rank_scale * contract(wide, up[...])
    for s in range(STEPS):
        lows = [t * MINE + s * LOCAL for t in range(N)]
        out[s] = jnp.concatenate([total[n : n + LOCAL] for n in lows], axis=0).astype(BF16)


def shard(
    hidden, w_query, w_key, w_value, w_out, key_cache, value_cache, lengths, row_slot, evict_slot,
    evict_adapter, owner, pool_a_in, pool_b_q, pool_b_k, pool_b_v, pool_a_o, pool_b_o,
    slot_a_in, slot_b_q, slot_b_k, slot_b_v, slot_a_o, slot_b_o,
):
    me = lax.axis_index("group")
    part = lax.axis_index(TP)
    place = lax.axis_index("x")[None]
    member = lax.axis_index("y")[None]

    with jax.named_scope("gather_in_maps"):
        packed = pl.pallas_call(
            pack_kernel,
            out_shape=jax.ShapeDtypeStruct((PACKED, IN_PART), BF16),
            in_specs=[hbm()] * 4,
            out_specs=vmem(),
            scratch_shapes=[
                pltpu.VMEM((HELD, RANK, QF), BF16),
                pltpu.VMEM((HELD, RANK, KF), BF16),
                pltpu.VMEM((HELD, RANK, KF), BF16),
                pltpu.SemaphoreType.DMA((HELD,)),
                pltpu.SemaphoreType.DMA((3,)),
            ],
            compiler_params=params(58),
            cost_estimate=cost(0, 2 << 20),
            name="pack",
        )(pool_a_in, pool_b_q, pool_b_k, pool_b_v)
        pool = lax.all_gather(packed, "group")

    with jax.named_scope("positions"):
        position = jnp.sum(
            jnp.where(evict_adapter[..., None] == jnp.arange(N * HELD), owner, 0), axis=-1
        )
        targets = lax.dynamic_slice_in_dim(evict_slot, me * LOADS, LOADS, 1)
        survivor = SLOTS * (SLOTS - 1) // 2 - jnp.sum(targets[0])
        placed = targets[:, :, None] == jnp.arange(SLOTS)
        order = 1 + jnp.arange(STEPS * LOADS).reshape(STEPS, LOADS, 1)
        slot_entry = jnp.sum(jnp.where(placed, order, 0), axis=1)
        second = jnp.where(slot_entry[1] > 0, slot_entry[1], slot_entry[0])
        slot_entry = jnp.stack([slot_entry[0], second])
        entry = jnp.sum(
            jnp.where(
                row_slot[:, :, None] == jnp.arange(SLOTS), slot_entry[:, None, :], 0
            ),
            axis=-1,
        )
        by_step = entry.reshape(1, ALL_ROWS)
        blocks = position % HELD % SHARED
        blocks = lax.dynamic_slice_in_dim(blocks, me * LOADS, LOADS, 1).reshape(1, 1, -1)
        load = jnp.arange(STEPS * LOADS) + 1
        blocks = jnp.sum(jnp.where(entry[:, :, None] == load, blocks, 0), axis=-1)
        blocks = blocks.reshape(ALL_ROWS, 1)
        by_owner = entry.reshape(STEPS, N, LOCAL).transpose(1, 0, 2)
        by_owner = by_owner.reshape(1, ALL_ROWS)
        my_wanted = lax.dynamic_slice_in_dim(position, me * LOADS, LOADS, 1)
        my_wanted = my_wanted.reshape(STEPS * LOADS)
        index = jnp.concatenate([survivor[None], my_wanted]).astype(jnp.int32)

    with jax.named_scope("columns_of_w_out"):
        w_out, packed = lax.optimization_barrier((w_out, packed))
        half = pl.pallas_call(
            split_kernel,
            out_shape=jax.ShapeDtypeStruct((SIDE, SIDE, QF, OUT_PART), BF16),
            in_specs=[hbm()],
            out_specs=vmem(),
            scratch_shapes=[pltpu.SemaphoreType.DMA((N,))],
            compiler_params=params(60),
            cost_estimate=cost(0, 8 << 20),
            name="split",
        )(w_out)
        mine = lax.all_to_all(half, "x", split_axis=0, concat_axis=0, tiled=True)

    with jax.named_scope("base_projections"):
        tokens = hidden.reshape(ALL_ROWS, -1)
        base_q = jnp.dot(tokens, w_query, preferred_element_type=F32)
        base_kv = jnp.concatenate(
            [
                jnp.dot(tokens, w_key, preferred_element_type=F32),
                jnp.dot(tokens, w_value, preferred_element_type=F32),
            ],
            axis=1,
        )
        tokens_part = lax.dynamic_slice_in_dim(tokens, part * IN_PART, IN_PART, 1).T

    with jax.named_scope("gather_out_maps"):
        out_pool = jnp.concatenate([pool_a_o, pool_b_o], axis=2)
        out_pool, index, base_q, base_kv, tokens_part, mine = lax.optimization_barrier(
            (out_pool, index, base_q, base_kv, tokens_part, mine)
        )
        out_pool = lax.all_gather(out_pool, "group").reshape(N * HELD, RANK, QF + OUT_PART)

    with jax.named_scope("shrink"):
        partial_in = pl.pallas_call(
            shrink_kernel,
            out_shape=jax.ShapeDtypeStruct((N, IN_RANK, ALL_ROWS), BF16),
            in_specs=[smem(), hbm(), hbm(), vmem(), vmem()],
            out_specs=vmem(),
            scratch_shapes=[
                pltpu.VMEM((ENTRIES * IN_RANK, IN_PART), BF16),
                pltpu.SemaphoreType.DMA((ENTRIES,)),
            ],
            compiler_params=params(60),
            cost_estimate=cost(2 * ENTRIES * IN_RANK * IN_PART * ALL_ROWS, 2 << 20),
            name="shrink",
        )(index, pool, slot_a_in, tokens_part, by_step)

        partial_in, picks = lax.optimization_barrier((partial_in, index))
        partials = lax.all_to_all(partial_in, TP, split_axis=0, concat_axis=0, tiled=True)

    with jax.named_scope("project"):
        up_q, up_kv = pl.pallas_call(
            pick_up_kernel,
            out_shape=[
                jax.ShapeDtypeStruct((ENTRIES * RANK, QF), BF16),
                jax.ShapeDtypeStruct((ENTRIES * RANK, IN_PART), BF16),
            ],
            in_specs=[smem(), hbm(), hbm(), vmem(), vmem()],
            out_specs=[vmem()] * 2,
            scratch_shapes=[pltpu.SemaphoreType.DMA((ENTRIES,))] * 2,
            compiler_params=params(52),
            cost_estimate=cost(0, 2 << 20),
            name="pick_up",
        )(picks, pool, slot_b_q, slot_b_k, slot_b_v)
        projected = pl.pallas_call(
            project_kernel,
            out_shape=jax.ShapeDtypeStruct((N, MINE, QF + 2 * KF), BF16),
            in_specs=[vmem()] * 7,
            out_specs=vmem(),
            compiler_params=params(16),
            cost_estimate=cost(2 * 400 * 512 * ALL_ROWS, 1 << 20),
            name="project",
        )(partials, by_step, blocks, base_q, base_kv, up_q, up_kv)

    with jax.named_scope("attend"):
        received = lax.all_to_all(projected, TP, split_axis=0, concat_axis=0, tiled=True)
        payload = pl.pallas_call(
            attend_kernel,
            out_shape=jax.ShapeDtypeStruct((N, SIDE, MINE, QF), BF16),
            in_specs=[smem(), vmem(), hbm(), hbm()],
            out_specs=hbm(),
            scratch_shapes=[
                pltpu.VMEM((LOCAL, LENGTH, KW), BF16),
                pltpu.VMEM((LOCAL, LENGTH, KW), BF16),
                pltpu.VMEM((N * MINE, QF), BF16),
                pltpu.VMEM((SIDE, SIDE, MINE, QF), BF16),
                pltpu.SemaphoreType.DMA((LOCAL,)),
                pltpu.SemaphoreType.DMA((LOCAL,)),
                pltpu.SemaphoreType.DMA((N,)),
            ],
            compiler_params=params(60),
            cost_estimate=cost(4 * LOCAL * 64 * KW * LENGTH, 12 << 20),
            name="attend",
        )(lengths, received, key_cache, value_cache)
        gathered = lax.all_to_all(payload, TP, split_axis=0, concat_axis=0, tiled=True)

        payload, picks = lax.optimization_barrier((payload, index))
        maps, up_o = pl.pallas_call(
            pick_kernel,
            out_shape=[
                jax.ShapeDtypeStruct((ENTRIES * RANK, QF), BF16),
                jax.ShapeDtypeStruct((ENTRIES * RANK, OUT_PART), BF16),
            ],
            in_specs=[smem()] + [hbm()] * 3,
            out_specs=[vmem()] * 2,
            scratch_shapes=[pltpu.SemaphoreType.DMA((ENTRIES,))] * 2,
            compiler_params=params(24),
            cost_estimate=cost(0, 3 << 20),
            name="pick",
        )(picks, slot_a_o, slot_b_o, out_pool)

    with jax.named_scope("output"):
        block = (ALL_ROWS, OUT_PART)
        partial_out, *passed, kept_out = pl.pallas_call(
            base_out_kernel,
            out_shape=[jax.ShapeDtypeStruct((N, RANK, ALL_ROWS), BF16)]
            + [jax.ShapeDtypeStruct(block, BF16)] * 3
            + [jax.ShapeDtypeStruct(block, F32)],
            in_specs=[smem()] * 2 + [vmem()] * 3 + [hbm()],
            out_specs=[vmem()] * 5,
            scratch_shapes=[
                pltpu.VMEM((SIDE, WIDE, OUT_PART), BF16),
                pltpu.SemaphoreType.DMA((SIDE, SIDE)),
            ],
            compiler_params=params(24),
            cost_estimate=cost(2 * ALL_ROWS * FEATURES * OUT_PART, 5 << 20),
            name="base_out",
        )(place, member, gathered, by_owner, maps, mine)
        partials_out = lax.all_to_all(partial_out, TP, split_axis=0, concat_axis=0, tiled=True)
        turns = [[(i, (i + k) % SIDE) for i in range(SIDE)] for k in range(1, SIDE)]
        passed = [lax.ppermute(p, "y", turn) for p, turn in zip(passed, turns)]
        return pl.pallas_call(
            final_kernel,
            out_shape=jax.ShapeDtypeStruct((STEPS, ROWS, OUT_PART), BF16),
            in_specs=[vmem()] * 7,
            out_specs=vmem(),
            compiler_params=params(16),
            cost_estimate=cost(2 * 400 * OUT_PART * ALL_ROWS, 1 << 20),
            name="final",
        )(partials_out, by_owner, kept_out, *passed, up_o)


def solution(mesh):
    grid = jax.sharding.Mesh(mesh.devices.reshape(N, SIDE, SIDE), ("group",) + TP)
    pooled = P("group", None, TP)
    cached = P(("group",) + TP, None, None)
    placed = (
        P(None, "group", None), P(None, TP), P(None, TP), P(None, TP), P(TP, None),
        cached, cached, P(("group",) + TP), P(None, "group"), P(), P(), P(),
    ) + (pooled,) * 12
    return jax.shard_map(
        shard, mesh=grid, in_specs=placed, out_specs=P(None, "group", TP), check_vma=False
    )
```

```python
import math

import jax
import jax.numpy as jnp
from jax import lax
from jax.experimental import pallas as pl
from jax.experimental.pallas import tpu as pltpu
from jax.sharding import PartitionSpec as P

QH = 32
KH = 4
HD = 128
STEPS = 2
ROWS = 128
RANK = 16
LOADS = 12
SLOTS = 13
HELD = 12
N = 16
SIDE = 4
GROUPED = 2
ALL_ROWS = STEPS * ROWS
LOCAL = ROWS // N
MINE = STEPS * LOCAL
ENTRIES = 1 + STEPS * LOADS
SHARED = 8
Q_AT = HELD * 48
KV_AT = Q_AT + HELD // 2 * RANK
PACKED = KV_AT + 2 * RANK
IN_RANK = 3 * RANK
QF = 256
KF = 32
IN_PART = 512
OUT_PART = 512
FEATURES = QH * HD
QKV = QF + 2 * KF
TP = ("y", "x")
LENGTH = 512
KW = KH * HD
BF16 = jnp.bfloat16
F32 = jnp.float32
low_rank_scale = 0.5


def vmem():
    return pl.BlockSpec(memory_space=pltpu.VMEM)


def hbm():
    return pl.BlockSpec(memory_space=pl.ANY)


def smem():
    return pl.BlockSpec(memory_space=pltpu.SMEM)


def params(mib=40):
    return pltpu.CompilerParams(vmem_limit_bytes=mib * 1024 * 1024)


def cost(flops, nbytes):
    return pl.CostEstimate(flops=flops, bytes_accessed=nbytes, transcendentals=0)


def iota(shape, axis):
    return lax.broadcasted_iota(jnp.int32, shape, axis)


def pack_kernel(maps_in, maps_q, maps_k, maps_v, out, all_q, all_k, all_v, in_sem, sem):
    copies = [
        pltpu.make_async_copy(maps_q, all_q, sem.at[0]),
        pltpu.make_async_copy(maps_k, all_k, sem.at[1]),
        pltpu.make_async_copy(maps_v, all_v, sem.at[2]),
    ]
    for k in range(HELD):
        rows = pl.ds(k * IN_RANK, IN_RANK)
        copies.append(pltpu.make_async_copy(maps_in.at[k], out.at[rows], in_sem.at[k]))
    for copy in copies:
        copy.start()
    for copy in copies[:3]:
        copy.wait()
    for k in range(HELD):
        low, block = Q_AT + k // 2 * RANK, k % 2 * QF
        out[low : low + RANK, block : block + QF] = all_q[k]
    empty = jnp.zeros((RANK, 2 * KF), BF16)
    for first in range(0, 2 * SHARED, SHARED):
        pieces = []
        for k in range(first, first + SHARED):
            pieces += [all_k[k], all_v[k]] if k < HELD else [empty]
        low = KV_AT + first // SHARED * RANK
        out[low : low + RANK] = jnp.concatenate(pieces, axis=1)
    for copy in copies[3:]:
        copy.wait()


def aligned(value, unit):
    return pl.multiple_of(value * unit, unit)


def shrink_kernel(index, pool, slot, tokens, entry, out, maps, arrived):
    copies = []
    for i in range(ENTRIES):
        if i == 0:
            origin = slot.at[index[0]]
        else:
            rows = pl.ds(aligned(lax.rem(index[i], HELD), IN_RANK), IN_RANK)
            origin = pool.at[index[i] // HELD, rows]
        copy = pltpu.make_async_copy(origin, maps.at[pl.ds(i * IN_RANK, IN_RANK)], arrived.at[i])
        copy.start()
        copies.append(copy)
    for copy in copies:
        copy.wait()
    used = entry[...]
    product = jnp.dot(maps[...], tokens[...], preferred_element_type=F32)
    total = jnp.zeros((IN_RANK, ALL_ROWS), F32)
    for i in range(ENTRIES):
        total = total + jnp.where(used == i, product[i * IN_RANK : (i + 1) * IN_RANK], 0.0)
    total = total.astype(BF16)
    for n in range(N):
        out[n] = total


def expand(shrunk, entry):
    blocks = [jnp.where(entry == i, shrunk, 0.0) for i in range(ENTRIES)]
    return jnp.concatenate(blocks, axis=0).astype(BF16)


def contract(left, right):
    return lax.dot_general(left, right, (((0,), (0,)), ((), ())), preferred_element_type=F32)


def pick_up_kernel(index, pool, slot_q, slot_k, slot_v, up_q, up_kv, q_sem, kv_sem):
    copies = []
    for i in range(ENTRIES):
        rows = pl.ds(i * RANK, RANK)
        if i == 0:
            copies.append(pltpu.make_async_copy(slot_q.at[index[0]], up_q.at[rows], q_sem.at[0]))
            continue
        source, k = index[i] // HELD, lax.rem(index[i], HELD)
        of_q = pl.ds(Q_AT + aligned(k // 2, RANK), RANK)
        block = pl.ds(aligned(lax.rem(k, 2), QF), QF)
        of_kv = pl.ds(KV_AT + aligned(k // SHARED, RANK), RANK)
        copies.append(
            pltpu.make_async_copy(pool.at[source, of_q, block], up_q.at[rows], q_sem.at[i])
        )
        copies.append(pltpu.make_async_copy(pool.at[source, of_kv], up_kv.at[rows], kv_sem.at[i]))
    for copy in copies:
        copy.start()
    empty = jnp.zeros((RANK, IN_PART - 2 * KF), BF16)
    up_kv[:RANK] = jnp.concatenate([slot_k[index[0]], slot_v[index[0]], empty], axis=1)
    for copy in copies:
        copy.wait()


def project_kernel(parts, entry, block, base_q, base_kv, up_q, up_kv, out):
    shrunk = jnp.sum(parts[...].astype(F32), axis=0).astype(BF16).astype(F32)
    used = entry[...]
    wide_q = expand(shrunk[:RANK], used)
    wide_k = expand(shrunk[RANK : 2 * RANK], used)
    wide_v = expand(shrunk[2 * RANK :], used)
    query = base_q[...] + low_rank_scale * contract(wide_q, up_q[...])
    delta_k = contract(wide_k, up_kv[...])
    delta_v = contract(wide_v, up_kv[...])
    delta = jnp.where(iota(delta_k.shape, 1) % (2 * KF) < KF, delta_k, delta_v)
    delta = jnp.where(iota(delta.shape, 1) // (2 * KF) == block[...], delta, 0.0)
    folded = jnp.zeros((ALL_ROWS, 2 * KF), F32)
    for j in range(SHARED):
        folded = folded + delta[:, j * 2 * KF : (j + 1) * 2 * KF]
    fresh = base_kv[...] + low_rank_scale * folded
    for t in range(N):
        lows = [s * ROWS + t * LOCAL for s in range(STEPS)]
        out[t, :, :QF] = jnp.concatenate([query[n : n + LOCAL] for n in lows], 0).astype(BF16)
        out[t, :, QF:] = jnp.concatenate([fresh[n : n + LOCAL] for n in lows], 0).astype(BF16)


def split_kernel(weight, out, arrived):
    copies = []
    for t in range(N):
        source = weight.at[:, pl.ds(t * OUT_PART, OUT_PART)]
        copies.append(
            pltpu.make_async_copy(source, out.at[t % SIDE, t // SIDE], arrived.at[t])
        )
    for copy in copies:
        copy.start()
    for copy in copies:
        copy.wait()


def transposing():
    shape = (N * MINE, N * MINE)
    row, column = iota(shape, 0), iota(shape, 1)
    return ((row // N == column % N) & (row % N == column // N)).astype(BF16)


def attend_kernel(
    lengths, received, keys, values, out, key_rows, value_rows, by_row, ready, key_sem, value_sem,
    sent,
):
    loads = []
    for i in range(LOCAL):
        pair = (
            pltpu.make_async_copy(keys.at[i], key_rows.at[i], key_sem.at[i]),
            pltpu.make_async_copy(values.at[i], value_rows.at[i], value_sem.at[i]),
        )
        for copy in pair:
            copy.start()
        loads.append(pair)
    swap = transposing()
    mine = jnp.dot(swap, received[...].reshape(N * MINE, -1), preferred_element_type=F32)
    mine = mine.astype(BF16)
    shape = (2 * KF, KW)
    feature, column = iota(shape, 0), iota(shape, 1) % KF
    block = iota((N * MINE, KW), 1) // KF == iota((N * MINE, KW), 0) % N
    fold = (iota((MINE, N * MINE), 1) // N == iota((MINE, N * MINE), 0)).astype(BF16)

    def fresh(first):
        repeat = (feature - first == column).astype(BF16)
        wide = jnp.dot(mine[:, QF:], repeat, preferred_element_type=F32)
        wide = jnp.where(block, wide, 0.0).astype(BF16)
        return jnp.dot(fold, wide, preferred_element_type=F32).astype(BF16)

    keys_new, values_new = fresh(0), fresh(KF)

    head_rows = STEPS * QH
    own = iota((head_rows, KW), 0) % N // (N // KH) == iota((head_rows, KW), 1) // HD
    place = iota((head_rows, LENGTH), 1)
    shape = (head_rows, MINE)
    new_step, new_row = iota(shape, 1) // LOCAL, iota(shape, 1) % LOCAL
    in_time = new_step <= iota(shape, 0) // QH
    scale = 1.0 / math.sqrt(HD)
    dims = (((1,), (1,)), ((), ()))
    for i in range(LOCAL):
        if i % GROUPED == 0:
            for pair in loads[i : i + GROUPED]:
                for copy in pair:
                    copy.wait()
        asked = []
        for s in range(STEPS):
            low = (s * LOCAL + i) * N
            asked += [mine[low : low + N, :HD], mine[low : low + N, HD:QF]]
        asked = jnp.concatenate(asked, axis=0)
        spread = jnp.where(own, jnp.concatenate([asked] * KH, axis=1), jnp.zeros((), BF16))
        new = lax.dot_general(spread, keys_new, dims, preferred_element_type=F32) * scale
        new = jnp.where(in_time & (new_row == i), new, -jnp.inf)
        old = lax.dot_general(spread, key_rows[i], dims, preferred_element_type=F32) * scale
        old = jnp.where(place < lengths[i], old, -jnp.inf)
        highest = jnp.maximum(
            jnp.max(old, axis=1, keepdims=True), jnp.max(new, axis=1, keepdims=True)
        )
        old, new = jnp.exp(old - highest), jnp.exp(new - highest)
        totals = jnp.sum(old, axis=1, keepdims=True) + jnp.sum(new, axis=1, keepdims=True)
        mixed = jnp.dot(old.astype(BF16), value_rows[i], preferred_element_type=F32)
        mixed = mixed + jnp.dot(new.astype(BF16), values_new, preferred_element_type=F32)
        mixed = jnp.where(own, mixed, 0.0)
        attended = mixed[:, :HD]
        for k in range(1, KH):
            attended = attended + mixed[:, k * HD : (k + 1) * HD]
        attended = (attended / totals).astype(BF16)
        for s in range(STEPS):
            low = (s * LOCAL + i) * N
            for half in range(2):
                piece = attended[(2 * s + half) * N : (2 * s + half + 1) * N]
                by_row[low : low + N, half * HD : (half + 1) * HD] = piece

    attended = jnp.dot(swap, by_row[...], preferred_element_type=F32).astype(BF16)
    ready[...] = attended.reshape(SIDE, SIDE, MINE, QF)
    copies = [
        pltpu.make_async_copy(ready.at[n // SIDE], out.at[n], sent.at[n]) for n in range(N)
    ]
    for copy in copies:
        copy.start()
    for copy in copies:
        copy.wait()


def pick_kernel(index, slot_in, slot_up, pool, maps, up, map_sem, up_sem):
    copies = []
    for i in range(ENTRIES):
        if i == 0:
            first, second = slot_in.at[index[0]], slot_up.at[index[0]]
        else:
            first = pool.at[index[i], :, pl.ds(0, QF)]
            second = pool.at[index[i], :, pl.ds(QF, OUT_PART)]
        rows = pl.ds(i * RANK, RANK)
        copies.append(pltpu.make_async_copy(first, maps.at[rows], map_sem.at[i]))
        copies.append(pltpu.make_async_copy(second, up.at[rows], up_sem.at[i]))
    for copy in copies:
        copy.start()
    for copy in copies:
        copy.wait()


def base_out_kernel(
    place, member, attended, entry, maps, source, partial, first, second, third, kept
):
    heads = attended[:, pl.ds(place[0], 1)].reshape(ALL_ROWS, QF)
    product = lax.dot_general(
        maps[...], heads, (((1,), (1,)), ((), ())), preferred_element_type=F32
    )
    used = entry[...]
    shrunk = jnp.zeros((RANK, ALL_ROWS), F32)
    for i in range(ENTRIES):
        shrunk = shrunk + jnp.where(used == i, product[i * RANK : (i + 1) * RANK], 0.0)
    shrunk = shrunk.astype(BF16)
    for n in range(N):
        partial[n] = shrunk
    heads = [attended[:, t].reshape(ALL_ROWS, QF) for t in range(SIDE)]
    for k, out in ((1, first), (2, second), (3, third), (0, kept)):
        whose = lax.rem(member[0] + k, SIDE)
        total = jnp.zeros((ALL_ROWS, OUT_PART), F32)
        for j in range(0, SIDE, 2):
            rows = jnp.concatenate([source[t, whose] for t in (j, j + 1)], axis=0)
            total = total + jnp.dot(
                jnp.concatenate(heads[j : j + 2], axis=1), rows, preferred_element_type=F32
            )
        out[...] = total.astype(out.dtype)


def final_kernel(parts, entry, kept, first, second, third, up, out):
    shrunk = jnp.sum(parts[...].astype(F32), axis=0).astype(BF16).astype(F32)
    wide = expand(shrunk, entry[...])
    total = kept[...]
    for arrived in (first, second, third):
        total = total + arrived[...].astype(F32)
    total = total + low_rank_scale * contract(wide, up[...])
    for s in range(STEPS):
        lows = [t * MINE + s * LOCAL for t in range(N)]
        out[s] = jnp.concatenate([total[n : n + LOCAL] for n in lows], axis=0).astype(BF16)


def shard(
    hidden, w_query, w_key, w_value, w_out, key_cache, value_cache, lengths, row_slot, evict_slot,
    evict_adapter, owner, pool_a_in, pool_b_q, pool_b_k, pool_b_v, pool_a_o, pool_b_o,
    slot_a_in, slot_b_q, slot_b_k, slot_b_v, slot_a_o, slot_b_o,
):
    me = lax.axis_index("group")
    part = lax.axis_index(TP)
    place = lax.axis_index("x")[None]
    member = lax.axis_index("y")[None]

    with jax.named_scope("gather_in_maps"):
        packed = pl.pallas_call(
            pack_kernel,
            out_shape=jax.ShapeDtypeStruct((PACKED, IN_PART), BF16),
            in_specs=[hbm()] * 4,
            out_specs=vmem(),
            scratch_shapes=[
                pltpu.VMEM((HELD, RANK, QF), BF16),
                pltpu.VMEM((HELD, RANK, KF), BF16),
                pltpu.VMEM((HELD, RANK, KF), BF16),
                pltpu.SemaphoreType.DMA((HELD,)),
                pltpu.SemaphoreType.DMA((3,)),
            ],
            compiler_params=params(58),
            cost_estimate=cost(0, 2 << 20),
            name="pack",
        )(pool_a_in, pool_b_q, pool_b_k, pool_b_v)
        pool = lax.all_gather(packed, "group")

    with jax.named_scope("positions"):
        position = jnp.sum(
            jnp.where(evict_adapter[..., None] == jnp.arange(N * HELD), owner, 0), axis=-1
        )
        targets = lax.dynamic_slice_in_dim(evict_slot, me * LOADS, LOADS, 1)
        survivor = SLOTS * (SLOTS - 1) // 2 - jnp.sum(targets[0])
        placed = targets[:, :, None] == jnp.arange(SLOTS)
        order = 1 + jnp.arange(STEPS * LOADS).reshape(STEPS, LOADS, 1)
        slot_entry = jnp.sum(jnp.where(placed, order, 0), axis=1)
        second = jnp.where(slot_entry[1] > 0, slot_entry[1], slot_entry[0])
        slot_entry = jnp.stack([slot_entry[0], second])
        entry = jnp.sum(
            jnp.where(
                row_slot[:, :, None] == jnp.arange(SLOTS), slot_entry[:, None, :], 0
            ),
            axis=-1,
        )
        by_step = entry.reshape(1, ALL_ROWS)
        blocks = position % HELD % SHARED
        blocks = lax.dynamic_slice_in_dim(blocks, me * LOADS, LOADS, 1).reshape(1, 1, -1)
        load = jnp.arange(STEPS * LOADS) + 1
        blocks = jnp.sum(jnp.where(entry[:, :, None] == load, blocks, 0), axis=-1)
        blocks = blocks.reshape(ALL_ROWS, 1)
        by_owner = entry.reshape(STEPS, N, LOCAL).transpose(1, 0, 2)
        by_owner = by_owner.reshape(1, ALL_ROWS)
        my_wanted = lax.dynamic_slice_in_dim(position, me * LOADS, LOADS, 1)
        my_wanted = my_wanted.reshape(STEPS * LOADS)
        index = jnp.concatenate([survivor[None], my_wanted]).astype(jnp.int32)

    with jax.named_scope("columns_of_w_out"):
        w_out, packed = lax.optimization_barrier((w_out, packed))
        half = pl.pallas_call(
            split_kernel,
            out_shape=jax.ShapeDtypeStruct((SIDE, SIDE, QF, OUT_PART), BF16),
            in_specs=[hbm()],
            out_specs=vmem(),
            scratch_shapes=[pltpu.SemaphoreType.DMA((N,))],
            compiler_params=params(60),
            cost_estimate=cost(0, 8 << 20),
            name="split",
        )(w_out)
        mine = lax.all_to_all(half, "x", split_axis=0, concat_axis=0, tiled=True)

    with jax.named_scope("base_projections"):
        tokens = hidden.reshape(ALL_ROWS, -1)
        base_q = jnp.dot(tokens, w_query, preferred_element_type=F32)
        base_kv = jnp.concatenate(
            [
                jnp.dot(tokens, w_key, preferred_element_type=F32),
                jnp.dot(tokens, w_value, preferred_element_type=F32),
            ],
            axis=1,
        )
        tokens_part = lax.dynamic_slice_in_dim(tokens, part * IN_PART, IN_PART, 1).T

    with jax.named_scope("gather_out_maps"):
        out_pool = jnp.concatenate([pool_a_o, pool_b_o], axis=2)
        out_pool, index, base_q, base_kv, tokens_part, mine = lax.optimization_barrier(
            (out_pool, index, base_q, base_kv, tokens_part, mine)
        )
        out_pool = lax.all_gather(out_pool, "group").reshape(N * HELD, RANK, QF + OUT_PART)

    with jax.named_scope("shrink"):
        partial_in = pl.pallas_call(
            shrink_kernel,
            out_shape=jax.ShapeDtypeStruct((N, IN_RANK, ALL_ROWS), BF16),
            in_specs=[smem(), hbm(), hbm(), vmem(), vmem()],
            out_specs=vmem(),
            scratch_shapes=[
                pltpu.VMEM((ENTRIES * IN_RANK, IN_PART), BF16),
                pltpu.SemaphoreType.DMA((ENTRIES,)),
            ],
            compiler_params=params(60),
            cost_estimate=cost(2 * ENTRIES * IN_RANK * IN_PART * ALL_ROWS, 2 << 20),
            name="shrink",
        )(index, pool, slot_a_in, tokens_part, by_step)

        partial_in, picks = lax.optimization_barrier((partial_in, index))
        partials = lax.all_to_all(partial_in, TP, split_axis=0, concat_axis=0, tiled=True)

    with jax.named_scope("project"):
        up_q, up_kv = pl.pallas_call(
            pick_up_kernel,
            out_shape=[
                jax.ShapeDtypeStruct((ENTRIES * RANK, QF), BF16),
                jax.ShapeDtypeStruct((ENTRIES * RANK, IN_PART), BF16),
            ],
            in_specs=[smem(), hbm(), hbm(), vmem(), vmem()],
            out_specs=[vmem()] * 2,
            scratch_shapes=[pltpu.SemaphoreType.DMA((ENTRIES,))] * 2,
            compiler_params=params(52),
            cost_estimate=cost(0, 2 << 20),
            name="pick_up",
        )(picks, pool, slot_b_q, slot_b_k, slot_b_v)
        projected = pl.pallas_call(
            project_kernel,
            out_shape=jax.ShapeDtypeStruct((N, MINE, QF + 2 * KF), BF16),
            in_specs=[vmem()] * 7,
            out_specs=vmem(),
            compiler_params=params(16),
            cost_estimate=cost(2 * 400 * 512 * ALL_ROWS, 1 << 20),
            name="project",
        )(partials, by_step, blocks, base_q, base_kv, up_q, up_kv)

    with jax.named_scope("attend"):
        received = lax.all_to_all(projected, TP, split_axis=0, concat_axis=0, tiled=True)
        payload = pl.pallas_call(
            attend_kernel,
            out_shape=jax.ShapeDtypeStruct((N, SIDE, MINE, QF), BF16),
            in_specs=[smem(), vmem(), hbm(), hbm()],
            out_specs=hbm(),
            scratch_shapes=[
                pltpu.VMEM((LOCAL, LENGTH, KW), BF16),
                pltpu.VMEM((LOCAL, LENGTH, KW), BF16),
                pltpu.VMEM((N * MINE, QF), BF16),
                pltpu.VMEM((SIDE, SIDE, MINE, QF), BF16),
                pltpu.SemaphoreType.DMA((LOCAL,)),
                pltpu.SemaphoreType.DMA((LOCAL,)),
                pltpu.SemaphoreType.DMA((N,)),
            ],
            compiler_params=params(60),
            cost_estimate=cost(4 * LOCAL * 64 * KW * LENGTH, 12 << 20),
            name="attend",
        )(lengths, received, key_cache, value_cache)
        gathered = lax.all_to_all(payload, TP, split_axis=0, concat_axis=0, tiled=True)

        payload, picks = lax.optimization_barrier((payload, index))
        maps, up_o = pl.pallas_call(
            pick_kernel,
            out_shape=[
                jax.ShapeDtypeStruct((ENTRIES * RANK, QF), BF16),
                jax.ShapeDtypeStruct((ENTRIES * RANK, OUT_PART), BF16),
            ],
            in_specs=[smem()] + [hbm()] * 3,
            out_specs=[vmem()] * 2,
            scratch_shapes=[pltpu.SemaphoreType.DMA((ENTRIES,))] * 2,
            compiler_params=params(24),
            cost_estimate=cost(0, 3 << 20),
            name="pick",
        )(picks, slot_a_o, slot_b_o, out_pool)

    with jax.named_scope("output"):
        block = (ALL_ROWS, OUT_PART)
        partial_out, *passed, kept_out = pl.pallas_call(
            base_out_kernel,
            out_shape=[jax.ShapeDtypeStruct((N, RANK, ALL_ROWS), BF16)]
            + [jax.ShapeDtypeStruct(block, BF16)] * 3
            + [jax.ShapeDtypeStruct(block, F32)],
            in_specs=[smem()] * 2 + [vmem()] * 4,
            out_specs=[vmem()] * 5,
            compiler_params=params(24),
            cost_estimate=cost(2 * ALL_ROWS * FEATURES * OUT_PART, 5 << 20),
            name="base_out",
        )(place, member, gathered, by_owner, maps, mine)
        partials_out = lax.all_to_all(partial_out, TP, split_axis=0, concat_axis=0, tiled=True)
        turns = [[(i, (i + k) % SIDE) for i in range(SIDE)] for k in range(1, SIDE)]
        passed = [lax.ppermute(p, "y", turn) for p, turn in zip(passed, turns)]
        return pl.pallas_call(
            final_kernel,
            out_shape=jax.ShapeDtypeStruct((STEPS, ROWS, OUT_PART), BF16),
            in_specs=[vmem()] * 7,
            out_specs=vmem(),
            compiler_params=params(16),
            cost_estimate=cost(2 * 400 * OUT_PART * ALL_ROWS, 1 << 20),
            name="final",
        )(partials_out, by_owner, kept_out, *passed, up_o)


def solution(mesh):
    grid = jax.sharding.Mesh(mesh.devices.reshape(N, SIDE, SIDE), ("group",) + TP)
    pooled = P("group", None, TP)
    cached = P(("group",) + TP, None, None)
    placed = (
        P(None, "group", None), P(None, TP), P(None, TP), P(None, TP), P(TP, None),
        cached, cached, P(("group",) + TP), P(None, "group"), P(), P(), P(),
    ) + (pooled,) * 12
    return jax.shard_map(
        shard, mesh=grid, in_specs=placed, out_specs=P(None, "group", TP), check_vma=False
    )
```

```python
import math

import jax
import jax.numpy as jnp
from jax import lax
from jax.experimental import pallas as pl
from jax.experimental.pallas import tpu as pltpu
from jax.sharding import PartitionSpec as P

QH = 32
KH = 4
HD = 128
STEPS = 2
ROWS = 128
RANK = 16
LOADS = 12
SLOTS = 13
HELD = 12
N = 16
SIDE = 4
GROUPED = 2
ALL_ROWS = STEPS * ROWS
LOCAL = ROWS // N
MINE = STEPS * LOCAL
ENTRIES = 1 + STEPS * LOADS
SHARED = 8
Q_AT = HELD * 48
KV_AT = Q_AT + HELD // 2 * RANK
PACKED = KV_AT + 2 * RANK
IN_RANK = 3 * RANK
QF = 256
KF = 32
IN_PART = 512
OUT_PART = 512
FEATURES = QH * HD
QKV = QF + 2 * KF
TP = ("y", "x")
LENGTH = 512
KW = KH * HD
BF16 = jnp.bfloat16
F32 = jnp.float32
low_rank_scale = 0.5


def vmem():
    return pl.BlockSpec(memory_space=pltpu.VMEM)


def hbm():
    return pl.BlockSpec(memory_space=pl.ANY)


def smem():
    return pl.BlockSpec(memory_space=pltpu.SMEM)


def params(mib=40):
    return pltpu.CompilerParams(vmem_limit_bytes=mib * 1024 * 1024)


def cost(flops, nbytes):
    return pl.CostEstimate(flops=flops, bytes_accessed=nbytes, transcendentals=0)


def iota(shape, axis):
    return lax.broadcasted_iota(jnp.int32, shape, axis)


def pack_kernel(maps_in, maps_q, maps_k, maps_v, out, all_q, all_k, all_v, in_sem, sem):
    copies = [
        pltpu.make_async_copy(maps_q, all_q, sem.at[0]),
        pltpu.make_async_copy(maps_k, all_k, sem.at[1]),
        pltpu.make_async_copy(maps_v, all_v, sem.at[2]),
    ]
    for k in range(HELD):
        rows = pl.ds(k * IN_RANK, IN_RANK)
        copies.append(pltpu.make_async_copy(maps_in.at[k], out.at[rows], in_sem.at[k]))
    for copy in copies:
        copy.start()
    for copy in copies[:3]:
        copy.wait()
    for k in range(HELD):
        low, block = Q_AT + k // 2 * RANK, k % 2 * QF
        out[low : low + RANK, block : block + QF] = all_q[k]
    empty = jnp.zeros((RANK, 2 * KF), BF16)
    for first in range(0, 2 * SHARED, SHARED):
        pieces = []
        for k in range(first, first + SHARED):
            pieces += [all_k[k], all_v[k]] if k < HELD else [empty]
        low = KV_AT + first // SHARED * RANK
        out[low : low + RANK] = jnp.concatenate(pieces, axis=1)
    for copy in copies[3:]:
        copy.wait()


def aligned(value, unit):
    return pl.multiple_of(value * unit, unit)


def shrink_kernel(index, pool, slot, tokens, entry, out, maps, arrived):
    copies = []
    for i in range(ENTRIES):
        if i == 0:
            origin = slot.at[index[0]]
        else:
            rows = pl.ds(aligned(lax.rem(index[i], HELD), IN_RANK), IN_RANK)
            origin = pool.at[index[i] // HELD, rows]
        copy = pltpu.make_async_copy(origin, maps.at[pl.ds(i * IN_RANK, IN_RANK)], arrived.at[i])
        copy.start()
        copies.append(copy)
    for copy in copies:
        copy.wait()
    used = entry[...]
    product = jnp.dot(maps[...], tokens[...], preferred_element_type=F32)
    total = jnp.zeros((IN_RANK, ALL_ROWS), F32)
    for i in range(ENTRIES):
        total = total + jnp.where(used == i, product[i * IN_RANK : (i + 1) * IN_RANK], 0.0)
    total = total.astype(BF16)
    for n in range(N):
        out[n] = total


def expand(shrunk, entry):
    blocks = [jnp.where(entry == i, shrunk, 0.0) for i in range(ENTRIES)]
    return jnp.concatenate(blocks, axis=0).astype(BF16)


def contract(left, right):
    return lax.dot_general(left, right, (((0,), (0,)), ((), ())), preferred_element_type=F32)


def pick_up_kernel(index, pool, slot_q, slot_k, slot_v, up_q, up_kv, q_sem, kv_sem):
    copies = []
    for i in range(ENTRIES):
        rows = pl.ds(i * RANK, RANK)
        if i == 0:
            copies.append(pltpu.make_async_copy(slot_q.at[index[0]], up_q.at[rows], q_sem.at[0]))
            continue
        source, k = index[i] // HELD, lax.rem(index[i], HELD)
        of_q = pl.ds(Q_AT + aligned(k // 2, RANK), RANK)
        block = pl.ds(aligned(lax.rem(k, 2), QF), QF)
        of_kv = pl.ds(KV_AT + aligned(k // SHARED, RANK), RANK)
        copies.append(
            pltpu.make_async_copy(pool.at[source, of_q, block], up_q.at[rows], q_sem.at[i])
        )
        copies.append(pltpu.make_async_copy(pool.at[source, of_kv], up_kv.at[rows], kv_sem.at[i]))
    for copy in copies:
        copy.start()
    empty = jnp.zeros((RANK, IN_PART - 2 * KF), BF16)
    up_kv[:RANK] = jnp.concatenate([slot_k[index[0]], slot_v[index[0]], empty], axis=1)
    for copy in copies:
        copy.wait()


def project_kernel(parts, entry, block, base_q, base_kv, up_q, up_kv, out):
    shrunk = jnp.sum(parts[...].astype(F32), axis=0).astype(BF16).astype(F32)
    used = entry[...]
    wide_q = expand(shrunk[:RANK], used)
    wide_k = expand(shrunk[RANK : 2 * RANK], used)
    wide_v = expand(shrunk[2 * RANK :], used)
    query = base_q[...] + low_rank_scale * contract(wide_q, up_q[...])
    delta_k = contract(wide_k, up_kv[...])
    delta_v = contract(wide_v, up_kv[...])
    delta = jnp.where(iota(delta_k.shape, 1) % (2 * KF) < KF, delta_k, delta_v)
    delta = jnp.where(iota(delta.shape, 1) // (2 * KF) == block[...], delta, 0.0)
    folded = jnp.zeros((ALL_ROWS, 2 * KF), F32)
    for j in range(SHARED):
        folded = folded + delta[:, j * 2 * KF : (j + 1) * 2 * KF]
    fresh = base_kv[...] + low_rank_scale * folded
    for t in range(N):
        lows = [s * ROWS + t * LOCAL for s in range(STEPS)]
        out[t, :, :QF] = jnp.concatenate([query[n : n + LOCAL] for n in lows], 0).astype(BF16)
        out[t, :, QF:] = jnp.concatenate([fresh[n : n + LOCAL] for n in lows], 0).astype(BF16)


def split_kernel(weight, out, arrived):
    copies = []
    for t in range(N):
        source = weight.at[:, pl.ds(t * OUT_PART, OUT_PART)]
        copies.append(
            pltpu.make_async_copy(source, out.at[t % SIDE, t // SIDE], arrived.at[t])
        )
    for copy in copies:
        copy.start()
    for copy in copies:
        copy.wait()


def transposing():
    shape = (N * MINE, N * MINE)
    row, column = iota(shape, 0), iota(shape, 1)
    return ((row // N == column % N) & (row % N == column // N)).astype(BF16)


def attend_kernel(
    lengths, received, keys, values, out, key_rows, value_rows, by_row, ready, key_sem, value_sem,
    sent,
):
    loads = []
    for i in range(LOCAL):
        pair = (
            pltpu.make_async_copy(keys.at[i], key_rows.at[i], key_sem.at[i]),
            pltpu.make_async_copy(values.at[i], value_rows.at[i], value_sem.at[i]),
        )
        for copy in pair:
            copy.start()
        loads.append(pair)
    swap = transposing()
    mine = jnp.dot(swap, received[...].reshape(N * MINE, -1), preferred_element_type=F32)
    mine = mine.astype(BF16)
    shape = (2 * KF, KW)
    feature, column = iota(shape, 0), iota(shape, 1) % KF
    block = iota((N * MINE, KW), 1) // KF == iota((N * MINE, KW), 0) % N
    fold = (iota((MINE, N * MINE), 1) // N == iota((MINE, N * MINE), 0)).astype(BF16)

    def fresh(first):
        repeat = (feature - first == column).astype(BF16)
        wide = jnp.dot(mine[:, QF:], repeat, preferred_element_type=F32)
        wide = jnp.where(block, wide, 0.0).astype(BF16)
        return jnp.dot(fold, wide, preferred_element_type=F32).astype(BF16)

    keys_new, values_new = fresh(0), fresh(KF)

    head_rows = STEPS * QH
    own = iota((head_rows, KW), 0) % N // (N // KH) == iota((head_rows, KW), 1) // HD
    place = iota((head_rows, LENGTH), 1)
    shape = (head_rows, MINE)
    new_step, new_row = iota(shape, 1) // LOCAL, iota(shape, 1) % LOCAL
    in_time = new_step <= iota(shape, 0) // QH
    scale = 1.0 / math.sqrt(HD)
    dims = (((1,), (1,)), ((), ()))
    spreads = []
    for i in range(LOCAL):
        asked = []
        for s in range(STEPS):
            low = (s * LOCAL + i) * N
            asked += [mine[low : low + N, :HD], mine[low : low + N, HD:QF]]
        asked = jnp.concatenate(asked, axis=0)
        spreads.append(jnp.where(own, jnp.concatenate([asked] * KH, axis=1), jnp.zeros((), BF16)))
    fresh_scores = lax.dot_general(
        jnp.concatenate(spreads, axis=0), keys_new, dims, preferred_element_type=F32
    ) * scale
    for i in range(LOCAL):
        if i % GROUPED == 0:
            for pair in loads[i : i + GROUPED]:
                for copy in pair:
                    copy.wait()
        spread = spreads[i]
        new = fresh_scores[i * head_rows : (i + 1) * head_rows]
        new = jnp.where(in_time & (new_row == i), new, -jnp.inf)
        old = lax.dot_general(spread, key_rows[i], dims, preferred_element_type=F32) * scale
        old = jnp.where(place < lengths[i], old, -jnp.inf)
        highest = jnp.maximum(
            jnp.max(old, axis=1, keepdims=True), jnp.max(new, axis=1, keepdims=True)
        )
        old, new = jnp.exp(old - highest), jnp.exp(new - highest)
        totals = jnp.sum(old, axis=1, keepdims=True) + jnp.sum(new, axis=1, keepdims=True)
        mixed = jnp.dot(old.astype(BF16), value_rows[i], preferred_element_type=F32)
        mixed = mixed + jnp.dot(new.astype(BF16), values_new, preferred_element_type=F32)
        mixed = jnp.where(own, mixed, 0.0)
        attended = mixed[:, :HD]
        for k in range(1, KH):
            attended = attended + mixed[:, k * HD : (k + 1) * HD]
        attended = (attended / totals).astype(BF16)
        for s in range(STEPS):
            low = (s * LOCAL + i) * N
            for half in range(2):
                piece = attended[(2 * s + half) * N : (2 * s + half + 1) * N]
                by_row[low : low + N, half * HD : (half + 1) * HD] = piece

    attended = jnp.dot(swap, by_row[...], preferred_element_type=F32).astype(BF16)
    ready[...] = attended.reshape(SIDE, SIDE, MINE, QF)
    copies = [
        pltpu.make_async_copy(ready.at[n // SIDE], out.at[n], sent.at[n]) for n in range(N)
    ]
    for copy in copies:
        copy.start()
    for copy in copies:
        copy.wait()


def pick_kernel(index, slot_in, slot_up, pool, maps, up, map_sem, up_sem):
    copies = []
    for i in range(ENTRIES):
        if i == 0:
            first, second = slot_in.at[index[0]], slot_up.at[index[0]]
        else:
            first = pool.at[index[i], :, pl.ds(0, QF)]
            second = pool.at[index[i], :, pl.ds(QF, OUT_PART)]
        rows = pl.ds(i * RANK, RANK)
        copies.append(pltpu.make_async_copy(first, maps.at[rows], map_sem.at[i]))
        copies.append(pltpu.make_async_copy(second, up.at[rows], up_sem.at[i]))
    for copy in copies:
        copy.start()
    for copy in copies:
        copy.wait()


def base_out_kernel(
    place, member, attended, entry, maps, source, partial, first, second, third, kept
):
    heads = attended[:, pl.ds(place[0], 1)].reshape(ALL_ROWS, QF)
    product = lax.dot_general(
        maps[...], heads, (((1,), (1,)), ((), ())), preferred_element_type=F32
    )
    used = entry[...]
    shrunk = jnp.zeros((RANK, ALL_ROWS), F32)
    for i in range(ENTRIES):
        shrunk = shrunk + jnp.where(used == i, product[i * RANK : (i + 1) * RANK], 0.0)
    shrunk = shrunk.astype(BF16)
    for n in range(N):
        partial[n] = shrunk
    heads = [attended[:, t].reshape(ALL_ROWS, QF) for t in range(SIDE)]
    for k, out in ((1, first), (2, second), (3, third), (0, kept)):
        whose = lax.rem(member[0] + k, SIDE)
        total = jnp.zeros((ALL_ROWS, OUT_PART), F32)
        for j in range(0, SIDE, 2):
            rows = jnp.concatenate([source[t, whose] for t in (j, j + 1)], axis=0)
            total = total + jnp.dot(
                jnp.concatenate(heads[j : j + 2], axis=1), rows, preferred_element_type=F32
            )
        out[...] = total.astype(out.dtype)


def final_kernel(parts, entry, kept, first, second, third, up, out):
    shrunk = jnp.sum(parts[...].astype(F32), axis=0).astype(BF16).astype(F32)
    wide = expand(shrunk, entry[...])
    total = kept[...]
    for arrived in (first, second, third):
        total = total + arrived[...].astype(F32)
    total = total + low_rank_scale * contract(wide, up[...])
    for s in range(STEPS):
        lows = [t * MINE + s * LOCAL for t in range(N)]
        out[s] = jnp.concatenate([total[n : n + LOCAL] for n in lows], axis=0).astype(BF16)


def shard(
    hidden, w_query, w_key, w_value, w_out, key_cache, value_cache, lengths, row_slot, evict_slot,
    evict_adapter, owner, pool_a_in, pool_b_q, pool_b_k, pool_b_v, pool_a_o, pool_b_o,
    slot_a_in, slot_b_q, slot_b_k, slot_b_v, slot_a_o, slot_b_o,
):
    me = lax.axis_index("group")
    part = lax.axis_index(TP)
    place = lax.axis_index("x")[None]
    member = lax.axis_index("y")[None]

    with jax.named_scope("gather_in_maps"):
        packed = pl.pallas_call(
            pack_kernel,
            out_shape=jax.ShapeDtypeStruct((PACKED, IN_PART), BF16),
            in_specs=[hbm()] * 4,
            out_specs=vmem(),
            scratch_shapes=[
                pltpu.VMEM((HELD, RANK, QF), BF16),
                pltpu.VMEM((HELD, RANK, KF), BF16),
                pltpu.VMEM((HELD, RANK, KF), BF16),
                pltpu.SemaphoreType.DMA((HELD,)),
                pltpu.SemaphoreType.DMA((3,)),
            ],
            compiler_params=params(58),
            cost_estimate=cost(0, 2 << 20),
            name="pack",
        )(pool_a_in, pool_b_q, pool_b_k, pool_b_v)
        pool = lax.all_gather(packed, "group")

    with jax.named_scope("positions"):
        position = jnp.sum(
            jnp.where(evict_adapter[..., None] == jnp.arange(N * HELD), owner, 0), axis=-1
        )
        targets = lax.dynamic_slice_in_dim(evict_slot, me * LOADS, LOADS, 1)
        survivor = SLOTS * (SLOTS - 1) // 2 - jnp.sum(targets[0])
        placed = targets[:, :, None] == jnp.arange(SLOTS)
        order = 1 + jnp.arange(STEPS * LOADS).reshape(STEPS, LOADS, 1)
        slot_entry = jnp.sum(jnp.where(placed, order, 0), axis=1)
        second = jnp.where(slot_entry[1] > 0, slot_entry[1], slot_entry[0])
        slot_entry = jnp.stack([slot_entry[0], second])
        entry = jnp.sum(
            jnp.where(
                row_slot[:, :, None] == jnp.arange(SLOTS), slot_entry[:, None, :], 0
            ),
            axis=-1,
        )
        by_step = entry.reshape(1, ALL_ROWS)
        blocks = position % HELD % SHARED
        blocks = lax.dynamic_slice_in_dim(blocks, me * LOADS, LOADS, 1).reshape(1, 1, -1)
        load = jnp.arange(STEPS * LOADS) + 1
        blocks = jnp.sum(jnp.where(entry[:, :, None] == load, blocks, 0), axis=-1)
        blocks = blocks.reshape(ALL_ROWS, 1)
        by_owner = entry.reshape(STEPS, N, LOCAL).transpose(1, 0, 2)
        by_owner = by_owner.reshape(1, ALL_ROWS)
        my_wanted = lax.dynamic_slice_in_dim(position, me * LOADS, LOADS, 1)
        my_wanted = my_wanted.reshape(STEPS * LOADS)
        index = jnp.concatenate([survivor[None], my_wanted]).astype(jnp.int32)

    with jax.named_scope("columns_of_w_out"):
        w_out, packed = lax.optimization_barrier((w_out, packed))
        half = pl.pallas_call(
            split_kernel,
            out_shape=jax.ShapeDtypeStruct((SIDE, SIDE, QF, OUT_PART), BF16),
            in_specs=[hbm()],
            out_specs=vmem(),
            scratch_shapes=[pltpu.SemaphoreType.DMA((N,))],
            compiler_params=params(60),
            cost_estimate=cost(0, 8 << 20),
            name="split",
        )(w_out)
        mine = lax.all_to_all(half, "x", split_axis=0, concat_axis=0, tiled=True)

    with jax.named_scope("base_projections"):
        tokens = hidden.reshape(ALL_ROWS, -1)
        base_q = jnp.dot(tokens, w_query, preferred_element_type=F32)
        base_kv = jnp.concatenate(
            [
                jnp.dot(tokens, w_key, preferred_element_type=F32),
                jnp.dot(tokens, w_value, preferred_element_type=F32),
            ],
            axis=1,
        )
        tokens_part = lax.dynamic_slice_in_dim(tokens, part * IN_PART, IN_PART, 1).T

    with jax.named_scope("gather_out_maps"):
        out_pool = jnp.concatenate([pool_a_o, pool_b_o], axis=2)
        out_pool, index, base_q, base_kv, tokens_part, mine = lax.optimization_barrier(
            (out_pool, index, base_q, base_kv, tokens_part, mine)
        )
        out_pool = lax.all_gather(out_pool, "group").reshape(N * HELD, RANK, QF + OUT_PART)

    with jax.named_scope("shrink"):
        partial_in = pl.pallas_call(
            shrink_kernel,
            out_shape=jax.ShapeDtypeStruct((N, IN_RANK, ALL_ROWS), BF16),
            in_specs=[smem(), hbm(), hbm(), vmem(), vmem()],
            out_specs=vmem(),
            scratch_shapes=[
                pltpu.VMEM((ENTRIES * IN_RANK, IN_PART), BF16),
                pltpu.SemaphoreType.DMA((ENTRIES,)),
            ],
            compiler_params=params(60),
            cost_estimate=cost(2 * ENTRIES * IN_RANK * IN_PART * ALL_ROWS, 2 << 20),
            name="shrink",
        )(index, pool, slot_a_in, tokens_part, by_step)

        partial_in, picks = lax.optimization_barrier((partial_in, index))
        partials = lax.all_to_all(partial_in, TP, split_axis=0, concat_axis=0, tiled=True)

    with jax.named_scope("project"):
        up_q, up_kv = pl.pallas_call(
            pick_up_kernel,
            out_shape=[
                jax.ShapeDtypeStruct((ENTRIES * RANK, QF), BF16),
                jax.ShapeDtypeStruct((ENTRIES * RANK, IN_PART), BF16),
            ],
            in_specs=[smem(), hbm(), hbm(), vmem(), vmem()],
            out_specs=[vmem()] * 2,
            scratch_shapes=[pltpu.SemaphoreType.DMA((ENTRIES,))] * 2,
            compiler_params=params(52),
            cost_estimate=cost(0, 2 << 20),
            name="pick_up",
        )(picks, pool, slot_b_q, slot_b_k, slot_b_v)
        projected = pl.pallas_call(
            project_kernel,
            out_shape=jax.ShapeDtypeStruct((N, MINE, QF + 2 * KF), BF16),
            in_specs=[vmem()] * 7,
            out_specs=vmem(),
            compiler_params=params(16),
            cost_estimate=cost(2 * 400 * 512 * ALL_ROWS, 1 << 20),
            name="project",
        )(partials, by_step, blocks, base_q, base_kv, up_q, up_kv)

    with jax.named_scope("attend"):
        received = lax.all_to_all(projected, TP, split_axis=0, concat_axis=0, tiled=True)
        payload = pl.pallas_call(
            attend_kernel,
            out_shape=jax.ShapeDtypeStruct((N, SIDE, MINE, QF), BF16),
            in_specs=[smem(), vmem(), hbm(), hbm()],
            out_specs=hbm(),
            scratch_shapes=[
                pltpu.VMEM((LOCAL, LENGTH, KW), BF16),
                pltpu.VMEM((LOCAL, LENGTH, KW), BF16),
                pltpu.VMEM((N * MINE, QF), BF16),
                pltpu.VMEM((SIDE, SIDE, MINE, QF), BF16),
                pltpu.SemaphoreType.DMA((LOCAL,)),
                pltpu.SemaphoreType.DMA((LOCAL,)),
                pltpu.SemaphoreType.DMA((N,)),
            ],
            compiler_params=params(60),
            cost_estimate=cost(4 * LOCAL * 64 * KW * LENGTH, 12 << 20),
            name="attend",
        )(lengths, received, key_cache, value_cache)
        gathered = lax.all_to_all(payload, TP, split_axis=0, concat_axis=0, tiled=True)

        payload, picks = lax.optimization_barrier((payload, index))
        maps, up_o = pl.pallas_call(
            pick_kernel,
            out_shape=[
                jax.ShapeDtypeStruct((ENTRIES * RANK, QF), BF16),
                jax.ShapeDtypeStruct((ENTRIES * RANK, OUT_PART), BF16),
            ],
            in_specs=[smem()] + [hbm()] * 3,
            out_specs=[vmem()] * 2,
            scratch_shapes=[pltpu.SemaphoreType.DMA((ENTRIES,))] * 2,
            compiler_params=params(24),
            cost_estimate=cost(0, 3 << 20),
            name="pick",
        )(picks, slot_a_o, slot_b_o, out_pool)

    with jax.named_scope("output"):
        block = (ALL_ROWS, OUT_PART)
        partial_out, *passed, kept_out = pl.pallas_call(
            base_out_kernel,
            out_shape=[jax.ShapeDtypeStruct((N, RANK, ALL_ROWS), BF16)]
            + [jax.ShapeDtypeStruct(block, BF16)] * 3
            + [jax.ShapeDtypeStruct(block, F32)],
            in_specs=[smem()] * 2 + [vmem()] * 4,
            out_specs=[vmem()] * 5,
            compiler_params=params(24),
            cost_estimate=cost(2 * ALL_ROWS * FEATURES * OUT_PART, 5 << 20),
            name="base_out",
        )(place, member, gathered, by_owner, maps, mine)
        partials_out = lax.all_to_all(partial_out, TP, split_axis=0, concat_axis=0, tiled=True)
        turns = [[(i, (i + k) % SIDE) for i in range(SIDE)] for k in range(1, SIDE)]
        passed = [lax.ppermute(p, "y", turn) for p, turn in zip(passed, turns)]
        return pl.pallas_call(
            final_kernel,
            out_shape=jax.ShapeDtypeStruct((STEPS, ROWS, OUT_PART), BF16),
            in_specs=[vmem()] * 7,
            out_specs=vmem(),
            compiler_params=params(16),
            cost_estimate=cost(2 * 400 * OUT_PART * ALL_ROWS, 1 << 20),
            name="final",
        )(partials_out, by_owner, kept_out, *passed, up_o)


def solution(mesh):
    grid = jax.sharding.Mesh(mesh.devices.reshape(N, SIDE, SIDE), ("group",) + TP)
    pooled = P("group", None, TP)
    cached = P(("group",) + TP, None, None)
    placed = (
        P(None, "group", None), P(None, TP), P(None, TP), P(None, TP), P(TP, None),
        cached, cached, P(("group",) + TP), P(None, "group"), P(), P(), P(),
    ) + (pooled,) * 12
    return jax.shard_map(
        shard, mesh=grid, in_specs=placed, out_specs=P(None, "group", TP), check_vma=False
    )
```

```python
import math

import jax
import jax.numpy as jnp
from jax import lax
from jax.experimental import pallas as pl
from jax.experimental.pallas import tpu as pltpu
from jax.sharding import PartitionSpec as P

QH = 32
KH = 4
HD = 128
STEPS = 2
ROWS = 128
RANK = 16
LOADS = 12
SLOTS = 13
HELD = 12
N = 16
SIDE = 4
GROUPED = 1
ALL_ROWS = STEPS * ROWS
LOCAL = ROWS // N
MINE = STEPS * LOCAL
ENTRIES = 1 + STEPS * LOADS
SHARED = 8
Q_AT = HELD * 48
KV_AT = Q_AT + HELD // 2 * RANK
PACKED = KV_AT + 2 * RANK
IN_RANK = 3 * RANK
QF = 256
KF = 32
IN_PART = 512
OUT_PART = 512
FEATURES = QH * HD
QKV = QF + 2 * KF
TP = ("y", "x")
LENGTH = 512
KW = KH * HD
BF16 = jnp.bfloat16
F32 = jnp.float32
low_rank_scale = 0.5


def vmem():
    return pl.BlockSpec(memory_space=pltpu.VMEM)


def hbm():
    return pl.BlockSpec(memory_space=pl.ANY)


def smem():
    return pl.BlockSpec(memory_space=pltpu.SMEM)


def params(mib=40):
    return pltpu.CompilerParams(vmem_limit_bytes=mib * 1024 * 1024)


def cost(flops, nbytes):
    return pl.CostEstimate(flops=flops, bytes_accessed=nbytes, transcendentals=0)


def iota(shape, axis):
    return lax.broadcasted_iota(jnp.int32, shape, axis)


def pack_kernel(maps_in, maps_q, maps_k, maps_v, out, all_q, all_k, all_v, in_sem, sem):
    copies = [
        pltpu.make_async_copy(maps_q, all_q, sem.at[0]),
        pltpu.make_async_copy(maps_k, all_k, sem.at[1]),
        pltpu.make_async_copy(maps_v, all_v, sem.at[2]),
    ]
    for k in range(HELD):
        rows = pl.ds(k * IN_RANK, IN_RANK)
        copies.append(pltpu.make_async_copy(maps_in.at[k], out.at[rows], in_sem.at[k]))
    for copy in copies:
        copy.start()
    for copy in copies[:3]:
        copy.wait()
    for k in range(HELD):
        low, block = Q_AT + k // 2 * RANK, k % 2 * QF
        out[low : low + RANK, block : block + QF] = all_q[k]
    empty = jnp.zeros((RANK, 2 * KF), BF16)
    for first in range(0, 2 * SHARED, SHARED):
        pieces = []
        for k in range(first, first + SHARED):
            pieces += [all_k[k], all_v[k]] if k < HELD else [empty]
        low = KV_AT + first // SHARED * RANK
        out[low : low + RANK] = jnp.concatenate(pieces, axis=1)
    for copy in copies[3:]:
        copy.wait()


def aligned(value, unit):
    return pl.multiple_of(value * unit, unit)


def shrink_kernel(index, pool, slot, tokens, entry, out, maps, arrived):
    copies = []
    for i in range(ENTRIES):
        if i == 0:
            origin = slot.at[index[0]]
        else:
            rows = pl.ds(aligned(lax.rem(index[i], HELD), IN_RANK), IN_RANK)
            origin = pool.at[index[i] // HELD, rows]
        copy = pltpu.make_async_copy(origin, maps.at[pl.ds(i * IN_RANK, IN_RANK)], arrived.at[i])
        copy.start()
        copies.append(copy)
    for copy in copies:
        copy.wait()
    used = entry[...]
    product = jnp.dot(maps[...], tokens[...], preferred_element_type=F32)
    total = jnp.zeros((IN_RANK, ALL_ROWS), F32)
    for i in range(ENTRIES):
        total = total + jnp.where(used == i, product[i * IN_RANK : (i + 1) * IN_RANK], 0.0)
    total = total.astype(BF16)
    for n in range(N):
        out[n] = total


def expand(shrunk, entry):
    blocks = [jnp.where(entry == i, shrunk, 0.0) for i in range(ENTRIES)]
    return jnp.concatenate(blocks, axis=0).astype(BF16)


def contract(left, right):
    return lax.dot_general(left, right, (((0,), (0,)), ((), ())), preferred_element_type=F32)


def pick_up_kernel(index, pool, slot_q, slot_k, slot_v, up_q, up_kv, q_sem, kv_sem):
    copies = []
    for i in range(ENTRIES):
        rows = pl.ds(i * RANK, RANK)
        if i == 0:
            copies.append(pltpu.make_async_copy(slot_q.at[index[0]], up_q.at[rows], q_sem.at[0]))
            continue
        source, k = index[i] // HELD, lax.rem(index[i], HELD)
        of_q = pl.ds(Q_AT + aligned(k // 2, RANK), RANK)
        block = pl.ds(aligned(lax.rem(k, 2), QF), QF)
        of_kv = pl.ds(KV_AT + aligned(k // SHARED, RANK), RANK)
        copies.append(
            pltpu.make_async_copy(pool.at[source, of_q, block], up_q.at[rows], q_sem.at[i])
        )
        copies.append(pltpu.make_async_copy(pool.at[source, of_kv], up_kv.at[rows], kv_sem.at[i]))
    for copy in copies:
        copy.start()
    empty = jnp.zeros((RANK, IN_PART - 2 * KF), BF16)
    up_kv[:RANK] = jnp.concatenate([slot_k[index[0]], slot_v[index[0]], empty], axis=1)
    for copy in copies:
        copy.wait()


def project_kernel(parts, entry, block, base_q, base_kv, up_q, up_kv, out):
    shrunk = jnp.sum(parts[...].astype(F32), axis=0).astype(BF16).astype(F32)
    used = entry[...]
    wide_q = expand(shrunk[:RANK], used)
    wide_k = expand(shrunk[RANK : 2 * RANK], used)
    wide_v = expand(shrunk[2 * RANK :], used)
    query = base_q[...] + low_rank_scale * contract(wide_q, up_q[...])
    delta_k = contract(wide_k, up_kv[...])
    delta_v = contract(wide_v, up_kv[...])
    delta = jnp.where(iota(delta_k.shape, 1) % (2 * KF) < KF, delta_k, delta_v)
    delta = jnp.where(iota(delta.shape, 1) // (2 * KF) == block[...], delta, 0.0)
    folded = jnp.zeros((ALL_ROWS, 2 * KF), F32)
    for j in range(SHARED):
        folded = folded + delta[:, j * 2 * KF : (j + 1) * 2 * KF]
    fresh = base_kv[...] + low_rank_scale * folded
    for t in range(N):
        lows = [s * ROWS + t * LOCAL for s in range(STEPS)]
        out[t, :, :QF] = jnp.concatenate([query[n : n + LOCAL] for n in lows], 0).astype(BF16)
        out[t, :, QF:] = jnp.concatenate([fresh[n : n + LOCAL] for n in lows], 0).astype(BF16)


def split_kernel(weight, out, arrived):
    copies = []
    for t in range(N):
        source = weight.at[:, pl.ds(t * OUT_PART, OUT_PART)]
        copies.append(
            pltpu.make_async_copy(source, out.at[t % SIDE, t // SIDE], arrived.at[t])
        )
    for copy in copies:
        copy.start()
    for copy in copies:
        copy.wait()


def transposing():
    shape = (N * MINE, N * MINE)
    row, column = iota(shape, 0), iota(shape, 1)
    return ((row // N == column % N) & (row % N == column // N)).astype(BF16)


def attend_kernel(
    lengths, received, keys, values, out, key_rows, value_rows, by_row, ready, key_sem, value_sem,
    sent,
):
    loads = []
    for i in range(LOCAL):
        pair = (
            pltpu.make_async_copy(keys.at[i], key_rows.at[i], key_sem.at[i]),
            pltpu.make_async_copy(values.at[i], value_rows.at[i], value_sem.at[i]),
        )
        for copy in pair:
            copy.start()
        loads.append(pair)
    swap = transposing()
    mine = jnp.dot(swap, received[...].reshape(N * MINE, -1), preferred_element_type=F32)
    mine = mine.astype(BF16)
    shape = (2 * KF, KW)
    feature, column = iota(shape, 0), iota(shape, 1) % KF
    block = iota((N * MINE, KW), 1) // KF == iota((N * MINE, KW), 0) % N
    fold = (iota((MINE, N * MINE), 1) // N == iota((MINE, N * MINE), 0)).astype(BF16)

    def fresh(first):
        repeat = (feature - first == column).astype(BF16)
        wide = jnp.dot(mine[:, QF:], repeat, preferred_element_type=F32)
        wide = jnp.where(block, wide, 0.0).astype(BF16)
        return jnp.dot(fold, wide, preferred_element_type=F32).astype(BF16)

    keys_new, values_new = fresh(0), fresh(KF)

    head_rows = STEPS * QH
    own = iota((head_rows, KW), 0) % N // (N // KH) == iota((head_rows, KW), 1) // HD
    place = iota((head_rows, LENGTH), 1)
    shape = (head_rows, MINE)
    new_step, new_row = iota(shape, 1) // LOCAL, iota(shape, 1) % LOCAL
    in_time = new_step <= iota(shape, 0) // QH
    scale = 1.0 / math.sqrt(HD)
    dims = (((1,), (1,)), ((), ()))
    spreads = []
    for i in range(LOCAL):
        asked = []
        for s in range(STEPS):
            low = (s * LOCAL + i) * N
            asked += [mine[low : low + N, :HD], mine[low : low + N, HD:QF]]
        asked = jnp.concatenate(asked, axis=0)
        spreads.append(jnp.where(own, jnp.concatenate([asked] * KH, axis=1), jnp.zeros((), BF16)))
    fresh_scores = lax.dot_general(
        jnp.concatenate(spreads, axis=0), keys_new, dims, preferred_element_type=F32
    ) * scale
    for i in range(LOCAL):
        if i % GROUPED == 0:
            for pair in loads[i : i + GROUPED]:
                for copy in pair:
                    copy.wait()
        spread = spreads[i]
        new = fresh_scores[i * head_rows : (i + 1) * head_rows]
        new = jnp.where(in_time & (new_row == i), new, -jnp.inf)
        old = lax.dot_general(spread, key_rows[i], dims, preferred_element_type=F32) * scale
        old = jnp.where(place < lengths[i], old, -jnp.inf)
        highest = jnp.maximum(
            jnp.max(old, axis=1, keepdims=True), jnp.max(new, axis=1, keepdims=True)
        )
        old, new = jnp.exp(old - highest), jnp.exp(new - highest)
        totals = jnp.sum(old, axis=1, keepdims=True) + jnp.sum(new, axis=1, keepdims=True)
        mixed = jnp.dot(old.astype(BF16), value_rows[i], preferred_element_type=F32)
        mixed = mixed + jnp.dot(new.astype(BF16), values_new, preferred_element_type=F32)
        mixed = jnp.where(own, mixed, 0.0)
        attended = mixed[:, :HD]
        for k in range(1, KH):
            attended = attended + mixed[:, k * HD : (k + 1) * HD]
        attended = (attended / totals).astype(BF16)
        for s in range(STEPS):
            low = (s * LOCAL + i) * N
            for half in range(2):
                piece = attended[(2 * s + half) * N : (2 * s + half + 1) * N]
                by_row[low : low + N, half * HD : (half + 1) * HD] = piece

    attended = jnp.dot(swap, by_row[...], preferred_element_type=F32).astype(BF16)
    ready[...] = attended.reshape(SIDE, SIDE, MINE, QF)
    copies = [
        pltpu.make_async_copy(ready.at[n // SIDE], out.at[n], sent.at[n]) for n in range(N)
    ]
    for copy in copies:
        copy.start()
    for copy in copies:
        copy.wait()


def pick_kernel(index, slot_in, slot_up, pool, maps, up, map_sem, up_sem):
    copies = []
    for i in range(ENTRIES):
        if i == 0:
            first, second = slot_in.at[index[0]], slot_up.at[index[0]]
        else:
            first = pool.at[index[i], :, pl.ds(0, QF)]
            second = pool.at[index[i], :, pl.ds(QF, OUT_PART)]
        rows = pl.ds(i * RANK, RANK)
        copies.append(pltpu.make_async_copy(first, maps.at[rows], map_sem.at[i]))
        copies.append(pltpu.make_async_copy(second, up.at[rows], up_sem.at[i]))
    for copy in copies:
        copy.start()
    for copy in copies:
        copy.wait()


def base_out_kernel(
    place, member, attended, entry, maps, source, partial, first, second, third, kept
):
    heads = attended[:, pl.ds(place[0], 1)].reshape(ALL_ROWS, QF)
    product = lax.dot_general(
        maps[...], heads, (((1,), (1,)), ((), ())), preferred_element_type=F32
    )
    used = entry[...]
    shrunk = jnp.zeros((RANK, ALL_ROWS), F32)
    for i in range(ENTRIES):
        shrunk = shrunk + jnp.where(used == i, product[i * RANK : (i + 1) * RANK], 0.0)
    shrunk = shrunk.astype(BF16)
    for n in range(N):
        partial[n] = shrunk
    heads = [attended[:, t].reshape(ALL_ROWS, QF) for t in range(SIDE)]
    for k, out in ((1, first), (2, second), (3, third), (0, kept)):
        whose = lax.rem(member[0] + k, SIDE)
        total = jnp.zeros((ALL_ROWS, OUT_PART), F32)
        for j in range(0, SIDE, 2):
            rows = jnp.concatenate([source[t, whose] for t in (j, j + 1)], axis=0)
            total = total + jnp.dot(
                jnp.concatenate(heads[j : j + 2], axis=1), rows, preferred_element_type=F32
            )
        out[...] = total.astype(out.dtype)


def final_kernel(parts, entry, kept, first, second, third, up, out):
    shrunk = jnp.sum(parts[...].astype(F32), axis=0).astype(BF16).astype(F32)
    wide = expand(shrunk, entry[...])
    total = kept[...]
    for arrived in (first, second, third):
        total = total + arrived[...].astype(F32)
    total = total + low_rank_scale * contract(wide, up[...])
    for s in range(STEPS):
        lows = [t * MINE + s * LOCAL for t in range(N)]
        out[s] = jnp.concatenate([total[n : n + LOCAL] for n in lows], axis=0).astype(BF16)


def shard(
    hidden, w_query, w_key, w_value, w_out, key_cache, value_cache, lengths, row_slot, evict_slot,
    evict_adapter, owner, pool_a_in, pool_b_q, pool_b_k, pool_b_v, pool_a_o, pool_b_o,
    slot_a_in, slot_b_q, slot_b_k, slot_b_v, slot_a_o, slot_b_o,
):
    me = lax.axis_index("group")
    part = lax.axis_index(TP)
    place = lax.axis_index("x")[None]
    member = lax.axis_index("y")[None]

    with jax.named_scope("gather_in_maps"):
        packed = pl.pallas_call(
            pack_kernel,
            out_shape=jax.ShapeDtypeStruct((PACKED, IN_PART), BF16),
            in_specs=[hbm()] * 4,
            out_specs=vmem(),
            scratch_shapes=[
                pltpu.VMEM((HELD, RANK, QF), BF16),
                pltpu.VMEM((HELD, RANK, KF), BF16),
                pltpu.VMEM((HELD, RANK, KF), BF16),
                pltpu.SemaphoreType.DMA((HELD,)),
                pltpu.SemaphoreType.DMA((3,)),
            ],
            compiler_params=params(58),
            cost_estimate=cost(0, 2 << 20),
            name="pack",
        )(pool_a_in, pool_b_q, pool_b_k, pool_b_v)
        pool = lax.all_gather(packed, "group")

    with jax.named_scope("positions"):
        position = jnp.sum(
            jnp.where(evict_adapter[..., None] == jnp.arange(N * HELD), owner, 0), axis=-1
        )
        targets = lax.dynamic_slice_in_dim(evict_slot, me * LOADS, LOADS, 1)
        survivor = SLOTS * (SLOTS - 1) // 2 - jnp.sum(targets[0])
        placed = targets[:, :, None] == jnp.arange(SLOTS)
        order = 1 + jnp.arange(STEPS * LOADS).reshape(STEPS, LOADS, 1)
        slot_entry = jnp.sum(jnp.where(placed, order, 0), axis=1)
        second = jnp.where(slot_entry[1] > 0, slot_entry[1], slot_entry[0])
        slot_entry = jnp.stack([slot_entry[0], second])
        entry = jnp.sum(
            jnp.where(
                row_slot[:, :, None] == jnp.arange(SLOTS), slot_entry[:, None, :], 0
            ),
            axis=-1,
        )
        by_step = entry.reshape(1, ALL_ROWS)
        blocks = position % HELD % SHARED
        blocks = lax.dynamic_slice_in_dim(blocks, me * LOADS, LOADS, 1).reshape(1, 1, -1)
        load = jnp.arange(STEPS * LOADS) + 1
        blocks = jnp.sum(jnp.where(entry[:, :, None] == load, blocks, 0), axis=-1)
        blocks = blocks.reshape(ALL_ROWS, 1)
        by_owner = entry.reshape(STEPS, N, LOCAL).transpose(1, 0, 2)
        by_owner = by_owner.reshape(1, ALL_ROWS)
        my_wanted = lax.dynamic_slice_in_dim(position, me * LOADS, LOADS, 1)
        my_wanted = my_wanted.reshape(STEPS * LOADS)
        index = jnp.concatenate([survivor[None], my_wanted]).astype(jnp.int32)

    with jax.named_scope("columns_of_w_out"):
        w_out, packed = lax.optimization_barrier((w_out, packed))
        half = pl.pallas_call(
            split_kernel,
            out_shape=jax.ShapeDtypeStruct((SIDE, SIDE, QF, OUT_PART), BF16),
            in_specs=[hbm()],
            out_specs=vmem(),
            scratch_shapes=[pltpu.SemaphoreType.DMA((N,))],
            compiler_params=params(60),
            cost_estimate=cost(0, 8 << 20),
            name="split",
        )(w_out)
        mine = lax.all_to_all(half, "x", split_axis=0, concat_axis=0, tiled=True)

    with jax.named_scope("base_projections"):
        tokens = hidden.reshape(ALL_ROWS, -1)
        base_q = jnp.dot(tokens, w_query, preferred_element_type=F32)
        base_kv = jnp.concatenate(
            [
                jnp.dot(tokens, w_key, preferred_element_type=F32),
                jnp.dot(tokens, w_value, preferred_element_type=F32),
            ],
            axis=1,
        )
        tokens_part = lax.dynamic_slice_in_dim(tokens, part * IN_PART, IN_PART, 1).T

    with jax.named_scope("gather_out_maps"):
        out_pool = jnp.concatenate([pool_a_o, pool_b_o], axis=2)
        out_pool, index, base_q, base_kv, tokens_part, mine = lax.optimization_barrier(
            (out_pool, index, base_q, base_kv, tokens_part, mine)
        )
        out_pool = lax.all_gather(out_pool, "group").reshape(N * HELD, RANK, QF + OUT_PART)

    with jax.named_scope("shrink"):
        partial_in = pl.pallas_call(
            shrink_kernel,
            out_shape=jax.ShapeDtypeStruct((N, IN_RANK, ALL_ROWS), BF16),
            in_specs=[smem(), hbm(), hbm(), vmem(), vmem()],
            out_specs=vmem(),
            scratch_shapes=[
                pltpu.VMEM((ENTRIES * IN_RANK, IN_PART), BF16),
                pltpu.SemaphoreType.DMA((ENTRIES,)),
            ],
            compiler_params=params(60),
            cost_estimate=cost(2 * ENTRIES * IN_RANK * IN_PART * ALL_ROWS, 2 << 20),
            name="shrink",
        )(index, pool, slot_a_in, tokens_part, by_step)

        partial_in, picks = lax.optimization_barrier((partial_in, index))
        partials = lax.all_to_all(partial_in, TP, split_axis=0, concat_axis=0, tiled=True)

    with jax.named_scope("project"):
        up_q, up_kv = pl.pallas_call(
            pick_up_kernel,
            out_shape=[
                jax.ShapeDtypeStruct((ENTRIES * RANK, QF), BF16),
                jax.ShapeDtypeStruct((ENTRIES * RANK, IN_PART), BF16),
            ],
            in_specs=[smem(), hbm(), hbm(), vmem(), vmem()],
            out_specs=[vmem()] * 2,
            scratch_shapes=[pltpu.SemaphoreType.DMA((ENTRIES,))] * 2,
            compiler_params=params(52),
            cost_estimate=cost(0, 2 << 20),
            name="pick_up",
        )(picks, pool, slot_b_q, slot_b_k, slot_b_v)
        projected = pl.pallas_call(
            project_kernel,
            out_shape=jax.ShapeDtypeStruct((N, MINE, QF + 2 * KF), BF16),
            in_specs=[vmem()] * 7,
            out_specs=vmem(),
            compiler_params=params(16),
            cost_estimate=cost(2 * 400 * 512 * ALL_ROWS, 1 << 20),
            name="project",
        )(partials, by_step, blocks, base_q, base_kv, up_q, up_kv)

    with jax.named_scope("attend"):
        received = lax.all_to_all(projected, TP, split_axis=0, concat_axis=0, tiled=True)
        payload = pl.pallas_call(
            attend_kernel,
            out_shape=jax.ShapeDtypeStruct((N, SIDE, MINE, QF), BF16),
            in_specs=[smem(), vmem(), hbm(), hbm()],
            out_specs=hbm(),
            scratch_shapes=[
                pltpu.VMEM((LOCAL, LENGTH, KW), BF16),
                pltpu.VMEM((LOCAL, LENGTH, KW), BF16),
                pltpu.VMEM((N * MINE, QF), BF16),
                pltpu.VMEM((SIDE, SIDE, MINE, QF), BF16),
                pltpu.SemaphoreType.DMA((LOCAL,)),
                pltpu.SemaphoreType.DMA((LOCAL,)),
                pltpu.SemaphoreType.DMA((N,)),
            ],
            compiler_params=params(60),
            cost_estimate=cost(4 * LOCAL * 64 * KW * LENGTH, 12 << 20),
            name="attend",
        )(lengths, received, key_cache, value_cache)
        gathered = lax.all_to_all(payload, TP, split_axis=0, concat_axis=0, tiled=True)

        payload, picks = lax.optimization_barrier((payload, index))
        maps, up_o = pl.pallas_call(
            pick_kernel,
            out_shape=[
                jax.ShapeDtypeStruct((ENTRIES * RANK, QF), BF16),
                jax.ShapeDtypeStruct((ENTRIES * RANK, OUT_PART), BF16),
            ],
            in_specs=[smem()] + [hbm()] * 3,
            out_specs=[vmem()] * 2,
            scratch_shapes=[pltpu.SemaphoreType.DMA((ENTRIES,))] * 2,
            compiler_params=params(24),
            cost_estimate=cost(0, 3 << 20),
            name="pick",
        )(picks, slot_a_o, slot_b_o, out_pool)

    with jax.named_scope("output"):
        block = (ALL_ROWS, OUT_PART)
        partial_out, *passed, kept_out = pl.pallas_call(
            base_out_kernel,
            out_shape=[jax.ShapeDtypeStruct((N, RANK, ALL_ROWS), BF16)]
            + [jax.ShapeDtypeStruct(block, BF16)] * 3
            + [jax.ShapeDtypeStruct(block, F32)],
            in_specs=[smem()] * 2 + [vmem()] * 4,
            out_specs=[vmem()] * 5,
            compiler_params=params(24),
            cost_estimate=cost(2 * ALL_ROWS * FEATURES * OUT_PART, 5 << 20),
            name="base_out",
        )(place, member, gathered, by_owner, maps, mine)
        partials_out = lax.all_to_all(partial_out, TP, split_axis=0, concat_axis=0, tiled=True)
        turns = [[(i, (i + k) % SIDE) for i in range(SIDE)] for k in range(1, SIDE)]
        passed = [lax.ppermute(p, "y", turn) for p, turn in zip(passed, turns)]
        return pl.pallas_call(
            final_kernel,
            out_shape=jax.ShapeDtypeStruct((STEPS, ROWS, OUT_PART), BF16),
            in_specs=[vmem()] * 7,
            out_specs=vmem(),
            compiler_params=params(16),
            cost_estimate=cost(2 * 400 * OUT_PART * ALL_ROWS, 1 << 20),
            name="final",
        )(partials_out, by_owner, kept_out, *passed, up_o)


def solution(mesh):
    grid = jax.sharding.Mesh(mesh.devices.reshape(N, SIDE, SIDE), ("group",) + TP)
    pooled = P("group", None, TP)
    cached = P(("group",) + TP, None, None)
    placed = (
        P(None, "group", None), P(None, TP), P(None, TP), P(None, TP), P(TP, None),
        cached, cached, P(("group",) + TP), P(None, "group"), P(), P(), P(),
    ) + (pooled,) * 12
    return jax.shard_map(
        shard, mesh=grid, in_specs=placed, out_specs=P(None, "group", TP), check_vma=False
    )
```
